32 devices in a mesh: parts: 2 (over y), rows: 4 (over z), layer: 4 (over x, core).
Axes of the slice: x: 2, y: 2, z: 4, core: 2. Of those that a mesh axis runs over, the one named last changes fastest.
Arguments:
- query_hidden: bfloat16 [4, 384, 6144], P('layer', 'rows'), may hold values from -6 to 6
- query_model: bfloat16 [4, 384, 4096], P('layer', 'rows'), may hold values from -6 to 6
- train_hidden: bfloat16 [4, 320, 6144], P('layer', ('parts', 'rows')), parts along dimension 1, may hold values from -0.009765625 to 0.009765625
- train_model: bfloat16 [4, 320, 4096], P('layer', ('parts', 'rows')), parts along dimension 1, may hold values from -0.01171875 to 0.01171875
- hidden_basis: bfloat16 [4, 6144, 6144], P('layer', 'rows'), may hold values from -0.078125 to 0.078125
- model_basis: bfloat16 [4, 4096, 4096], P('layer', 'rows'), may hold values from -0.09375 to 0.09375
- hidden_eigen: float32 [4, 6144], P('layer', 'rows'), may hold values from 0.05 to 5
- model_eigen: float32 [4, 4096], P('layer', 'rows'), may hold values from 0.05 to 5
Outputs:
- scores: float32 [40, 48], P(('parts', 'rows'), 'layer'), parts along dimension 0
The draws below stay inside these ranges and needn't reach their ends.
There are 2 independent parts, one for each index of `parts`. The reference program is written for one: setup_inputs(seed, part) draws one part's arguments, and reference() takes and returns one part's arrays. A program takes and returns all parts, laid end to end along the dimension named above; an argument that names none is the same for every part. Nothing has to cross between parts.
All inputs are finite; a program needn't handle non-finite values.
Results may differ from the reference program's by a relative error of at most 0.0041.
Values may be sent and summed in bfloat16 or wider, within the bound.
No kernel may reach another device: no remote copies, remote signals or barrier semaphores. Data moves between devices by JAX's collectives and lax.ppermute only.
A program may use at most 128 MiB of HBM per device.

```python
import math
import jax
import jax.numpy as jnp

FFW = 6144
D = 4096
RANK = 8
QUERIES = 48
LAYERS = 4
TRAIN = 20


def block_levels(stream_key, dims, pieces, smallest, largest):
    def one(position, shards_of):
        steps = jax.random.uniform(jax.random.fold_in(jax.random.fold_in(stream_key, 6), position), (shards_of,), jnp.float32, smallest / len(pieces), largest / len(pieces))
        return jnp.repeat(jnp.exp(steps), dims[position] // shards_of).reshape((-1,) + (1,) * (len(dims) - position - 1))

    gain = one(*pieces[0])
    for cut in pieces[1:]:
        gain = gain * one(*cut)
    return gain


def centred(rng, dims, deviation, bound, shards=(), kind=jnp.bfloat16):
    result = deviation * jax.random.normal(rng, dims, jnp.float32)
    if shards:
        result = result * block_levels(rng, dims, shards, -0.22, 0.18)
    return jnp.clip(result, -bound, bound).astype(kind)


def setup_inputs(seed: int = 0, part: int = 0) -> dict:
    splits = jax.random.split(jax.random.key(seed), 9)
    part_splits = jax.random.split(jax.random.fold_in(splits[8], part), 9)
    return {
        "query_hidden": centred(splits[0], (LAYERS, QUERIES * RANK, FFW), 1.0, 6.0, ((0, 4), (1, 4))),
        "query_model": centred(splits[1], (LAYERS, QUERIES * RANK, D), 1.0, 6.0, ((0, 4), (1, 4))),
        "train_hidden": centred(part_splits[2], (LAYERS, TRAIN * RANK, FFW), (64 * FFW) ** -0.5, 0.009765625, ((0, 4), (1, 4))),
        "train_model": centred(part_splits[3], (LAYERS, TRAIN * RANK, D), (64 * D) ** -0.5, 0.01171875, ((0, 4), (1, 4))),
        "hidden_basis": centred(splits[4], (LAYERS, FFW, FFW), FFW ** -0.5, 0.078125, ((0, 4), (1, 4))),
        "model_basis": centred(splits[5], (LAYERS, D, D), D ** -0.5, 0.09375, ((0, 4), (1, 4))),
        "hidden_eigen": jnp.clip(jnp.exp(math.log(5.0) - 4.6051702 * jax.random.uniform(splits[6], (LAYERS, FFW), jnp.float32) ** block_levels(splits[6], (LAYERS, FFW), ((0, 4), (1, 4)), -0.2, 0.2)), 0.05, 5.0),
        "model_eigen": jnp.clip(jnp.exp(math.log(5.0) - 4.6051702 * jax.random.uniform(splits[7], (LAYERS, D), jnp.float32) ** block_levels(splits[7], (LAYERS, D), ((0, 4), (1, 4)), -0.2, 0.2)), 0.05, 5.0),
    }


damping = 0.1


def reference(query_hidden, query_model, train_hidden, train_model, hidden_basis, model_basis, hidden_eigen, model_eigen):
    summed = jnp.zeros((TRAIN, QUERIES), jnp.float32)
    for layer_index in range(LAYERS):
        rotated_hidden = jnp.dot(hidden_basis[layer_index], query_hidden[layer_index].T, preferred_element_type=jnp.float32)
        rotated_model = jnp.dot(model_basis[layer_index], query_model[layer_index].T, preferred_element_type=jnp.float32)
        inverse_hidden = 1.0 / (hidden_eigen[layer_index] + damping)
        inverse_model = 1.0 / (model_eigen[layer_index] + damping)
        scaled_hidden = (inverse_hidden[:, None] * rotated_hidden).astype(jnp.bfloat16)
        scaled_model = (inverse_model[:, None] * rotated_model).astype(jnp.bfloat16)
        hidden_gram = jnp.dot(train_hidden[layer_index], scaled_hidden, preferred_element_type=jnp.float32)
        model_gram = jnp.dot(train_model[layer_index], scaled_model, preferred_element_type=jnp.float32)
        layer_scores = jnp.einsum("isqr,isqr->iq", hidden_gram.reshape(TRAIN, RANK, QUERIES, RANK), model_gram.reshape(TRAIN, RANK, QUERIES, RANK))
        summed = summed + layer_scores
    return summed
```

```python
import jax
import jax.numpy as jnp
from jax import lax
from jax.sharding import PartitionSpec as P

RANK = 8


damping = 0.1


def shift(value, axis, by):
    size = lax.axis_size(axis)
    return lax.ppermute(value, axis, [(i, (i + by) % size) for i in range(size)])


def per_device(
    query_hidden,
    query_model,
    train_hidden,
    train_model,
    hidden_basis,
    model_basis,
    hidden_eigen,
    model_eigen,
):
    rows = lax.axis_size("rows")
    parts = lax.axis_size("parts")
    layers = lax.axis_size("layer")
    row = lax.axis_index("rows")
    part = lax.axis_index("parts")
    hidden_share = hidden_basis.shape[1]
    model_share = model_basis.shape[1]
    held = train_hidden.shape[1]
    columns = query_hidden.shape[1] // parts
    queries = query_hidden.shape[1] * rows // RANK

    own_model = lax.dynamic_slice_in_dim(query_model[0], part * columns, columns, 0)
    own_hidden = lax.dynamic_slice_in_dim(query_hidden[0], part * columns, columns, 0)

    def directions_of(owner):
        return jnp.concatenate(
            [
                lax.dynamic_slice_in_dim(train_hidden[0], owner * hidden_share, hidden_share, 1),
                lax.dynamic_slice_in_dim(train_model[0], owner * model_share, model_share, 1),
            ],
            axis=1,
        )

    blocks = [directions_of(row)]
    for k in range(1, rows):
        blocks.append(shift(directions_of((row + k) % rows), "rows", k))
    store = jnp.concatenate(blocks, axis=0)
    stores = jnp.concatenate([store] + [shift(store, "parts", j) for j in range(1, parts)], axis=0)

    all_model = lax.all_gather(own_model, "rows", axis=0, tiled=True)
    all_hidden = lax.all_gather(own_hidden, "rows", axis=0, tiled=True)

    def gram(basis, eigen, gathered, train):
        rotated = jnp.einsum("eh,qh->eq", basis, gathered, preferred_element_type=jnp.float32)
        scaled = (rotated * (1.0 / (eigen + damping))[:, None]).astype(jnp.bfloat16)
        return jnp.dot(train, scaled, preferred_element_type=jnp.float32)

    model_gram = gram(model_basis[0], model_eigen[0], all_model, stores[:, hidden_share:])
    hidden_gram = gram(hidden_basis[0], hidden_eigen[0], all_hidden, stores[:, :hidden_share])

    def summed(partial):
        partial = partial.reshape(parts, rows, held, columns * rows)
        total = partial[:, 0]
        for k in range(1, rows):
            total = total + shift(partial[:, k].astype(jnp.bfloat16), "rows", -k).astype(jnp.float32)
        return total

    product = summed(model_gram) * summed(hidden_gram)
    examples = held // RANK
    by_column = product.reshape(parts, examples, RANK, rows * columns).sum(axis=2)
    if columns % RANK == 0:
        by_query = by_column.reshape(parts, examples, rows, 1, columns // RANK, RANK).sum(axis=-1)
        mine = lax.broadcasted_iota(jnp.int32, (1, 1, 1, parts, 1), 3) == part
        partial_value = jnp.where(mine, by_query, 0.0).reshape(parts, examples, queries)
    else:
        place = jnp.arange(rows * columns)
        place = (place // columns) * (columns * parts) + part * columns + place % columns
        pick = (place[:, None] // RANK == jnp.arange(queries)[None, :]).astype(jnp.float32)
        partial_value = jnp.einsum("pic,cq->piq", by_column, pick, precision=lax.Precision.HIGHEST)
    partial_value = jnp.stack(
        [lax.dynamic_index_in_dim(partial_value, (part - j) % parts, 0, False) for j in range(parts)]
    )
    whole = lax.psum(partial_value, ("parts", "layer"))
    here = lax.dynamic_index_in_dim(whole, part, 0, False)
    width = queries // layers
    return lax.dynamic_slice_in_dim(here, lax.axis_index("layer") * width, width, 1)


def solution(mesh):
    placed = (
        P("layer", "rows", None),
        P("layer", "rows", None),
        P("layer", ("parts", "rows"), None),
        P("layer", ("parts", "rows"), None),
        P("layer", "rows", None),
        P("layer", "rows", None),
        P("layer", "rows"),
        P("layer", "rows"),
    )
    return jax.shard_map(
        per_device,
        mesh=mesh,
        in_specs=placed,
        out_specs=P(("parts", "rows"), "layer"),
        check_vma=False,
    )
```

```python
import jax
import jax.numpy as jnp
from jax import lax
from jax.experimental import pallas as pl
from jax.experimental.pallas import tpu as pltpu
from jax.sharding import PartitionSpec as P

RANK = 8


damping = 0.1

VMEM_LIMIT = 56 * 1024 * 1024


def shift(value, axis, by):
    size = lax.axis_size(axis)
    return lax.ppermute(value, axis, [(i, (i + by) % size) for i in range(size)])


def along(value, by):
    size = lax.axis_size("rows")
    return lax.ppermute(value, "rows", [(i, i + by) for i in range(size) if 0 <= i + by < size])


def high_low(value):
    high = value.astype(jnp.bfloat16)
    low = (value - high.astype(jnp.float32)).astype(jnp.bfloat16)
    return high, low


def project_kernel(
    split, train_ref, basis_hidden_ref, basis_model_ref, eigen_hidden_ref, eigen_model_ref, out_ref, scaled_hidden, scaled_model
):
    step = pl.program_id(0)
    count = train_ref.shape[0]
    share = basis_hidden_ref.shape[0]

    @pl.when(step == 0)
    def _():
        for train, eigen, scaled in (
            (train_ref[:, :share], eigen_hidden_ref, scaled_hidden),
            (train_ref[:, share:], eigen_model_ref, scaled_model),
        ):
            inverse = 1.0 / (eigen[...] + damping)
            high, low = high_low(train.astype(jnp.float32) * inverse)
            scaled[:count, :] = high
            scaled[count:, :] = low

    def project(scaled, basis):
        both = jnp.dot(scaled[...], basis[...], preferred_element_type=jnp.float32)
        high, low = high_low(both[:count] + both[count:])
        out_ref[:count, :] = high
        out_ref[count:, :] = low

    @pl.when(step < split)
    def _():
        project(scaled_hidden, basis_hidden_ref)

    @pl.when(step >= split)
    def _():
        project(scaled_model, basis_model_ref)


def project(train, hidden_basis, model_basis, hidden_eigen, model_eigen):
    count = train.shape[0]
    hidden_share, hidden_width = hidden_basis.shape
    model_share, model_width = model_basis.shape
    tile = 512
    split = hidden_width // tile

    def whole(shape):
        return pl.BlockSpec(shape, lambda i: (0, 0))

    return pl.pallas_call(
        lambda *refs: project_kernel(split, *refs),
        grid=(split + model_width // tile,),
        in_specs=[
            whole(train.shape),
            pl.BlockSpec((hidden_share, tile), lambda i: (0, jnp.minimum(i, split - 1))),
            pl.BlockSpec((model_share, tile), lambda i: (0, jnp.maximum(i - split, 0))),
            whole(hidden_eigen.shape),
            whole(model_eigen.shape),
        ],
        out_specs=pl.BlockSpec((2 * count, tile), lambda i: (0, i)),
        out_shape=jax.ShapeDtypeStruct((2 * count, hidden_width + model_width), jnp.bfloat16),
        scratch_shapes=[
            pltpu.VMEM((2 * count, hidden_share), jnp.bfloat16),
            pltpu.VMEM((2 * count, model_share), jnp.bfloat16),
        ],
        compiler_params=pltpu.CompilerParams(vmem_limit_bytes=VMEM_LIMIT),
        cost_estimate=pl.CostEstimate(
            flops=4 * count * (hidden_share * hidden_width + model_share * model_width),
            bytes_accessed=2 * (hidden_share * hidden_width + model_share * model_width),
            transcendentals=0,
        ),
    )(train, hidden_basis, model_basis, hidden_eigen, model_eigen)


def gram_kernel(split, places, projected_ref, *refs):
    query_refs, gram_ref, query = refs[:-2], refs[-2], refs[-1]
    step = pl.program_id(0)
    count = gram_ref.shape[1]
    columns = query_refs[0].shape[0]
    for place, group in enumerate(places):
        rows = query_refs[group[0]][...]
        for other in group[1:]:
            rows = rows + query_refs[other][...]
        if len(places) > 1:
            place = lax.rem(lax.axis_index("rows") + place, len(places))
        query[pl.ds(pl.multiple_of(place * columns, columns), columns), :] = rows
    both = lax.dot_general(
        projected_ref[...], query[...], (((1,), (1,)), ((), ())), preferred_element_type=jnp.float32
    )
    term = both[:count] + both[count:]
    first = jnp.logical_or(step == 0, step == split)

    @pl.when(first)
    def _():
        gram_ref[0] = term

    @pl.when(jnp.logical_not(first))
    def _():
        gram_ref[0] += term


def grams(projected, queries, places, hidden_width):
    count, width = projected.shape[0] // 2, projected.shape[1]
    columns = queries[0].shape[0]
    held = len(places) * columns
    tile = 1024
    split = hidden_width // tile
    return pl.pallas_call(
        lambda *refs: gram_kernel(split, places, *refs),
        grid=(width // tile,),
        in_specs=[pl.BlockSpec((2 * count, tile), lambda i: (0, i))]
        + [pl.BlockSpec((columns, tile), lambda i: (0, i)) for _ in queries],
        out_specs=pl.BlockSpec((1, count, held), lambda i: (jnp.where(i < split, 0, 1), 0, 0)),
        out_shape=jax.ShapeDtypeStruct((2, count, held), jnp.float32),
        scratch_shapes=[pltpu.VMEM((held, tile), jnp.bfloat16)],
        compiler_params=pltpu.CompilerParams(vmem_limit_bytes=VMEM_LIMIT),
        cost_estimate=pl.CostEstimate(flops=1, bytes_accessed=4 * count * width, transcendentals=0),
    )(projected, *queries)


def exchange(partial):
    total = partial[:, :, 0]
    for k in range(1, lax.axis_size("rows")):
        total = total + shift(partial[:, :, k].astype(jnp.bfloat16), "rows", -k).astype(jnp.float32)
    return total


def along_four(query, projected, hidden_width, blocked):
    row = lax.axis_index("rows")
    columns = query.shape[0]
    after, before = [query], [query]
    for step in range(3):
        if step == 2:
            projected, after[2], before[2] = lax.optimization_barrier((projected, after[2], before[2]))
        after.append(along(after[-1], -1))
        before.append(along(before[-1], 1))
    most = grams(projected, [query, after[1], after[2], before[2], before[1]], ((0,), (1,), (2, 3), (4,)), hidden_width)
    total = exchange(blocked(most))

    total, last_after, last_before = lax.optimization_barrier((total, after[3], before[3]))
    partial = blocked(grams(projected, [last_after, last_before], ((0, 1),), hidden_width))
    first = jnp.where(row == 3, partial[:, :, 0], 0.0)
    final = jnp.where(row == 0, partial[:, :, 0], 0.0)
    for k in range(1, 4):
        ends = [(0, (0 - k) % 4), (3, (3 - k) % 4)]
        part = lax.ppermute(partial[:, :, k].astype(jnp.bfloat16), "rows", ends).astype(jnp.float32)
        source = (row + k) % 4
        first = first + jnp.where(source == 3, part, 0.0)
        final = final + jnp.where(source == 0, part, 0.0)
    between = jnp.zeros(first.shape[:-1] + (2 * columns,), jnp.float32)
    return total + jnp.concatenate([first, between, final], axis=-1)


def per_device(
    query_hidden,
    query_model,
    train_hidden,
    train_model,
    hidden_basis,
    model_basis,
    hidden_eigen,
    model_eigen,
):
    rows = lax.axis_size("rows")
    parts = lax.axis_size("parts")
    layers = lax.axis_size("layer")
    row = lax.axis_index("rows")
    part = lax.axis_index("parts")
    hidden_share, hidden_width = hidden_basis.shape[1:]
    model_share = model_basis.shape[1]
    held = train_hidden.shape[1]
    columns = query_hidden.shape[1] // parts
    queries = query_hidden.shape[1] * rows // RANK

    def directions_of(owner):
        return jnp.concatenate(
            [
                lax.dynamic_slice_in_dim(train_hidden[0], owner * hidden_share, hidden_share, 1),
                lax.dynamic_slice_in_dim(train_model[0], owner * model_share, model_share, 1),
            ],
            axis=1,
        )

    blocks = [directions_of(row)]
    for k in range(1, rows):
        blocks.append(shift(directions_of((row + k) % rows), "rows", k))
    store = jnp.concatenate(blocks, axis=0)
    stores = jnp.concatenate([store] + [shift(store, "parts", j) for j in range(1, parts)], axis=0)

    query = jnp.concatenate(
        [
            lax.dynamic_slice_in_dim(query_hidden[0], part * columns, columns, 0),
            lax.dynamic_slice_in_dim(query_model[0], part * columns, columns, 0),
        ],
        axis=1,
    )

    def blocked(partial):
        return partial.reshape(2, parts, rows, held, partial.shape[-1])

    if rows == 4:
        projected = project(stores, hidden_basis[0], model_basis[0], hidden_eigen, model_eigen)
        total = along_four(query, projected, hidden_width, blocked)
    else:
        every = lax.all_gather(query, "rows", axis=0, tiled=True)

        def gram(basis, eigen, gathered, train):
            rotated = jnp.einsum("eh,qh->eq", basis, gathered, preferred_element_type=jnp.float32)
            scaled = (rotated * (1.0 / (eigen + damping))[:, None]).astype(jnp.bfloat16)
            return jnp.dot(train, scaled, preferred_element_type=jnp.float32)

        hidden_gram = gram(hidden_basis[0], hidden_eigen[0], every[:, :hidden_width], stores[:, :hidden_share])
        model_gram = gram(model_basis[0], model_eigen[0], every[:, hidden_width:], stores[:, hidden_share:])
        total = exchange(blocked(jnp.stack([hidden_gram, model_gram])))

    product = total[0] * total[1]
    examples = held // RANK
    by_column = product.reshape(parts, examples, RANK, rows * columns).sum(axis=2)
    if columns % RANK == 0:
        by_query = by_column.reshape(parts, examples, rows, 1, columns // RANK, RANK).sum(axis=-1)
        mine = lax.broadcasted_iota(jnp.int32, (1, 1, 1, parts, 1), 3) == part
        scores = jnp.where(mine, by_query, 0.0).reshape(parts, examples, queries)
    else:
        place = jnp.arange(rows * columns)
        place = (place // columns) * (columns * parts) + part * columns + place % columns
        pick = (place[:, None] // RANK == jnp.arange(queries)[None, :]).astype(jnp.float32)
        scores = jnp.einsum("pic,cq->piq", by_column, pick, precision=lax.Precision.HIGHEST)

    kept = scores[0]
    for j in range(1, parts):
        kept = kept + shift(scores[j], "parts", -j)
    layer = lax.axis_index("layer")
    width = queries // layers

    def queries_of(owner):
        return lax.dynamic_slice_in_dim(kept, owner * width, width, 1)

    result = queries_of(layer)
    for k in range(1, layers):
        result = result + shift(queries_of((layer + k) % layers), "layer", k)
    return result


def solution(mesh):
    placed = (
        P("layer", "rows", None),
        P("layer", "rows", None),
        P("layer", ("parts", "rows"), None),
        P("layer", ("parts", "rows"), None),
        P("layer", "rows", None),
        P("layer", "rows", None),
        P("layer", "rows"),
        P("layer", "rows"),
    )
    return jax.shard_map(
        per_device,
        mesh=mesh,
        in_specs=placed,
        out_specs=P(("parts", "rows"), "layer"),
        check_vma=False,
    )
```

```python
import jax
import jax.numpy as jnp
from jax import lax
from jax.experimental import pallas as pl
from jax.experimental.pallas import tpu as pltpu
from jax.sharding import PartitionSpec as P

RANK = 8


damping = 0.1

VMEM_LIMIT = 24 * 1024 * 1024


def shift(value, axis, by):
    size = lax.axis_size(axis)
    return lax.ppermute(value, axis, [(i, (i + by) % size) for i in range(size)])


def along(value, by):
    size = lax.axis_size("rows")
    return lax.ppermute(value, "rows", [(i, i + by) for i in range(size) if 0 <= i + by < size])


def rotate_kernel(basis_ref, eigen_ref, *refs):
    query_refs, out_ref, total = refs[:-2], refs[-2], refs[-1]
    step = pl.program_id(1)
    blocks = [ref[...] for ref in query_refs]
    query = blocks[0] if len(blocks) == 1 else jnp.concatenate(blocks, axis=0)
    term = lax.dot_general(
        query, basis_ref[...], (((1,), (1,)), ((), ())), preferred_element_type=jnp.float32
    )

    @pl.when(step == 0)
    def _():
        total[...] = term

    @pl.when(step != 0)
    def _():
        total[...] += term

    @pl.when(step == pl.num_programs(1) - 1)
    def _():
        out_ref[...] = (total[...] * (1.0 / (eigen_ref[...] + damping))).astype(jnp.bfloat16)


def rotate(basis, eigen, queries, start):
    share, width = basis.shape
    columns = queries[0].shape[0]
    held = columns * len(queries)
    tile, depth = 512, 2048
    first = start // depth
    return pl.pallas_call(
        rotate_kernel,
        grid=(share // tile, width // depth),
        in_specs=[
            pl.BlockSpec((tile, depth), lambda e, k: (e, k)),
            pl.BlockSpec((1, tile), lambda e, k: (0, e)),
        ]
        + [pl.BlockSpec((columns, depth), lambda e, k: (0, first + k)) for _ in queries],
        out_specs=pl.BlockSpec((held, tile), lambda e, k: (0, e)),
        out_shape=jax.ShapeDtypeStruct((held, share), jnp.bfloat16),
        scratch_shapes=[pltpu.VMEM((held, tile), jnp.float32)],
        compiler_params=pltpu.CompilerParams(vmem_limit_bytes=VMEM_LIMIT),
        cost_estimate=pl.CostEstimate(flops=1, bytes_accessed=1, transcendentals=0),
    )(
        pltpu.with_memory_space_constraint(basis, pltpu.HBM),
        eigen,
        *[pltpu.with_memory_space_constraint(query, pltpu.VMEM) for query in queries],
    )


def grams(stores, rotated, places):
    columns = rotated[0][0].shape[0]
    share = rotated[0][0].shape[1]
    count = stores.shape[0]
    held = columns * places

    def kernel(stores_ref, *refs):
        hidden_refs, model_refs = refs[:places], refs[places : 2 * places]
        gram_ref, sent_ref, hidden, model = refs[2 * places :]
        for place in range(places):
            where = place if places == 1 else lax.rem(lax.axis_index("rows") + place, places)
            rows = pl.ds(pl.multiple_of(where * columns, columns), columns)
            hidden[rows, :] = hidden_refs[place][...]
            model[rows, :] = model_refs[place][...]
        for side, (store, query) in enumerate(((stores_ref[:, :share], hidden), (stores_ref[:, share:], model))):
            gram = lax.dot_general(
                store, query[...], (((1,), (1,)), ((), ())), preferred_element_type=jnp.float32
            )
            gram_ref[side] = gram
            sent_ref[side] = gram.astype(jnp.bfloat16)

    return pl.pallas_call(
        kernel,
        out_shape=[
            jax.ShapeDtypeStruct((2, count, held), jnp.float32),
            jax.ShapeDtypeStruct((2, count, held), jnp.bfloat16),
        ],
        scratch_shapes=[pltpu.VMEM((held, side.shape[1]), jnp.bfloat16) for side in (rotated[0][0], rotated[1][0])],
        compiler_params=pltpu.CompilerParams(vmem_limit_bytes=VMEM_LIMIT),
        cost_estimate=pl.CostEstimate(
            flops=2 * count * held * stores.shape[1], bytes_accessed=2 * stores.size, transcendentals=0
        ),
    )(stores, *rotated[0], *rotated[1])


def exchange(partial, sent):
    total = partial[:, :, 0]
    for k in range(1, lax.axis_size("rows")):
        total = total + shift(sent[:, :, k], "rows", -k).astype(jnp.float32)
    return total


def along_four(query, bases, eigens, stores, blocked):
    row = lax.axis_index("rows")
    columns = query.shape[0]
    width = bases[0].shape[1]

    def rotated(*queries):
        return [rotate(bases[side], eigens[side], queries, start) for side, start in enumerate((0, width))]

    after, before = along(query, -1), along(query, 1)
    own = rotated(query)
    own, after, before = lax.optimization_barrier((own, after, before))
    after_two, before_two = along(after, -1), along(before, 1)
    near = rotated(after, before)
    near, after_two, before_two = lax.optimization_barrier((near, after_two, before_two))
    two = [jnp.where(row < 2, after_two[:, s], before_two[:, s]) for s in (slice(0, width), slice(width, None))]
    three = [lax.ppermute(side, "rows", [(1, 0), (2, 3)]) for side in two]
    far = [rotate(bases[side], eigens[side], [two[side]], 0) for side in range(2)]
    most = [[own[s], near[s][:columns], far[s], near[s][columns:]] for s in range(2)]
    partial, sent = grams(stores, most, 4)
    total = exchange(blocked(partial), blocked(sent))

    total, three = lax.optimization_barrier((total, three))
    last = [rotate(bases[side], eigens[side], [three[side]], 0) for side in range(2)]
    partial, sent = grams(stores, [[side] for side in last], 1)
    partial, sent = blocked(partial), blocked(sent)
    first = jnp.where(row == 3, partial[:, :, 0], 0.0)
    final = jnp.where(row == 0, partial[:, :, 0], 0.0)
    for k in range(1, 4):
        ends = [(0, (0 - k) % 4), (3, (3 - k) % 4)]
        part = lax.ppermute(sent[:, :, k], "rows", ends).astype(jnp.float32)
        source = (row + k) % 4
        first = first + jnp.where(source == 3, part, 0.0)
        final = final + jnp.where(source == 0, part, 0.0)
    between = jnp.zeros(first.shape[:-1] + (2 * columns,), jnp.float32)
    return total + jnp.concatenate([first, between, final], axis=-1)


def per_device(
    query_hidden,
    query_model,
    train_hidden,
    train_model,
    hidden_basis,
    model_basis,
    hidden_eigen,
    model_eigen,
):
    rows = lax.axis_size("rows")
    parts = lax.axis_size("parts")
    layers = lax.axis_size("layer")
    row = lax.axis_index("rows")
    part = lax.axis_index("parts")
    hidden_share = hidden_basis.shape[1]
    model_share = model_basis.shape[1]
    held = train_hidden.shape[1]
    columns = query_hidden.shape[1] // parts
    queries = query_hidden.shape[1] * rows // RANK

    def directions_of(owner):
        return jnp.concatenate(
            [
                lax.dynamic_slice_in_dim(train_hidden[0], owner * hidden_share, hidden_share, 1),
                lax.dynamic_slice_in_dim(train_model[0], owner * model_share, model_share, 1),
            ],
            axis=1,
        )

    blocks = [directions_of(row)]
    for k in range(1, rows):
        blocks.append(shift(directions_of((row + k) % rows), "rows", k))
    store = jnp.concatenate(blocks, axis=0)
    stores = jnp.concatenate([store] + [shift(store, "parts", j) for j in range(1, parts)], axis=0)

    query = jnp.concatenate(
        [lax.dynamic_slice_in_dim(side[0], part * columns, columns, 0) for side in (query_hidden, query_model)],
        axis=1,
    )

    def blocked(partial):
        return partial.reshape(2, parts, rows, held, partial.shape[-1])

    if rows == 4:
        total = along_four(query, [hidden_basis[0], model_basis[0]], [hidden_eigen, model_eigen], stores, blocked)
    else:
        every = lax.all_gather(query, "rows", axis=0, tiled=True)
        width = hidden_basis.shape[2]

        def gram(basis, eigen, gathered, train):
            rotated = jnp.einsum("eh,qh->eq", basis, gathered, preferred_element_type=jnp.float32)
            scaled = (rotated * (1.0 / (eigen + damping))[:, None]).astype(jnp.bfloat16)
            return jnp.dot(train, scaled, preferred_element_type=jnp.float32)

        hidden_gram = gram(hidden_basis[0], hidden_eigen[0], every[:, :width], stores[:, :hidden_share])
        model_gram = gram(model_basis[0], model_eigen[0], every[:, width:], stores[:, hidden_share:])
        both = blocked(jnp.stack([hidden_gram, model_gram]))
        total = exchange(both, both.astype(jnp.bfloat16))

    product = total[0] * total[1]
    examples = held // RANK
    by_column = product.reshape(parts, examples, RANK, rows * columns).sum(axis=2)
    if columns % RANK == 0:
        by_query = by_column.reshape(parts, examples, rows, 1, columns // RANK, RANK).sum(axis=-1)
        mine = lax.broadcasted_iota(jnp.int32, (1, 1, 1, parts, 1), 3) == part
        scores = jnp.where(mine, by_query, 0.0).reshape(parts, examples, queries)
    else:
        place = jnp.arange(rows * columns)
        place = (place // columns) * (columns * parts) + part * columns + place % columns
        pick = (place[:, None] // RANK == jnp.arange(queries)[None, :]).astype(jnp.float32)
        scores = jnp.einsum("pic,cq->piq", by_column, pick, precision=lax.Precision.HIGHEST)

    kept = scores[0]
    for j in range(1, parts):
        kept = kept + shift(scores[j], "parts", -j)
    layer = lax.axis_index("layer")
    width = queries // layers

    def queries_of(owner):
        return lax.dynamic_slice_in_dim(kept, owner * width, width, 1)

    result = queries_of(layer)
    for k in range(1, layers):
        result = result + shift(queries_of((layer + k) % layers), "layer", k)
    return result


def solution(mesh):
    placed = (
        P("layer", "rows", None),
        P("layer", "rows", None),
        P("layer", ("parts", "rows"), None),
        P("layer", ("parts", "rows"), None),
        P("layer", "rows", None),
        P("layer", "rows", None),
        P("layer", "rows"),
        P("layer", "rows"),
    )
    return jax.shard_map(
        per_device,
        mesh=mesh,
        in_specs=placed,
        out_specs=P(("parts", "rows"), "layer"),
        check_vma=False,
    )
```

```python
import jax
import jax.numpy as jnp
from jax import lax
from jax.experimental import pallas as pl
from jax.experimental.pallas import tpu as pltpu
from jax.sharding import PartitionSpec as P

RANK = 8


damping = 0.1

VMEM_LIMIT = 24 * 1024 * 1024
STREAMS = 4
TILE = 512
DEPTH = 2048


def along(value, by):
    size = lax.axis_size("rows")
    return lax.ppermute(value, "rows", [(i, i + by) for i in range(size) if 0 <= i + by < size])


def rotate(bases, eigens, queries):
    columns = queries[0].shape[0]
    held = columns * len(queries)
    part = TILE // STREAMS
    depths = [basis.shape[1] // DEPTH for basis in bases]
    steps = [basis.shape[0] // TILE * depth for basis, depth in zip(bases, depths)]

    def place(side, i):
        i = jnp.minimum(i, steps[0] - 1) if side == 0 else jnp.maximum(i - steps[0], 0)
        return lax.div(i, depths[side]), lax.rem(i, depths[side])

    def basis_spec(side, stream):
        def index(i):
            tile, k = place(side, i)
            return tile * STREAMS + stream, k

        return pl.BlockSpec((part, DEPTH), index)

    def row_spec(side, height):
        return pl.BlockSpec((height, TILE), lambda i: (0, place(side, i)[0]))

    def query_index(i):
        return 0, jnp.where(i < steps[0], place(0, i)[1], depths[0] + place(1, i)[1])

    def kernel(*refs):
        basis_refs = refs[:STREAMS], refs[STREAMS : 2 * STREAMS]
        eigen_refs = refs[2 * STREAMS : 2 * STREAMS + 2]
        query_refs = refs[2 * STREAMS + 2 : -3]
        out_refs, total = refs[-3:-1], refs[-1]
        step = pl.program_id(0)
        blocks = [ref[...] for ref in query_refs]
        query = blocks[0] if len(blocks) == 1 else jnp.concatenate(blocks, axis=0)

        def one(side):
            k = place(side, step)[1]
            for stream, ref in enumerate(basis_refs[side]):
                where = slice(stream * part, (stream + 1) * part)
                term = lax.dot_general(
                    query, ref[...], (((1,), (1,)), ((), ())), preferred_element_type=jnp.float32
                )
                total[:, where] = jnp.where(k == 0, 0.0, total[:, where]) + term

            @pl.when(k == depths[side] - 1)
            def _():
                scale = 1.0 / (eigen_refs[side][...] + damping)
                out_refs[side][...] = (total[...] * scale).astype(jnp.bfloat16)

        @pl.when(step < steps[0])
        def _():
            one(0)

        @pl.when(step >= steps[0])
        def _():
            one(1)

    constrain = pltpu.with_memory_space_constraint
    return pl.pallas_call(
        kernel,
        grid=(sum(steps),),
        in_specs=[basis_spec(side, stream) for side in range(2) for stream in range(STREAMS)]
        + [row_spec(side, 1) for side in range(2)]
        + [pl.BlockSpec((columns, DEPTH), query_index) for _ in queries],
        out_specs=[row_spec(side, held) for side in range(2)],
        out_shape=[jax.ShapeDtypeStruct((held, basis.shape[0]), jnp.bfloat16) for basis in bases],
        scratch_shapes=[pltpu.VMEM((held, TILE), jnp.float32)],
        compiler_params=pltpu.CompilerParams(vmem_limit_bytes=VMEM_LIMIT),
        cost_estimate=pl.CostEstimate(flops=1, bytes_accessed=1, transcendentals=0),
    )(
        *[constrain(basis, pltpu.HBM) for basis in bases for _ in range(STREAMS)],
        *eigens,
        *[constrain(query, pltpu.VMEM) for query in queries],
    )


def grams(stores, near, two, three, rows):
    shares = [side.shape[1] for side in near]
    columns = two[0].shape[0]
    held = stores[0].shape[0] // rows
    count = len(stores)

    def kernel(*refs):
        store_refs, (out_ref, *queries) = refs[:count], refs[count + 6 :]
        row = lax.axis_index("rows")
        for side in range(2):
            near_ref, two_ref, three_ref = refs[count + side : count + 6 : 2]
            query = queries[side]

            def put(row_of, block, query=query):
                where = pl.multiple_of(row_of * columns, columns)
                query[pl.ds(where, columns), :] = block

            put(row, near_ref[:columns, :])
            put(lax.rem(row + 1, rows), near_ref[columns : 2 * columns, :])
            put(lax.rem(row + 3, rows), near_ref[2 * columns :, :])
            put(lax.rem(row + 2, rows), two_ref[...])

            @pl.when(row == 0)
            def _(put=put, three_ref=three_ref):
                put(3, three_ref[...])

            @pl.when(row == 3)
            def _(put=put, three_ref=three_ref):
                put(0, three_ref[...])

            begin = side * shares[0]
            for j, store_ref in enumerate(store_refs):
                gram = lax.dot_general(
                    store_ref[:, begin : begin + shares[side]],
                    query[...],
                    (((1,), (1,)), ((), ())),
                    preferred_element_type=jnp.float32,
                ).astype(jnp.bfloat16)
                for owner in range(rows):
                    out_ref[owner, side, j] = gram[owner * held : (owner + 1) * held]

    return pl.pallas_call(
        kernel,
        out_shape=jax.ShapeDtypeStruct((rows, 2, count, held, columns * rows), jnp.bfloat16),
        scratch_shapes=[pltpu.VMEM((columns * rows, share), jnp.bfloat16) for share in shares],
        compiler_params=pltpu.CompilerParams(vmem_limit_bytes=VMEM_LIMIT),
        cost_estimate=pl.CostEstimate(flops=1, bytes_accessed=1, transcendentals=0),
    )(*stores, *near, *two, *three)


def along_four(query, bases, eigens, stores):
    row = lax.axis_index("rows")
    after, before = along(query, -1), along(query, 1)
    after_two, before_two = along(after, -1), along(before, 1)
    near = rotate(bases, eigens, [query, after, before])
    near, after_two, before_two = lax.optimization_barrier((near, after_two, before_two))
    two = jnp.where(row < 2, after_two, before_two)
    three = lax.ppermute(two, "rows", [(1, 0), (2, 3)])
    two = rotate(bases, eigens, [two])
    two, three = lax.optimization_barrier((two, three))
    return grams(stores, near, two, rotate(bases, eigens, [three]), 4)


def per_device(
    query_hidden,
    query_model,
    train_hidden,
    train_model,
    hidden_basis,
    model_basis,
    hidden_eigen,
    model_eigen,
):
    rows = lax.axis_size("rows")
    parts = lax.axis_size("parts")
    layers = lax.axis_size("layer")
    part = lax.axis_index("parts")
    held = train_hidden.shape[1]
    columns = query_hidden.shape[1] // parts
    queries = query_hidden.shape[1] * rows // RANK
    bases = [hidden_basis[0], model_basis[0]]
    eigens = [hidden_eigen, model_eigen]
    share = bases[0].shape[0]
    width = bases[0].shape[1]

    query = jnp.concatenate(
        [lax.dynamic_slice_in_dim(side[0], part * columns, columns, 0) for side in (query_hidden, query_model)],
        axis=1,
    )

    by_owner = jnp.concatenate(
        [side[0].reshape(held, rows, -1).transpose(1, 0, 2) for side in (train_hidden, train_model)], axis=2
    )
    store = lax.all_to_all(by_owner, "rows", 0, 0, tiled=True).reshape(rows * held, -1)
    stores = [store]
    for j in range(1, parts):
        stores.append(lax.ppermute(store, "parts", [(i, (i + j) % parts) for i in range(parts)]))

    if rows == 4:
        partial = along_four(query, bases, eigens, stores)
    else:
        every = lax.all_gather(query, "rows", axis=0, tiled=True)
        sides = []
        for basis, eigen, gathered, begin in zip(bases, eigens, (every[:, :width], every[:, width:]), (0, share)):
            rotated = jnp.einsum("eh,qh->eq", basis, gathered, preferred_element_type=jnp.float32)
            scaled = (rotated * (1.0 / (eigen[0] + damping))[:, None]).astype(jnp.bfloat16)
            sides.append(
                [
                    jnp.dot(one[:, begin : begin + basis.shape[0]], scaled, preferred_element_type=jnp.float32)
                    for one in stores
                ]
            )
        partial = jnp.array(sides).astype(jnp.bfloat16)
        partial = partial.reshape(2, parts, rows, held, rows * columns).transpose(2, 0, 1, 3, 4)

    received = lax.all_to_all(partial, "rows", 0, 0, tiled=True)
    total = received.astype(jnp.float32).sum(axis=0)
    product = total[0] * total[1]
    examples = held // RANK
    by_column = product.reshape(parts, examples, RANK, rows * columns).sum(axis=2)
    if columns % RANK == 0:
        by_query = by_column.reshape(parts, examples, rows, 1, columns // RANK, RANK).sum(axis=-1)
        mine = lax.broadcasted_iota(jnp.int32, (1, 1, 1, parts, 1), 3) == part
        scores = jnp.where(mine, by_query, 0.0).reshape(parts, examples, queries)
    else:
        place = jnp.arange(rows * columns)
        place = (place // columns) * (columns * parts) + part * columns + place % columns
        pick = (place[:, None] // RANK == jnp.arange(queries)[None, :]).astype(jnp.float32)
        scores = jnp.einsum("pic,cq->piq", by_column, pick, precision=lax.Precision.HIGHEST)

    scores = jnp.stack([lax.dynamic_index_in_dim(scores, (part - j) % parts, 0, False) for j in range(parts)])
    scores = scores.reshape(parts, examples, layers, queries // layers).transpose(0, 2, 1, 3)
    scores = scores.reshape(parts * layers, examples, queries // layers)
    return lax.all_to_all(scores, ("parts", "layer"), 0, 0, tiled=True).sum(axis=0)


def solution(mesh):
    placed = (
        P("layer", "rows", None),
        P("layer", "rows", None),
        P("layer", ("parts", "rows"), None),
        P("layer", ("parts", "rows"), None),
        P("layer", "rows", None),
        P("layer", "rows", None),
        P("layer", "rows"),
        P("layer", "rows"),
    )
    return jax.shard_map(
        per_device,
        mesh=mesh,
        in_specs=placed,
        out_specs=P(("parts", "rows"), "layer"),
        check_vma=False,
    )
```

```python
import jax
import jax.numpy as jnp
from jax import lax
from jax.experimental import pallas as pl
from jax.experimental.pallas import tpu as pltpu
from jax.sharding import PartitionSpec as P

RANK = 8


damping = 0.1

VMEM_LIMIT = 16 * 1024 * 1024
TILE = 256


def along(value, by):
    size = lax.axis_size("rows")
    return lax.ppermute(value, "rows", [(i, i + by) for i in range(size) if 0 <= i + by < size])


def rotate(bases, eigens, queries, keep=False, kept=False):
    columns = queries[0].shape[0]
    held = columns * len(queries)
    count = len(queries)

    def kernel(*refs):
        basis_refs, eigen_refs, query_refs = refs[:2], refs[2:4], refs[4 : 4 + count]
        out_refs = refs[4 + count : 6 + count]
        here_refs = basis_refs if kept else refs[6 + count : 8 + count]
        query, *semaphores = refs[6 + count if kept else 8 + count :]
        tiles = [(side, tile) for side in range(2) for tile in range(basis_refs[side].shape[0] // TILE)]
        copies = []
        if not kept:
            for at, (side, tile) in enumerate(tiles):
                where = slice(tile * TILE, (tile + 1) * TILE)
                copies.append(
                    pltpu.make_async_copy(basis_refs[side].at[where], here_refs[side].at[where], semaphores[0].at[at])
                )
                copies[-1].start()
        for place, ref in enumerate(query_refs):
            query[place * columns : (place + 1) * columns, :] = ref[...]
        begins = (0, basis_refs[0].shape[1], query.shape[1])
        for at, (side, tile) in enumerate(tiles):
            where = slice(tile * TILE, (tile + 1) * TILE)
            if not kept:
                copies[at].wait()
            rotated = lax.dot_general(
                here_refs[side][where, :],
                query[:, begins[side] : begins[side + 1]],
                (((1,), (1,)), ((), ())),
                preferred_element_type=jnp.float32,
            )
            scale = 1.0 / (eigen_refs[side][where, :] + damping)
            out_refs[side][where, :] = (rotated * scale).astype(jnp.bfloat16)

    constrain = pltpu.with_memory_space_constraint
    in_vmem = pl.BlockSpec(memory_space=pltpu.VMEM)
    here = [pltpu.VMEM(basis.shape, basis.dtype) for basis in bases]
    copies = sum(basis.shape[0] for basis in bases) // TILE
    return pl.pallas_call(
        kernel,
        in_specs=[in_vmem if kept else pl.BlockSpec(memory_space=pltpu.HBM)] * 2 + [in_vmem] * (2 + count),
        out_specs=[in_vmem] * (4 if keep else 2),
        out_shape=[jax.ShapeDtypeStruct((basis.shape[0], held), jnp.bfloat16) for basis in bases]
        + (here if keep else []),
        scratch_shapes=([] if keep or kept else here)
        + [pltpu.VMEM((held, sum(basis.shape[1] for basis in bases)), jnp.bfloat16)]
        + ([] if kept else [pltpu.SemaphoreType.DMA((copies,))]),
        compiler_params=pltpu.CompilerParams(
            vmem_limit_bytes=VMEM_LIMIT if keep or kept else VMEM_LIMIT + 28 * 1024 * 1024
        ),
        cost_estimate=pl.CostEstimate(flops=1, bytes_accessed=1, transcendentals=0),
    )(
        *[constrain(basis, pltpu.VMEM if kept else pltpu.HBM) for basis in bases],
        *[constrain(one, pltpu.VMEM) for one in (*eigens, *queries)],
    )


def grams(stores, near, two, three, rows):
    shares = [side.shape[0] for side in near]
    columns = two[0].shape[1]
    held = stores[0].shape[0] // rows
    count = len(stores)

    def kernel(*refs):
        store_refs, out_ref = refs[:count], refs[count + 6]
        row = lax.axis_index("rows")
        for side in range(2):
            near_ref, two_ref, three_ref = refs[count + side : count + 6 : 2]
            begin = side * shares[0]
            for j, store_ref in enumerate(store_refs):
                store = store_ref[:, begin : begin + shares[side]]
                close, far, last = (
                    jnp.dot(store, ref[...], preferred_element_type=jnp.float32)
                    for ref in (near_ref, two_ref, three_ref)
                )
                own, after, before = (close[:, p * columns : (p + 1) * columns] for p in range(3))
                after = jnp.where(row == 3, last, after)
                before = jnp.where(row == 0, last, before)
                ring = [own, after, far, before]
                blocks = []
                for c in range(rows):
                    block = ring[c]
                    for r in range(1, rows):
                        block = jnp.where(row == r, ring[(c - r) % rows], block)
                    blocks.append(block)
                gram = jnp.concatenate(blocks, axis=1).astype(jnp.bfloat16)
                for owner in range(rows):
                    out_ref[owner, side, j] = gram[owner * held : (owner + 1) * held]

    return pl.pallas_call(
        kernel,
        out_shape=jax.ShapeDtypeStruct((rows, 2, count, held, columns * rows), jnp.bfloat16),
        compiler_params=pltpu.CompilerParams(vmem_limit_bytes=VMEM_LIMIT),
        cost_estimate=pl.CostEstimate(flops=1, bytes_accessed=1, transcendentals=0),
    )(*stores, *near, *two, *three)


def along_four(query, bases, eigens, stores):
    row = lax.axis_index("rows")
    eigens = [eigen.reshape(-1, 1) for eigen in eigens]
    after, before = along(query, -1), along(query, 1)
    after_two, before_two = along(after, -1), along(before, 1)
    near = rotate(bases, eigens, [query, after, before])
    near, after_two, before_two = lax.optimization_barrier((near, after_two, before_two))
    two = jnp.where(row < 2, after_two, before_two)
    three = lax.ppermute(two, "rows", [(1, 0), (2, 3)])
    *two, hidden_here, model_here = rotate(bases, eigens, [two], keep=True)
    two, three = lax.optimization_barrier((two, three))
    return grams(stores, near, two, rotate([hidden_here, model_here], eigens, [three], kept=True), 4)


def per_device(
    query_hidden,
    query_model,
    train_hidden,
    train_model,
    hidden_basis,
    model_basis,
    hidden_eigen,
    model_eigen,
):
    rows = lax.axis_size("rows")
    parts = lax.axis_size("parts")
    layers = lax.axis_size("layer")
    part = lax.axis_index("parts")
    held = train_hidden.shape[1]
    columns = query_hidden.shape[1] // parts
    queries = query_hidden.shape[1] * rows // RANK
    bases = [hidden_basis[0], model_basis[0]]
    eigens = [hidden_eigen, model_eigen]
    share = bases[0].shape[0]
    width = bases[0].shape[1]

    query = jnp.concatenate(
        [lax.dynamic_slice_in_dim(side[0], part * columns, columns, 0) for side in (query_hidden, query_model)],
        axis=1,
    )

    by_owner = jnp.concatenate(
        [side[0].reshape(held, rows, -1).transpose(1, 0, 2) for side in (train_hidden, train_model)], axis=2
    )
    store = lax.all_to_all(by_owner, "rows", 0, 0, tiled=True).reshape(rows * held, -1)
    stores = [store]
    for j in range(1, parts):
        stores.append(lax.ppermute(store, "parts", [(i, (i + j) % parts) for i in range(parts)]))

    if rows == 4:
        partial = along_four(query, bases, eigens, stores)
    else:
        every = lax.all_gather(query, "rows", axis=0, tiled=True)
        sides = []
        for basis, eigen, gathered, begin in zip(bases, eigens, (every[:, :width], every[:, width:]), (0, share)):
            rotated = jnp.einsum("eh,qh->eq", basis, gathered, preferred_element_type=jnp.float32)
            scaled = (rotated * (1.0 / (eigen[0] + damping))[:, None]).astype(jnp.bfloat16)
            sides.append(
                [
                    jnp.dot(one[:, begin : begin + basis.shape[0]], scaled, preferred_element_type=jnp.float32)
                    for one in stores
                ]
            )
        partial = jnp.array(sides).astype(jnp.bfloat16)
        partial = partial.reshape(2, parts, rows, held, rows * columns).transpose(2, 0, 1, 3, 4)

    received = lax.all_to_all(partial, "rows", 0, 0, tiled=True)
    total = received.astype(jnp.float32).sum(axis=0)
    product = total[0] * total[1]
    examples = held // RANK
    by_column = product.reshape(parts, examples, RANK, rows * columns).sum(axis=2)
    if columns % RANK == 0:
        by_query = by_column.reshape(parts, examples, rows, 1, columns // RANK, RANK).sum(axis=-1)
        mine = lax.broadcasted_iota(jnp.int32, (1, 1, 1, parts, 1), 3) == part
        scores = jnp.where(mine, by_query, 0.0).reshape(parts, examples, queries)
    else:
        place = jnp.arange(rows * columns)
        place = (place // columns) * (columns * parts) + part * columns + place % columns
        pick = (place[:, None] // RANK == jnp.arange(queries)[None, :]).astype(jnp.float32)
        scores = jnp.einsum("pic,cq->piq", by_column, pick, precision=lax.Precision.HIGHEST)

    scores = jnp.stack([lax.dynamic_index_in_dim(scores, (part - j) % parts, 0, False) for j in range(parts)])
    scores = scores.reshape(parts, examples, layers, queries // layers).transpose(0, 2, 1, 3)
    scores = scores.reshape(parts * layers, examples, queries // layers)
    return lax.all_to_all(scores, ("parts", "layer"), 0, 0, tiled=True).sum(axis=0)


def solution(mesh):
    placed = (
        P("layer", "rows", None),
        P("layer", "rows", None),
        P("layer", ("parts", "rows"), None),
        P("layer", ("parts", "rows"), None),
        P("layer", "rows", None),
        P("layer", "rows", None),
        P("layer", "rows"),
        P("layer", "rows"),
    )
    return jax.shard_map(
        per_device,
        mesh=mesh,
        in_specs=placed,
        out_specs=P(("parts", "rows"), "layer"),
        check_vma=False,
    )
```

```python
import jax
import jax.numpy as jnp
from jax import lax
from jax.experimental import pallas as pl
from jax.experimental.pallas import tpu as pltpu
from jax.sharding import PartitionSpec as P

RANK = 8


damping = 0.1

VMEM_LIMIT = 16 * 1024 * 1024
TILE = 256


def along(value, by):
    size = lax.axis_size("rows")
    return lax.ppermute(value, "rows", [(i, i + by) for i in range(size) if 0 <= i + by < size])


def rotate(bases, eigens, queries, keep=False, kept=False):
    columns = queries[0].shape[0]
    held = columns * len(queries)
    count = len(queries)

    def kernel(*refs):
        basis_refs, eigen_refs, query_refs = refs[:2], refs[2:4], refs[4 : 4 + count]
        out_refs = refs[4 + count : 6 + count]
        here_refs = basis_refs if kept else refs[6 + count : 8 + count]
        query, *semaphores = refs[6 + count if kept else 8 + count :]
        tiles = [(side, tile) for side in range(2) for tile in range(basis_refs[side].shape[0] // TILE)]
        copies = []
        if not kept:
            for at, (side, tile) in enumerate(tiles):
                where = slice(tile * TILE, (tile + 1) * TILE)
                copies.append(
                    pltpu.make_async_copy(basis_refs[side].at[where], here_refs[side].at[where], semaphores[0].at[at])
                )
                copies[-1].start()
        for place, ref in enumerate(query_refs):
            query[place * columns : (place + 1) * columns, :] = ref[...]
        begins = (0, basis_refs[0].shape[1], query.shape[1])
        for at, (side, tile) in enumerate(tiles):
            where = slice(tile * TILE, (tile + 1) * TILE)
            if not kept:
                copies[at].wait()
            rotated = lax.dot_general(
                here_refs[side][where, :],
                query[:, begins[side] : begins[side + 1]],
                (((1,), (1,)), ((), ())),
                preferred_element_type=jnp.float32,
            )
            scale = 1.0 / (eigen_refs[side][where, :] + damping)
            out_refs[side][where, :] = (rotated * scale).astype(jnp.bfloat16)

    constrain = pltpu.with_memory_space_constraint
    in_vmem = pl.BlockSpec(memory_space=pltpu.VMEM)
    here = [pltpu.VMEM(basis.shape, basis.dtype) for basis in bases]
    copies = sum(basis.shape[0] for basis in bases) // TILE
    return pl.pallas_call(
        kernel,
        in_specs=[in_vmem if kept else pl.BlockSpec(memory_space=pltpu.HBM)] * 2 + [in_vmem] * (2 + count),
        out_specs=[in_vmem] * (4 if keep else 2),
        out_shape=[jax.ShapeDtypeStruct((basis.shape[0], held), jnp.bfloat16) for basis in bases]
        + (here if keep else []),
        scratch_shapes=([] if keep or kept else here)
        + [pltpu.VMEM((held, sum(basis.shape[1] for basis in bases)), jnp.bfloat16)]
        + ([] if kept else [pltpu.SemaphoreType.DMA((copies,))]),
        compiler_params=pltpu.CompilerParams(
            vmem_limit_bytes=VMEM_LIMIT if keep or kept else VMEM_LIMIT + 28 * 1024 * 1024
        ),
        cost_estimate=pl.CostEstimate(flops=1, bytes_accessed=1, transcendentals=0),
    )(
        *[constrain(basis, pltpu.VMEM if kept else pltpu.HBM) for basis in bases],
        *[constrain(one, pltpu.VMEM) for one in (*eigens, *queries)],
    )


def packed_width(examples, columns):
    return -(-examples * columns // 128) * 128


def grams(stores, blocks, offsets, base=None):
    rows, parts = lax.axis_size("rows"), lax.axis_size("parts")
    shares = [side.shape[0] for side in blocks[0]]
    columns = blocks[0][0].shape[1] // len(offsets[0])
    count = len(stores)
    held = stores[0].shape[0] // rows
    examples = held // RANK
    width = packed_width(examples, columns)

    def kernel(*refs):
        store_refs, block_refs, out_ref = refs[:count], refs[count : count + 2 * len(blocks)], refs[-1]
        row, part = lax.axis_index("rows"), lax.axis_index("parts")
        if base is not None:
            base_ref = refs[-2]
            out_ref[...] = base_ref[...]

        def write():
            for at, block_offsets in enumerate(offsets):
                for j, store_ref in enumerate(store_refs):
                    sides = []
                    for side, begin in enumerate((0, shares[0])):
                        store = store_ref[:, begin : begin + shares[side]]
                        sides.append(
                            jnp.dot(store, block_refs[2 * at + side][...], preferred_element_type=jnp.float32)
                        )
                    owner_part = lax.rem(part + parts - j, parts)
                    for place, offset in enumerate(block_offsets):
                        shard = lax.rem(row + offset, rows) if base is None else jnp.where(row == 0, rows - 1, 0)
                        for owner in range(rows):
                            packed = []
                            for gram in sides:
                                pieces = [
                                    gram[
                                        owner * held + i * RANK : owner * held + (i + 1) * RANK,
                                        place * columns : (place + 1) * columns,
                                    ]
                                    for i in range(examples)
                                ]
                                fill = width - examples * columns
                                if fill:
                                    pieces.append(jnp.zeros((RANK, fill), jnp.float32))
                                packed.append(jnp.concatenate(pieces, axis=1))
                            out_ref[owner_part, owner, shard] = jnp.concatenate(packed, axis=0).astype(jnp.bfloat16)

        if base is None:
            write()
        else:
            pl.when(jnp.logical_or(row == 0, row == rows - 1))(write)

    operands = [*stores, *[side for block in blocks for side in block]]
    return pl.pallas_call(
        kernel,
        out_shape=jax.ShapeDtypeStruct((parts, rows, rows, 2 * RANK, width), jnp.bfloat16),
        compiler_params=pltpu.CompilerParams(vmem_limit_bytes=VMEM_LIMIT),
        cost_estimate=pl.CostEstimate(flops=1, bytes_accessed=1, transcendentals=0),
    )(*operands, *([] if base is None else [base]))


def along_four(query, bases, eigens, by_owner):
    row = lax.axis_index("rows")
    columns = query.shape[0]
    eigens = [eigen.reshape(-1, 1) for eigen in eigens]
    after, before = along(query, -1), along(query, 1)
    store = to_owners(by_owner)
    *own, hidden_here, model_here = rotate(bases, eigens, [query], keep=True)
    bases = [hidden_here, model_here]
    own, store, after, before = lax.optimization_barrier((own, store, after, before))
    stores = to_parts(store)
    after_two, before_two = along(after, -1), along(before, 1)
    near = rotate(bases, eigens, [after, before], kept=True)
    near, stores, after_two, before_two = lax.optimization_barrier((near, stores, after_two, before_two))
    two = jnp.where(row < 2, after_two, before_two)
    three = lax.ppermute(two, "rows", [(1, 0), (2, 3)])
    far = rotate(bases, eigens, [two], kept=True)
    base = grams(stores, [own, near, far], [(0,), (1, 3), (2,)])
    base, three = lax.optimization_barrier((base, three))
    return grams(stores, [rotate(bases, eigens, [three], kept=True)], [(3,)], base)


def to_owners(by_owner):
    received = lax.all_to_all(by_owner, "rows", 0, 0, tiled=True)
    return received.reshape(-1, received.shape[-1])


def to_parts(store):
    parts = lax.axis_size("parts")
    return [store] + [
        lax.ppermute(store, "parts", [(i, (i + j) % parts) for i in range(parts)]) for j in range(1, parts)
    ]


def per_device(
    query_hidden,
    query_model,
    train_hidden,
    train_model,
    hidden_basis,
    model_basis,
    hidden_eigen,
    model_eigen,
):
    rows = lax.axis_size("rows")
    parts = lax.axis_size("parts")
    layers = lax.axis_size("layer")
    part = lax.axis_index("parts")
    held = train_hidden.shape[1]
    examples = held // RANK
    columns = query_hidden.shape[1] // parts
    width = query_hidden.shape[1] * rows // RANK // layers
    bases = [hidden_basis[0], model_basis[0]]
    eigens = [hidden_eigen, model_eigen]
    share = bases[0].shape[0]
    depth = bases[0].shape[1]

    query = jnp.concatenate(
        [lax.dynamic_slice_in_dim(side[0], part * columns, columns, 0) for side in (query_hidden, query_model)],
        axis=1,
    )
    by_owner = jnp.concatenate(
        [side[0].reshape(held, rows, -1).transpose(1, 0, 2) for side in (train_hidden, train_model)], axis=2
    )
    if rows == 4:
        partial = along_four(query, bases, eigens, by_owner)
    else:
        stores = to_parts(to_owners(by_owner))
        every = lax.all_gather(query, "rows", axis=0, tiled=True)
        sides = []
        for basis, eigen, gathered, begin in zip(bases, eigens, (every[:, :depth], every[:, depth:]), (0, share)):
            rotated = jnp.einsum("eh,qh->eq", basis, gathered, preferred_element_type=jnp.float32)
            scaled = (rotated * (1.0 / (eigen[0] + damping))[:, None]).astype(jnp.bfloat16)
            sides.append(
                [
                    jnp.dot(one[:, begin : begin + basis.shape[0]], scaled, preferred_element_type=jnp.float32)
                    for one in stores
                ]
            )
        partial = jnp.array(sides).reshape(2, parts, rows, examples, RANK, layers, rows // layers * columns)
        partial = partial.transpose(1, 2, 5, 0, 4, 3, 6).reshape(parts, rows, layers, 2 * RANK, -1)
        fill = packed_width(examples, rows // layers * columns) - partial.shape[-1]
        partial = jnp.pad(partial.astype(jnp.bfloat16), [(0, 0)] * 4 + [(0, fill)])
        partial = jnp.stack([lax.dynamic_index_in_dim(partial, (part - j) % parts, 0, False) for j in range(parts)])

    received = lax.all_to_all(
        partial.reshape((parts * rows * layers,) + partial.shape[3:]), ("parts", "rows", "layer"), 0, 0, tiled=True
    )
    gram = received.astype(jnp.float32).reshape(parts, rows, layers, 2, RANK, -1).sum(axis=1)
    by_column = (gram[:, :, 0] * gram[:, :, 1]).sum(axis=(1, 2))[:, : examples * width * RANK // parts]
    by_column = by_column.reshape(parts, examples, rows // layers, columns).transpose(1, 2, 0, 3)
    return by_column.reshape(examples, width, RANK).sum(axis=2)


def solution(mesh):
    placed = (
        P("layer", "rows", None),
        P("layer", "rows", None),
        P("layer", ("parts", "rows"), None),
        P("layer", ("parts", "rows"), None),
        P("layer", "rows", None),
        P("layer", "rows", None),
        P("layer", "rows"),
        P("layer", "rows"),
    )
    return jax.shard_map(
        per_device,
        mesh=mesh,
        in_specs=placed,
        out_specs=P(("parts", "rows"), "layer"),
        check_vma=False,
    )
```

```python
import jax
import jax.numpy as jnp
from jax import lax
from jax.experimental import pallas as pl
from jax.experimental.pallas import tpu as pltpu
from jax.sharding import PartitionSpec as P

RANK = 8


damping = 0.1

VMEM_LIMIT = 16 * 1024 * 1024
TILE = 256
AHEAD = 3


def along(value, by):
    size = lax.axis_size("rows")
    return lax.ppermute(value, "rows", [(i, i + by) for i in range(size) if 0 <= i + by < size])


def rotate(bases, eigens, queries, begins, keep=False, kept=False):
    groups = [query if isinstance(query, tuple) else (query,) for query in queries]
    queries = [query for group in groups for query in group]
    columns = queries[0].shape[0]
    held = columns * len(groups)
    count, sides = len(queries), len(bases)
    tiles = [(side, tile) for side in range(sides) for tile in range(bases[side].shape[0] // TILE)]

    def kernel(*refs):
        refs = list(refs)
        take = lambda many: [refs.pop(0) for _ in range(many)]
        basis_refs, eigen_refs, query_refs, out_refs = take(sides), take(sides), take(count), take(sides)
        here_refs = take(sides) if keep else []
        query = take(1)[0]
        slots = None if keep or kept else take(1)[0]
        semaphores = None if kept else take(1)[0]

        def block(at):
            side, tile = tiles[at]
            where = slice(tile * TILE, (tile + 1) * TILE)
            if kept:
                return basis_refs[side].at[where]
            if keep:
                return here_refs[side].at[where]
            return slots.at[at % AHEAD, :, : basis_refs[side].shape[1]]

        def copy(at):
            side, tile = tiles[at]
            where = slice(tile * TILE, (tile + 1) * TILE)
            return pltpu.make_async_copy(basis_refs[side].at[where], block(at), semaphores.at[at])

        if not kept:
            for at in range(min(AHEAD, len(tiles))):
                copy(at).start()
        for place, group in enumerate(groups):
            block_of = query_refs.pop(0)[...]
            for _ in group[1:]:
                block_of = block_of + query_refs.pop(0)[...]
            query[place * columns : (place + 1) * columns, :] = block_of
        for at, (side, tile) in enumerate(tiles):
            where = slice(tile * TILE, (tile + 1) * TILE)
            if not kept:
                copy(at).wait()
            if keep and at + AHEAD < len(tiles):
                copy(at + AHEAD).start()
            rotated = lax.dot_general(
                block(at)[...],
                query[:, begins[side] : begins[side] + basis_refs[side].shape[1]],
                (((1,), (1,)), ((), ())),
                preferred_element_type=jnp.float32,
            )
            scale = 1.0 / (eigen_refs[side][where, :] + damping)
            out_refs[side][where, :] = (rotated * scale).astype(jnp.bfloat16)
            if not (keep or kept) and at + AHEAD < len(tiles):
                copy(at + AHEAD).start()

    constrain = pltpu.with_memory_space_constraint
    in_vmem = pl.BlockSpec(memory_space=pltpu.VMEM)
    scratch = [pltpu.VMEM((held, queries[0].shape[1]), jnp.bfloat16)]
    if not (keep or kept):
        scratch.append(pltpu.VMEM((AHEAD, TILE, max(basis.shape[1] for basis in bases)), jnp.bfloat16))
    if not kept:
        scratch.append(pltpu.SemaphoreType.DMA((len(tiles),)))
    return pl.pallas_call(
        kernel,
        in_specs=[in_vmem if kept else pl.BlockSpec(memory_space=pltpu.HBM)] * sides + [in_vmem] * (sides + count),
        out_specs=[in_vmem] * (2 * sides if keep else sides),
        out_shape=[jax.ShapeDtypeStruct((basis.shape[0], held), jnp.bfloat16) for basis in bases]
        + ([pltpu.VMEM(basis.shape, basis.dtype) for basis in bases] if keep else []),
        scratch_shapes=scratch,
        compiler_params=pltpu.CompilerParams(
            vmem_limit_bytes=VMEM_LIMIT if keep or kept else VMEM_LIMIT + 8 * 1024 * 1024
        ),
        cost_estimate=pl.CostEstimate(flops=1, bytes_accessed=1, transcendentals=0),
    )(
        *[constrain(basis, pltpu.VMEM if kept else pltpu.HBM) for basis in bases],
        *[constrain(one, pltpu.VMEM) for one in (*eigens, *queries)],
    )


def packed_width(examples, columns):
    return -(-examples * columns // 128) * 128


def grams(stores, blocks, offsets, base=None):
    rows, parts = lax.axis_size("rows"), lax.axis_size("parts")
    shares = [side.shape[0] for side in blocks[0]]
    columns = blocks[0][0].shape[1] // len(offsets[0])
    count = len(stores)
    held = stores[0].shape[0] // rows
    examples = held // RANK
    width = packed_width(examples, columns)

    def kernel(*refs):
        store_refs, block_refs, out_ref = refs[:count], refs[count : count + 2 * len(blocks)], refs[-1]
        row, part = lax.axis_index("rows"), lax.axis_index("parts")
        if base is not None:
            base_ref = refs[-2]
            out_ref[...] = base_ref[...]

        def write():
            for at, block_offsets in enumerate(offsets):
                for j, store_ref in enumerate(store_refs):
                    sides = []
                    for side, begin in enumerate((0, shares[0])):
                        store = store_ref[:, begin : begin + shares[side]]
                        sides.append(
                            jnp.dot(store, block_refs[2 * at + side][...], preferred_element_type=jnp.float32)
                        )
                    owner_part = lax.rem(part + parts - j, parts)
                    for place, offset in enumerate(block_offsets):
                        shard = lax.rem(row + offset, rows) if base is None else jnp.where(row == 0, rows - 1, 0)
                        for owner in range(rows):
                            packed = []
                            for gram in sides:
                                pieces = [
                                    gram[
                                        owner * held + i * RANK : owner * held + (i + 1) * RANK,
                                        place * columns : (place + 1) * columns,
                                    ]
                                    for i in range(examples)
                                ]
                                fill = width - examples * columns
                                if fill:
                                    pieces.append(jnp.zeros((RANK, fill), jnp.float32))
                                packed.append(jnp.concatenate(pieces, axis=1))
                            out_ref[owner_part, owner, shard] = jnp.concatenate(packed, axis=0).astype(jnp.bfloat16)

        if base is None:
            write()
        else:
            pl.when(jnp.logical_or(row == 0, row == rows - 1))(write)

    operands = [*stores, *[side for block in blocks for side in block]]
    return pl.pallas_call(
        kernel,
        out_shape=jax.ShapeDtypeStruct((parts, rows, rows, 2 * RANK, width), jnp.bfloat16),
        compiler_params=pltpu.CompilerParams(vmem_limit_bytes=VMEM_LIMIT),
        cost_estimate=pl.CostEstimate(flops=1, bytes_accessed=1, transcendentals=0),
    )(*operands, *([] if base is None else [base]))


def along_four(query, bases, eigens, by_owner):
    row = lax.axis_index("rows")
    depth = bases[0].shape[1]
    eigens = [eigen.reshape(-1, 1) for eigen in eigens]
    after, before = along(query, -1), along(query, 1)
    stores = to_parts(to_owners(by_owner))
    after_two, before_two = along(after, -1), along(before, 1)
    near = rotate(bases, eigens, [query, after, before], (0, depth))
    near, after_two, before_two = lax.optimization_barrier((near, after_two, before_two))
    three_model, three_hidden = (
        lax.ppermute(jnp.where(row < 2, after_two[:, side], before_two[:, side]), "rows", [(1, 0), (2, 3)])
        for side in (slice(depth, None), slice(0, depth))
    )
    *far, hidden_here, model_here = rotate(bases, eigens, [(after_two, before_two)], (0, depth), keep=True)
    base = grams(stores, [near, far], [(0, 1, 3), (2,)])
    base, three_model = lax.optimization_barrier((base, three_model))
    last_model = rotate([model_here], eigens[1:], [three_model], (0,), kept=True)
    last_model, three_hidden = lax.optimization_barrier((last_model, three_hidden))
    last_hidden = rotate([hidden_here], eigens[:1], [three_hidden], (0,), kept=True)
    return grams(stores, [last_hidden + last_model], [(3,)], base)


def to_owners(by_owner):
    received = lax.all_to_all(by_owner, "rows", 0, 0, tiled=True)
    return received.reshape(-1, received.shape[-1])


def to_parts(store):
    parts = lax.axis_size("parts")
    return [store] + [
        lax.ppermute(store, "parts", [(i, (i + j) % parts) for i in range(parts)]) for j in range(1, parts)
    ]


def per_device(
    query_hidden,
    query_model,
    train_hidden,
    train_model,
    hidden_basis,
    model_basis,
    hidden_eigen,
    model_eigen,
):
    rows = lax.axis_size("rows")
    parts = lax.axis_size("parts")
    layers = lax.axis_size("layer")
    part = lax.axis_index("parts")
    held = train_hidden.shape[1]
    examples = held // RANK
    columns = query_hidden.shape[1] // parts
    width = query_hidden.shape[1] * rows // RANK // layers
    bases = [hidden_basis[0], model_basis[0]]
    eigens = [hidden_eigen, model_eigen]
    share = bases[0].shape[0]
    depth = bases[0].shape[1]

    query = jnp.concatenate(
        [lax.dynamic_slice_in_dim(side[0], part * columns, columns, 0) for side in (query_hidden, query_model)],
        axis=1,
    )
    by_owner = jnp.concatenate(
        [side[0].reshape(held, rows, -1).transpose(1, 0, 2) for side in (train_hidden, train_model)], axis=2
    )
    if rows == 4:
        partial = along_four(query, bases, eigens, by_owner)
    else:
        stores = to_parts(to_owners(by_owner))
        every = lax.all_gather(query, "rows", axis=0, tiled=True)
        sides = []
        for basis, eigen, gathered, begin in zip(bases, eigens, (every[:, :depth], every[:, depth:]), (0, share)):
            rotated = jnp.einsum("eh,qh->eq", basis, gathered, preferred_element_type=jnp.float32)
            scaled = (rotated * (1.0 / (eigen[0] + damping))[:, None]).astype(jnp.bfloat16)
            sides.append(
                [
                    jnp.dot(one[:, begin : begin + basis.shape[0]], scaled, preferred_element_type=jnp.float32)
                    for one in stores
                ]
            )
        partial = jnp.array(sides).reshape(2, parts, rows, examples, RANK, layers, rows // layers * columns)
        partial = partial.transpose(1, 2, 5, 0, 4, 3, 6).reshape(parts, rows, layers, 2 * RANK, -1)
        fill = packed_width(examples, rows // layers * columns) - partial.shape[-1]
        partial = jnp.pad(partial.astype(jnp.bfloat16), [(0, 0)] * 4 + [(0, fill)])
        partial = jnp.stack([lax.dynamic_index_in_dim(partial, (part - j) % parts, 0, False) for j in range(parts)])

    received = lax.all_to_all(
        partial.reshape((parts * rows * layers,) + partial.shape[3:]), ("parts", "rows", "layer"), 0, 0, tiled=True
    )
    gram = received.astype(jnp.float32).reshape(parts, rows, layers, 2, RANK, -1).sum(axis=1)
    by_column = (gram[:, :, 0] * gram[:, :, 1]).sum(axis=(1, 2))[:, : examples * width * RANK // parts]
    by_column = by_column.reshape(parts, examples, rows // layers, columns).transpose(1, 2, 0, 3)
    return by_column.reshape(examples, width, RANK).sum(axis=2)


def solution(mesh):
    placed = (
        P("layer", "rows", None),
        P("layer", "rows", None),
        P("layer", ("parts", "rows"), None),
        P("layer", ("parts", "rows"), None),
        P("layer", "rows", None),
        P("layer", "rows", None),
        P("layer", "rows"),
        P("layer", "rows"),
    )
    return jax.shard_map(
        per_device,
        mesh=mesh,
        in_specs=placed,
        out_specs=P(("parts", "rows"), "layer"),
        check_vma=False,
    )
```

```python
import jax
import jax.numpy as jnp
from jax import lax
from jax.experimental import pallas as pl
from jax.experimental.pallas import tpu as pltpu
from jax.sharding import PartitionSpec as P

RANK = 8


damping = 0.1

MIB = 1024 * 1024
TILE = 256
AHEAD = 4


def along(value, by):
    size = lax.axis_size("rows")
    return lax.ppermute(value, "rows", [(i, i + by) for i in range(size) if 0 <= i + by < size])


def rotate(bases, eigens, queries, begins, keep=False, kept=False):
    groups = [query if isinstance(query, tuple) else (query,) for query in queries]
    queries = [query for group in groups for query in group]
    columns = queries[0].shape[0]
    held = columns * len(groups)
    count, sides = len(queries), len(bases)
    tiles = [(side, tile) for side in range(sides) for tile in range(bases[side].shape[0] // TILE)]

    def kernel(*refs):
        refs = list(refs)
        take = lambda many: [refs.pop(0) for _ in range(many)]
        basis_refs, eigen_refs, query_refs, out_refs = take(sides), take(sides), take(count), take(sides)
        here_refs = take(sides) if keep else []
        query = take(1)[0]
        slots = None if keep or kept else take(1)[0]
        semaphores = None if kept else take(1)[0]

        def block(at):
            side, tile = tiles[at]
            where = slice(tile * TILE, (tile + 1) * TILE)
            if kept:
                return basis_refs[side].at[where]
            if keep:
                return here_refs[side].at[where]
            return slots.at[at % AHEAD, :, : basis_refs[side].shape[1]]

        def copy(at):
            side, tile = tiles[at]
            where = slice(tile * TILE, (tile + 1) * TILE)
            return pltpu.make_async_copy(basis_refs[side].at[where], block(at), semaphores.at[at])

        if not kept:
            for at in range(min(AHEAD, len(tiles))):
                copy(at).start(priority=at % 2)
        for place, group in enumerate(groups):
            block_of = query_refs.pop(0)[...]
            for _ in group[1:]:
                block_of = block_of + query_refs.pop(0)[...]
            query[place * columns : (place + 1) * columns, :] = block_of
        for at, (side, tile) in enumerate(tiles):
            where = slice(tile * TILE, (tile + 1) * TILE)
            if not kept:
                copy(at).wait()
            if keep and at + AHEAD < len(tiles):
                copy(at + AHEAD).start(priority=(at + AHEAD) % 2)
            rotated = lax.dot_general(
                block(at)[...],
                query[:, begins[side] : begins[side] + basis_refs[side].shape[1]],
                (((1,), (1,)), ((), ())),
                preferred_element_type=jnp.float32,
            )
            scale = 1.0 / (eigen_refs[side][where, :] + damping)
            out_refs[side][where, :] = (rotated * scale).astype(jnp.bfloat16)
            if not (keep or kept) and at + AHEAD < len(tiles):
                copy(at + AHEAD).start(priority=(at + AHEAD) % 2)

    constrain = pltpu.with_memory_space_constraint
    in_vmem = pl.BlockSpec(memory_space=pltpu.VMEM)
    scratch = [pltpu.VMEM((held, queries[0].shape[1]), jnp.bfloat16)]
    if not (keep or kept):
        scratch.append(pltpu.VMEM((AHEAD, TILE, max(basis.shape[1] for basis in bases)), jnp.bfloat16))
    if not kept:
        scratch.append(pltpu.SemaphoreType.DMA((len(tiles),)))
    return pl.pallas_call(
        kernel,
        in_specs=[in_vmem if kept else pl.BlockSpec(memory_space=pltpu.HBM)] * sides + [in_vmem] * (sides + count),
        out_specs=[in_vmem] * (2 * sides if keep else sides),
        out_shape=[jax.ShapeDtypeStruct((basis.shape[0], held), jnp.bfloat16) for basis in bases]
        + ([pltpu.VMEM(basis.shape, basis.dtype) for basis in bases] if keep else []),
        scratch_shapes=scratch,
        compiler_params=pltpu.CompilerParams(vmem_limit_bytes=(6 if keep or kept else 22) * MIB),
        cost_estimate=pl.CostEstimate(flops=1, bytes_accessed=1, transcendentals=0),
    )(
        *[constrain(basis, pltpu.VMEM if kept else pltpu.HBM) for basis in bases],
        *[constrain(one, pltpu.VMEM) for one in (*eigens, *queries)],
    )


def packed_width(examples, columns):
    return -(-examples * columns // 128) * 128


def grams(stores, blocks, offsets, base=None):
    rows, parts = lax.axis_size("rows"), lax.axis_size("parts")
    shares = [side.shape[0] for side in blocks[0]]
    columns = blocks[0][0].shape[1] // len(offsets[0])
    count = len(stores)
    held = stores[0].shape[0] // rows
    examples = held // RANK
    width = packed_width(examples, columns)

    def kernel(*refs):
        store_refs, block_refs, out_ref = refs[:count], refs[count : count + 2 * len(blocks)], refs[-1]
        row, part = lax.axis_index("rows"), lax.axis_index("parts")
        if base is not None:
            base_ref = refs[-2]
            out_ref[...] = base_ref[...]

        def write():
            for at, block_offsets in enumerate(offsets):
                for j, store_ref in enumerate(store_refs):
                    sides = []
                    for side, begin in enumerate((0, shares[0])):
                        store = store_ref[:, begin : begin + shares[side]]
                        sides.append(
                            jnp.dot(store, block_refs[2 * at + side][...], preferred_element_type=jnp.float32)
                        )
                    owner_part = lax.rem(part + parts - j, parts)
                    for place, offset in enumerate(block_offsets):
                        shard = lax.rem(row + offset, rows) if base is None else jnp.where(row == 0, rows - 1, 0)
                        for owner in range(rows):
                            packed = []
                            for gram in sides:
                                pieces = [
                                    gram[
                                        owner * held + i * RANK : owner * held + (i + 1) * RANK,
                                        place * columns : (place + 1) * columns,
                                    ]
                                    for i in range(examples)
                                ]
                                fill = width - examples * columns
                                if fill:
                                    pieces.append(jnp.zeros((RANK, fill), jnp.float32))
                                packed.append(jnp.concatenate(pieces, axis=1))
                            out_ref[owner_part, owner, shard] = jnp.concatenate(packed, axis=0).astype(jnp.bfloat16)

        if base is None:
            write()
        else:
            pl.when(jnp.logical_or(row == 0, row == rows - 1))(write)

    operands = [*stores, *[side for block in blocks for side in block]]
    return pl.pallas_call(
        kernel,
        out_shape=jax.ShapeDtypeStruct((parts, rows, rows, 2 * RANK, width), jnp.bfloat16),
        compiler_params=pltpu.CompilerParams(vmem_limit_bytes=6 * MIB),
        cost_estimate=pl.CostEstimate(flops=1, bytes_accessed=1, transcendentals=0),
    )(*operands, *([] if base is None else [base]))


def along_four(query, bases, eigens, by_owner):
    row = lax.axis_index("rows")
    depth = bases[0].shape[1]
    eigens = [eigen.reshape(-1, 1) for eigen in eigens]
    after, before = along(query, -1), along(query, 1)
    stores = to_parts(to_owners(by_owner))
    after_two, before_two = along(after, -1), along(before, 1)
    near = rotate(bases, eigens, [query, after, before], (0, depth))
    near, after_two, before_two = lax.optimization_barrier((near, after_two, before_two))
    three_model, three_hidden = (
        lax.ppermute(jnp.where(row < 2, after_two[:, side], before_two[:, side]), "rows", [(1, 0), (2, 3)])
        for side in (slice(depth, None), slice(0, depth))
    )
    *far, hidden_here, model_here = rotate(bases, eigens, [(after_two, before_two)], (0, depth), keep=True)
    base = grams(stores, [near, far], [(0, 1, 3), (2,)])
    base, three_model = lax.optimization_barrier((base, three_model))
    last_model = rotate([model_here], eigens[1:], [three_model], (0,), kept=True)
    last_model, three_hidden = lax.optimization_barrier((last_model, three_hidden))
    last_hidden = rotate([hidden_here], eigens[:1], [three_hidden], (0,), kept=True)
    return grams(stores, [last_hidden + last_model], [(3,)], base)


def to_owners(by_owner):
    received = lax.all_to_all(by_owner, "rows", 0, 0, tiled=True)
    return received.reshape(-1, received.shape[-1])


def to_parts(store):
    parts = lax.axis_size("parts")
    return [store] + [
        lax.ppermute(store, "parts", [(i, (i + j) % parts) for i in range(parts)]) for j in range(1, parts)
    ]


def per_device(
    query_hidden,
    query_model,
    train_hidden,
    train_model,
    hidden_basis,
    model_basis,
    hidden_eigen,
    model_eigen,
):
    rows = lax.axis_size("rows")
    parts = lax.axis_size("parts")
    layers = lax.axis_size("layer")
    part = lax.axis_index("parts")
    held = train_hidden.shape[1]
    examples = held // RANK
    columns = query_hidden.shape[1] // parts
    width = query_hidden.shape[1] * rows // RANK // layers
    bases = [hidden_basis[0], model_basis[0]]
    eigens = [hidden_eigen, model_eigen]
    share = bases[0].shape[0]
    depth = bases[0].shape[1]

    query = jnp.concatenate(
        [lax.dynamic_slice_in_dim(side[0], part * columns, columns, 0) for side in (query_hidden, query_model)],
        axis=1,
    )
    by_owner = jnp.concatenate(
        [side[0].reshape(held, rows, -1).transpose(1, 0, 2) for side in (train_hidden, train_model)], axis=2
    )
    if rows == 4:
        partial = along_four(query, bases, eigens, by_owner)
    else:
        stores = to_parts(to_owners(by_owner))
        every = lax.all_gather(query, "rows", axis=0, tiled=True)
        sides = []
        for basis, eigen, gathered, begin in zip(bases, eigens, (every[:, :depth], every[:, depth:]), (0, share)):
            rotated = jnp.einsum("eh,qh->eq", basis, gathered, preferred_element_type=jnp.float32)
            scaled = (rotated * (1.0 / (eigen[0] + damping))[:, None]).astype(jnp.bfloat16)
            sides.append(
                [
                    jnp.dot(one[:, begin : begin + basis.shape[0]], scaled, preferred_element_type=jnp.float32)
                    for one in stores
                ]
            )
        partial = jnp.array(sides).reshape(2, parts, rows, examples, RANK, layers, rows // layers * columns)
        partial = partial.transpose(1, 2, 5, 0, 4, 3, 6).reshape(parts, rows, layers, 2 * RANK, -1)
        fill = packed_width(examples, rows // layers * columns) - partial.shape[-1]
        partial = jnp.pad(partial.astype(jnp.bfloat16), [(0, 0)] * 4 + [(0, fill)])
        partial = jnp.stack([lax.dynamic_index_in_dim(partial, (part - j) % parts, 0, False) for j in range(parts)])

    received = lax.all_to_all(
        partial.reshape((parts * rows * layers,) + partial.shape[3:]), ("parts", "rows", "layer"), 0, 0, tiled=True
    )
    gram = received.astype(jnp.float32).reshape(parts, rows, layers, 2, RANK, -1).sum(axis=1)
    by_column = (gram[:, :, 0] * gram[:, :, 1]).sum(axis=(1, 2))[:, : examples * width * RANK // parts]
    by_column = by_column.reshape(parts, examples, rows // layers, columns).transpose(1, 2, 0, 3)
    return by_column.reshape(examples, width, RANK).sum(axis=2)


def solution(mesh):
    placed = (
        P("layer", "rows", None),
        P("layer", "rows", None),
        P("layer", ("parts", "rows"), None),
        P("layer", ("parts", "rows"), None),
        P("layer", "rows", None),
        P("layer", "rows", None),
        P("layer", "rows"),
        P("layer", "rows"),
    )
    return jax.shard_map(
        per_device,
        mesh=mesh,
        in_specs=placed,
        out_specs=P(("parts", "rows"), "layer"),
        check_vma=False,
    )
```

```python
import jax
import jax.numpy as jnp
from jax import lax
from jax.experimental import pallas as pl
from jax.experimental.pallas import tpu as pltpu
from jax.sharding import PartitionSpec as P

RANK = 8


damping = 0.1

MIB = 1024 * 1024
TILE = 256
AHEAD = 4


def along(value, by):
    size = lax.axis_size("rows")
    return lax.ppermute(value, "rows", [(i, i + by) for i in range(size) if 0 <= i + by < size])


def rotate(bases, eigens, queries, begins, kept):
    groups = [query if isinstance(query, tuple) else (query,) for query in queries]
    queries = [query for group in groups for query in group]
    columns = queries[0].shape[0]
    held = columns * len(groups)
    count, sides = len(queries), len(bases)
    tiles = [(side, tile) for side in range(sides) for tile in range(bases[side].shape[0] // TILE)]

    def kernel(*refs):
        refs = list(refs)
        take = lambda many: [refs.pop(0) for _ in range(many)]
        basis_refs, eigen_refs, query_refs, out_refs = take(sides), take(sides), take(count), take(sides)
        here_refs = [] if kept else take(sides)
        query = take(1)[0]
        semaphores = None if kept else take(1)[0]

        def block(at):
            side, tile = tiles[at]
            where = slice(tile * TILE, (tile + 1) * TILE)
            if kept:
                return basis_refs[side].at[where]
            return here_refs[side].at[where]

        def copy(at):
            side, tile = tiles[at]
            where = slice(tile * TILE, (tile + 1) * TILE)
            return pltpu.make_async_copy(basis_refs[side].at[where], block(at), semaphores.at[at])

        if not kept:
            for at in range(min(AHEAD, len(tiles))):
                copy(at).start(priority=at % 2)
        for place, group in enumerate(groups):
            block_of = query_refs.pop(0)[...]
            for _ in group[1:]:
                block_of = block_of + query_refs.pop(0)[...]
            query[place * columns : (place + 1) * columns, :] = block_of
        for at, (side, tile) in enumerate(tiles):
            where = slice(tile * TILE, (tile + 1) * TILE)
            if not kept:
                copy(at).wait()
            if not kept and at + AHEAD < len(tiles):
                copy(at + AHEAD).start(priority=(at + AHEAD) % 2)
            rotated = lax.dot_general(
                block(at)[...],
                query[:, begins[side] : begins[side] + basis_refs[side].shape[1]],
                (((1,), (1,)), ((), ())),
                preferred_element_type=jnp.float32,
            )
            scale = 1.0 / (eigen_refs[side][where, :] + damping)
            out_refs[side][where, :] = (rotated * scale).astype(jnp.bfloat16)

    constrain = pltpu.with_memory_space_constraint
    in_vmem = pl.BlockSpec(memory_space=pltpu.VMEM)
    scratch = [pltpu.VMEM((held, queries[0].shape[1]), jnp.bfloat16)]
    if not kept:
        scratch.append(pltpu.SemaphoreType.DMA((len(tiles),)))
    return pl.pallas_call(
        kernel,
        in_specs=[in_vmem if kept else pl.BlockSpec(memory_space=pltpu.HBM)] * sides + [in_vmem] * (sides + count),
        out_specs=[in_vmem] * (sides if kept else 2 * sides),
        out_shape=[jax.ShapeDtypeStruct((basis.shape[0], held), jnp.bfloat16) for basis in bases]
        + ([] if kept else [pltpu.VMEM(basis.shape, basis.dtype) for basis in bases]),
        scratch_shapes=scratch,
        compiler_params=pltpu.CompilerParams(vmem_limit_bytes=8 * MIB),
        cost_estimate=pl.CostEstimate(flops=1, bytes_accessed=1, transcendentals=0),
    )(
        *[constrain(basis, pltpu.VMEM if kept else pltpu.HBM) for basis in bases],
        *[constrain(one, pltpu.VMEM) for one in (*eigens, *queries)],
    )


def packed_width(examples, columns):
    return -(-examples * columns // 128) * 128


def grams(stores, blocks, offsets, base=None):
    rows, parts = lax.axis_size("rows"), lax.axis_size("parts")
    shares = [side.shape[0] for side in blocks[0]]
    columns = blocks[0][0].shape[1] // len(offsets[0])
    count = len(stores)
    held = stores[0].shape[0] // rows
    examples = held // RANK
    width = packed_width(examples, columns)

    def kernel(*refs):
        store_refs, block_refs, out_ref = refs[:count], refs[count : count + 2 * len(blocks)], refs[-1]
        row, part = lax.axis_index("rows"), lax.axis_index("parts")
        if base is not None:
            base_ref = refs[-2]
            out_ref[...] = base_ref[...]

        def write():
            for at, block_offsets in enumerate(offsets):
                for j, store_ref in enumerate(store_refs):
                    sides = []
                    for side, begin in enumerate((0, shares[0])):
                        store = store_ref[:, begin : begin + shares[side]]
                        sides.append(
                            jnp.dot(store, block_refs[2 * at + side][...], preferred_element_type=jnp.float32)
                        )
                    owner_part = lax.rem(part + parts - j, parts)
                    for place, offset in enumerate(block_offsets):
                        shard = lax.rem(row + offset, rows) if base is None else jnp.where(row == 0, rows - 1, 0)
                        for owner in range(rows):
                            packed = []
                            for gram in sides:
                                pieces = [
                                    gram[
                                        owner * held + i * RANK : owner * held + (i + 1) * RANK,
                                        place * columns : (place + 1) * columns,
                                    ]
                                    for i in range(examples)
                                ]
                                fill = width - examples * columns
                                if fill:
                                    pieces.append(jnp.zeros((RANK, fill), jnp.float32))
                                packed.append(jnp.concatenate(pieces, axis=1))
                            out_ref[owner_part, lax.rem(row + rows - owner, rows), shard] = jnp.concatenate(packed, axis=0).astype(jnp.bfloat16)

        if base is None:
            write()
        else:
            pl.when(jnp.logical_or(row == 0, row == rows - 1))(write)

    operands = [*stores, *[side for block in blocks for side in block]]
    return pl.pallas_call(
        kernel,
        out_shape=jax.ShapeDtypeStruct((parts, rows, rows, 2 * RANK, width), jnp.bfloat16),
        compiler_params=pltpu.CompilerParams(vmem_limit_bytes=6 * MIB),
        cost_estimate=pl.CostEstimate(flops=1, bytes_accessed=1, transcendentals=0),
    )(*operands, *([] if base is None else [base]))


def along_four(query, bases, eigens, by_owner):
    row = lax.axis_index("rows")
    depth = bases[0].shape[1]
    eigens = [eigen.reshape(-1, 1) for eigen in eigens]
    after = lax.ppermute(query, "rows", [(1, 0), (2, 1), (3, 2)])
    before = lax.ppermute(query, "rows", [(0, 1), (1, 2), (2, 3)])
    sent = [lax.dynamic_index_in_dim(by_owner, (row + k) % 4, 0, False) for k in range(4)]
    query, sent = lax.optimization_barrier((query, sent))
    blocks = to_owners(sent)
    *own, hidden_here, model_here = rotate(bases, eigens, [query], (0, depth), kept=False)
    bases = [hidden_here, model_here]
    own, bases, after, before = lax.optimization_barrier((own, bases, after, before))
    after_two = lax.ppermute(after, "rows", [(1, 0), (2, 1)])
    before_two = lax.ppermute(before, "rows", [(1, 2), (2, 3)])
    near = rotate(bases, eigens, [after, before], (0, depth), kept=True)
    near, blocks = lax.optimization_barrier((near, blocks))
    stores = to_parts(jnp.concatenate(blocks, axis=0))
    near, after_two, before_two = lax.optimization_barrier((near, after_two, before_two))
    two_hidden, two_model = (
        jnp.where(row < 2, after_two[:, side], before_two[:, side]) for side in (slice(0, depth), slice(depth, None))
    )
    ends = [(1, 0), (2, 3)]
    three_hidden = lax.ppermute(two_hidden, "rows", ends)
    far = rotate(bases, eigens, [(after_two, before_two)], (0, depth), kept=True)
    far, three_hidden, two_model = lax.optimization_barrier((far, three_hidden, two_model))
    base = grams(stores, [own, near, far], [(0,), (1, 3), (2,)])
    three_model = lax.ppermute(two_model, "rows", ends)
    last_hidden = rotate(bases[:1], eigens[:1], [three_hidden], (0,), kept=True)
    base, last_hidden, three_model = lax.optimization_barrier((base, last_hidden, three_model))
    last_model = rotate(bases[1:], eigens[1:], [three_model], (0,), kept=True)
    return grams(stores, [last_hidden + last_model], [(3,)], base)


def to_owners(sent):
    rows = lax.axis_size("rows")
    return sent[:1] + [
        lax.ppermute(sent[k], "rows", [(i, (i + k) % rows) for i in range(rows)]) for k in range(1, rows)
    ]


def to_parts(store):
    parts = lax.axis_size("parts")
    return [store] + [
        lax.ppermute(store, "parts", [(i, (i + j) % parts) for i in range(parts)]) for j in range(1, parts)
    ]


def per_device(
    query_hidden,
    query_model,
    train_hidden,
    train_model,
    hidden_basis,
    model_basis,
    hidden_eigen,
    model_eigen,
):
    rows = lax.axis_size("rows")
    parts = lax.axis_size("parts")
    layers = lax.axis_size("layer")
    part = lax.axis_index("parts")
    held = train_hidden.shape[1]
    examples = held // RANK
    columns = query_hidden.shape[1] // parts
    width = query_hidden.shape[1] * rows // RANK // layers
    bases = [hidden_basis[0], model_basis[0]]
    eigens = [hidden_eigen, model_eigen]
    share = bases[0].shape[0]
    depth = bases[0].shape[1]

    query = jnp.concatenate(
        [lax.dynamic_slice_in_dim(side[0], part * columns, columns, 0) for side in (query_hidden, query_model)],
        axis=1,
    )
    by_owner = jnp.concatenate(
        [side[0].reshape(held, rows, -1).transpose(1, 0, 2) for side in (train_hidden, train_model)], axis=2
    )
    if rows == 4:
        partial = along_four(query, bases, eigens, by_owner)
    else:
        received = lax.all_to_all(by_owner, "rows", 0, 0, tiled=True)
        stores = to_parts(received.reshape(rows * held, -1))
        every = lax.all_gather(query, "rows", axis=0, tiled=True)
        sides = []
        for basis, eigen, gathered, begin in zip(bases, eigens, (every[:, :depth], every[:, depth:]), (0, share)):
            rotated = jnp.einsum("eh,qh->eq", basis, gathered, preferred_element_type=jnp.float32)
            scaled = (rotated * (1.0 / (eigen[0] + damping))[:, None]).astype(jnp.bfloat16)
            sides.append(
                [
                    jnp.dot(one[:, begin : begin + basis.shape[0]], scaled, preferred_element_type=jnp.float32)
                    for one in stores
                ]
            )
        partial = jnp.array(sides).reshape(2, parts, rows, examples, RANK, layers, rows // layers * columns)
        partial = partial.transpose(1, 2, 5, 0, 4, 3, 6).reshape(parts, rows, layers, 2 * RANK, -1)
        fill = packed_width(examples, rows // layers * columns) - partial.shape[-1]
        partial = jnp.pad(partial.astype(jnp.bfloat16), [(0, 0)] * 4 + [(0, fill)])
        partial = jnp.stack([lax.dynamic_index_in_dim(partial, (part - j) % parts, 0, False) for j in range(parts)])

    received = lax.all_to_all(
        partial.reshape((parts * rows * layers,) + partial.shape[3:]), ("parts", "rows", "layer"), 0, 0, tiled=True
    )
    gram = received.astype(jnp.float32).reshape(parts, rows, layers, 2, RANK, -1).sum(axis=1)
    by_column = (gram[:, :, 0] * gram[:, :, 1]).sum(axis=(1, 2))[:, : examples * width * RANK // parts]
    by_column = by_column.reshape(parts, examples, rows // layers, columns).transpose(1, 2, 0, 3)
    return by_column.reshape(examples, width, RANK).sum(axis=2)


def solution(mesh):
    placed = (
        P("layer", "rows", None),
        P("layer", "rows", None),
        P("layer", ("parts", "rows"), None),
        P("layer", ("parts", "rows"), None),
        P("layer", "rows", None),
        P("layer", "rows", None),
        P("layer", "rows"),
        P("layer", "rows"),
    )
    return jax.shard_map(
        per_device,
        mesh=mesh,
        in_specs=placed,
        out_specs=P(("parts", "rows"), "layer"),
        check_vma=False,
    )
```

```python
import jax
import jax.numpy as jnp
from jax import lax
from jax.experimental import pallas as pl
from jax.experimental.pallas import tpu as pltpu
from jax.sharding import PartitionSpec as P

RANK = 8


damping = 0.1

MIB = 1024 * 1024
TILE = 256
AHEAD = 4


def along(value, by):
    size = lax.axis_size("rows")
    return lax.ppermute(value, "rows", [(i, i + by) for i in range(size) if 0 <= i + by < size])


def rotate(bases, eigens, queries, begins, kept):
    groups = [query if isinstance(query, tuple) else (query,) for query in queries]
    queries = [query for group in groups for query in group]
    columns = queries[0].shape[0]
    held = columns * len(groups)
    count, sides = len(queries), len(bases)
    tiles = [(side, tile) for side in range(sides) for tile in range(bases[side].shape[0] // TILE)]

    def kernel(*refs):
        refs = list(refs)
        take = lambda many: [refs.pop(0) for _ in range(many)]
        basis_refs, eigen_refs, query_refs, out_refs = take(sides), take(sides), take(count), take(sides)
        here_refs = [] if kept else take(sides)
        query = take(1)[0]
        semaphores = None if kept else take(1)[0]

        def block(at):
            side, tile = tiles[at]
            where = slice(tile * TILE, (tile + 1) * TILE)
            if kept:
                return basis_refs[side].at[where]
            return here_refs[side].at[where]

        def copy(at):
            side, tile = tiles[at]
            where = slice(tile * TILE, (tile + 1) * TILE)
            return pltpu.make_async_copy(basis_refs[side].at[where], block(at), semaphores.at[at])

        if not kept:
            for at in range(min(AHEAD, len(tiles))):
                copy(at).start(priority=at % 2)
        for place, group in enumerate(groups):
            block_of = query_refs.pop(0)[...]
            for _ in group[1:]:
                block_of = block_of + query_refs.pop(0)[...]
            query[place * columns : (place + 1) * columns, :] = block_of
        for at, (side, tile) in enumerate(tiles):
            where = slice(tile * TILE, (tile + 1) * TILE)
            if not kept:
                copy(at).wait()
            if not kept and at + AHEAD < len(tiles):
                copy(at + AHEAD).start(priority=(at + AHEAD) % 2)
            rotated = lax.dot_general(
                block(at)[...],
                query[:, begins[side] : begins[side] + basis_refs[side].shape[1]],
                (((1,), (1,)), ((), ())),
                preferred_element_type=jnp.float32,
            )
            scale = 1.0 / (eigen_refs[side][where, :] + damping)
            out_refs[side][where, :] = (rotated * scale).astype(jnp.bfloat16)

    constrain = pltpu.with_memory_space_constraint
    in_vmem = pl.BlockSpec(memory_space=pltpu.VMEM)
    scratch = [pltpu.VMEM((held, queries[0].shape[1]), jnp.bfloat16)]
    if not kept:
        scratch.append(pltpu.SemaphoreType.DMA((len(tiles),)))
    return pl.pallas_call(
        kernel,
        in_specs=[in_vmem if kept else pl.BlockSpec(memory_space=pltpu.HBM)] * sides + [in_vmem] * (sides + count),
        out_specs=[in_vmem] * (sides if kept else 2 * sides),
        out_shape=[jax.ShapeDtypeStruct((basis.shape[0], held), jnp.bfloat16) for basis in bases]
        + ([] if kept else [pltpu.VMEM(basis.shape, basis.dtype) for basis in bases]),
        scratch_shapes=scratch,
        compiler_params=pltpu.CompilerParams(vmem_limit_bytes=8 * MIB),
        cost_estimate=pl.CostEstimate(flops=1, bytes_accessed=1, transcendentals=0),
    )(
        *[constrain(basis, pltpu.VMEM if kept else pltpu.HBM) for basis in bases],
        *[constrain(one, pltpu.VMEM) for one in (*eigens, *queries)],
    )


def packed_width(examples, columns):
    return -(-examples * columns // 128) * 128


def grams(stores, blocks, offsets, base=None):
    rows, parts = lax.axis_size("rows"), lax.axis_size("parts")
    shares = [side.shape[0] for side in blocks[0]]
    columns = blocks[0][0].shape[1] // len(offsets[0])
    count = len(stores)
    held = stores[0].shape[0] // rows
    examples = held // RANK
    width = packed_width(examples, columns)

    def kernel(*refs):
        store_refs, block_refs, out_ref = refs[:count], refs[count : count + 2 * len(blocks)], refs[-1]
        row, part = lax.axis_index("rows"), lax.axis_index("parts")
        if base is not None:
            base_ref = refs[-2]
            out_ref[...] = base_ref[...]

        def write():
            for at, block_offsets in enumerate(offsets):
                for j, store_ref in enumerate(store_refs):
                    sides = []
                    for side, begin in enumerate((0, shares[0])):
                        store = store_ref[:, begin : begin + shares[side]]
                        sides.append(
                            jnp.dot(store, block_refs[2 * at + side][...], preferred_element_type=jnp.float32)
                        )
                    owner_part = lax.rem(part + parts - j, parts)
                    for place, offset in enumerate(block_offsets):
                        shard = lax.rem(row + offset, rows) if base is None else jnp.where(row == 0, rows - 1, 0)
                        for owner in range(rows):
                            packed = []
                            for gram in sides:
                                pieces = [
                                    gram[
                                        owner * held + i * RANK : owner * held + (i + 1) * RANK,
                                        place * columns : (place + 1) * columns,
                                    ]
                                    for i in range(examples)
                                ]
                                fill = width - examples * columns
                                if fill:
                                    pieces.append(jnp.zeros((RANK, fill), jnp.float32))
                                packed.append(jnp.concatenate(pieces, axis=1))
                            out_ref[owner_part, lax.rem(row + rows - owner, rows), shard] = jnp.concatenate(packed, axis=0).astype(jnp.bfloat16)

        if base is None:
            write()
        else:
            pl.when(jnp.logical_or(row == 0, row == rows - 1))(write)

    operands = [*stores, *[side for block in blocks for side in block]]
    return pl.pallas_call(
        kernel,
        out_shape=jax.ShapeDtypeStruct((parts, rows, rows, 2 * RANK, width), jnp.bfloat16),
        compiler_params=pltpu.CompilerParams(vmem_limit_bytes=6 * MIB),
        cost_estimate=pl.CostEstimate(flops=1, bytes_accessed=1, transcendentals=0),
    )(*operands, *([] if base is None else [base]))


def along_four(query, bases, eigens, by_owner):
    row = lax.axis_index("rows")
    depth = bases[0].shape[1]
    eigens = [eigen.reshape(-1, 1) for eigen in eigens]
    after = lax.ppermute(query, "rows", [(1, 0), (2, 1), (3, 2)])
    before = lax.ppermute(query, "rows", [(0, 1), (1, 2), (2, 3)])
    sent = [lax.dynamic_index_in_dim(by_owner, (row + k) % 4, 0, False) for k in range(4)]
    query, sent = lax.optimization_barrier((query, sent))
    blocks = to_owners(sent)
    *own, hidden_here, model_here = rotate(bases, eigens, [query], (0, depth), kept=False)
    bases = [hidden_here, model_here]
    own, after, before = lax.optimization_barrier((own, after, before))
    after_two = lax.ppermute(after, "rows", [(1, 0), (2, 1)])
    before_two = lax.ppermute(before, "rows", [(1, 2), (2, 3)])
    near = rotate(bases, eigens, [after, before], (0, depth), kept=True)
    near, blocks = lax.optimization_barrier((near, blocks))
    stores = to_parts(jnp.concatenate(blocks, axis=0))
    near, after_two, before_two = lax.optimization_barrier((near, after_two, before_two))
    two_hidden, two_model = (
        jnp.where(row < 2, after_two[:, side], before_two[:, side]) for side in (slice(0, depth), slice(depth, None))
    )
    ends = [(1, 0), (2, 3)]
    three_hidden = lax.ppermute(two_hidden, "rows", ends)
    far = rotate(bases, eigens, [(after_two, before_two)], (0, depth), kept=True)
    far, three_hidden, two_model = lax.optimization_barrier((far, three_hidden, two_model))
    base = grams(stores, [own, near, far], [(0,), (1, 3), (2,)])
    three_model = lax.ppermute(two_model, "rows", ends)
    last_hidden = rotate(bases[:1], eigens[:1], [three_hidden], (0,), kept=True)
    base, last_hidden, three_model = lax.optimization_barrier((base, last_hidden, three_model))
    last_model = rotate(bases[1:], eigens[1:], [three_model], (0,), kept=True)
    return grams(stores, [last_hidden + last_model], [(3,)], base)


def to_owners(sent):
    rows = lax.axis_size("rows")
    return sent[:1] + [
        lax.ppermute(sent[k], "rows", [(i, (i + k) % rows) for i in range(rows)]) for k in range(1, rows)
    ]


def to_parts(store):
    parts = lax.axis_size("parts")
    return [store] + [
        lax.ppermute(store, "parts", [(i, (i + j) % parts) for i in range(parts)]) for j in range(1, parts)
    ]


def per_device(
    query_hidden,
    query_model,
    train_hidden,
    train_model,
    hidden_basis,
    model_basis,
    hidden_eigen,
    model_eigen,
):
    rows = lax.axis_size("rows")
    parts = lax.axis_size("parts")
    layers = lax.axis_size("layer")
    part = lax.axis_index("parts")
    held = train_hidden.shape[1]
    examples = held // RANK
    columns = query_hidden.shape[1] // parts
    width = query_hidden.shape[1] * rows // RANK // layers
    bases = [hidden_basis[0], model_basis[0]]
    eigens = [hidden_eigen, model_eigen]
    share = bases[0].shape[0]
    depth = bases[0].shape[1]

    query = jnp.concatenate(
        [lax.dynamic_slice_in_dim(side[0], part * columns, columns, 0) for side in (query_hidden, query_model)],
        axis=1,
    )
    by_owner = jnp.concatenate(
        [side[0].reshape(held, rows, -1).transpose(1, 0, 2) for side in (train_hidden, train_model)], axis=2
    )
    if rows == 4:
        partial = along_four(query, bases, eigens, by_owner)
    else:
        received = lax.all_to_all(by_owner, "rows", 0, 0, tiled=True)
        stores = to_parts(received.reshape(rows * held, -1))
        every = lax.all_gather(query, "rows", axis=0, tiled=True)
        sides = []
        for basis, eigen, gathered, begin in zip(bases, eigens, (every[:, :depth], every[:, depth:]), (0, share)):
            rotated = jnp.einsum("eh,qh->eq", basis, gathered, preferred_element_type=jnp.float32)
            scaled = (rotated * (1.0 / (eigen[0] + damping))[:, None]).astype(jnp.bfloat16)
            sides.append(
                [
                    jnp.dot(one[:, begin : begin + basis.shape[0]], scaled, preferred_element_type=jnp.float32)
                    for one in stores
                ]
            )
        partial = jnp.array(sides).reshape(2, parts, rows, examples, RANK, layers, rows // layers * columns)
        partial = partial.transpose(1, 2, 5, 0, 4, 3, 6).reshape(parts, rows, layers, 2 * RANK, -1)
        fill = packed_width(examples, rows // layers * columns) - partial.shape[-1]
        partial = jnp.pad(partial.astype(jnp.bfloat16), [(0, 0)] * 4 + [(0, fill)])
        partial = jnp.stack([lax.dynamic_index_in_dim(partial, (part - j) % parts, 0, False) for j in range(parts)])

    received = lax.all_to_all(
        partial.reshape((parts * rows * layers,) + partial.shape[3:]), ("parts", "rows", "layer"), 0, 0, tiled=True
    )
    gram = received.astype(jnp.float32).reshape(parts, rows, layers, 2, RANK, -1).sum(axis=1)
    by_column = (gram[:, :, 0] * gram[:, :, 1]).sum(axis=(1, 2))[:, : examples * width * RANK // parts]
    by_column = by_column.reshape(parts, examples, rows // layers, columns).transpose(1, 2, 0, 3)
    return by_column.reshape(examples, width, RANK).sum(axis=2)


def solution(mesh):
    placed = (
        P("layer", "rows", None),
        P("layer", "rows", None),
        P("layer", ("parts", "rows"), None),
        P("layer", ("parts", "rows"), None),
        P("layer", "rows", None),
        P("layer", "rows", None),
        P("layer", "rows"),
        P("layer", "rows"),
    )
    return jax.shard_map(
        per_device,
        mesh=mesh,
        in_specs=placed,
        out_specs=P(("parts", "rows"), "layer"),
        check_vma=False,
    )
```

```python
import typing

import jax
import jax.numpy as jnp
from jax import lax
from jax.experimental import pallas as pl
from jax.experimental.pallas import tpu as pltpu
from jax.sharding import PartitionSpec as P

RANK = 8


damping = 0.1

MIB = 1024 * 1024
TILE = 256


def along(value, by):
    size = lax.axis_size("rows")
    return lax.ppermute(value, "rows", [(i, i + by) for i in range(size) if 0 <= i + by < size])


class Side(typing.NamedTuple):
    basis: jax.Array
    eigen: jax.Array
    begin: int | None
    here: bool = False
    keep: bool = False


def rotate(queries, sides):
    groups = [query if isinstance(query, tuple) else (query,) for query in queries]
    queries = [query for group in groups for query in group]
    columns = queries[0].shape[0]
    held = columns * len(groups)
    worked = [side for side in sides if side.begin is not None]
    kept = [side for side in sides if side.keep]
    tiles = [(side, tile) for side in sides for tile in range(side.basis.shape[0] // TILE)]
    copied = [at for at, (side, _) in enumerate(tiles) if not side.here]

    def kernel(*refs):
        refs = list(refs)
        take = lambda sides: {id(side): refs.pop(0) for side in sides}
        basis_refs, eigen_refs = take(sides), take(worked)
        query_refs = [refs.pop(0) for _ in queries]
        out_refs, here_refs, query = take(worked), take(kept), refs.pop(0)
        here_refs.update(take([side for side in sides if not (side.here or side.keep)]))

        def rows_of(at):
            return slice(tiles[at][1] * TILE, (tiles[at][1] + 1) * TILE)

        def copy(at):
            side = tiles[at][0]
            where = rows_of(at)
            return pltpu.make_async_copy(
                basis_refs[id(side)].at[where], here_refs[id(side)].at[where], refs[0].at[copied.index(at)]
            )

        for at in copied:
            copy(at).start()
        for place, group in enumerate(groups):
            block = query_refs.pop(0)[...]
            for _ in group[1:]:
                block = block + query_refs.pop(0)[...]
            query[place * columns : (place + 1) * columns, :] = block
        for at, (side, _) in enumerate(tiles):
            where = rows_of(at)
            if at in copied:
                copy(at).wait()
            if side.begin is None:
                continue
            basis_ref = (basis_refs if side.here else here_refs)[id(side)]
            rotated = lax.dot_general(
                basis_ref[where, :],
                query[:, side.begin : side.begin + side.basis.shape[1]],
                (((1,), (1,)), ((), ())),
                preferred_element_type=jnp.float32,
            )
            scale = 1.0 / (eigen_refs[id(side)][where, :] + damping)
            out_refs[id(side)][where, :] = (rotated * scale).astype(jnp.bfloat16)

    def here(side):
        return pltpu.VMEM(side.basis.shape, side.basis.dtype)

    constrain = pltpu.with_memory_space_constraint
    in_vmem = pl.BlockSpec(memory_space=pltpu.VMEM)
    operands = [constrain(side.basis, pltpu.VMEM if side.here else pltpu.HBM) for side in sides]
    operands += [constrain(one, pltpu.VMEM) for one in (*[side.eigen for side in worked], *queries)]
    streamed = [side for side in sides if not (side.here or side.keep)]
    return pl.pallas_call(
        kernel,
        in_specs=[in_vmem if side.here else pl.BlockSpec(memory_space=pltpu.HBM) for side in sides]
        + [in_vmem] * (len(worked) + len(queries)),
        out_specs=[in_vmem] * (len(worked) + len(kept)),
        out_shape=[jax.ShapeDtypeStruct((side.basis.shape[0], held), jnp.bfloat16) for side in worked]
        + [here(side) for side in kept],
        input_output_aliases={
            at: len(worked) + kept.index(side) for at, side in enumerate(sides) if side.here and side.keep
        },
        scratch_shapes=[pltpu.VMEM((held, queries[0].shape[1]), jnp.bfloat16)]
        + [here(side) for side in streamed]
        + ([pltpu.SemaphoreType.DMA((len(copied),))] if copied else []),
        compiler_params=pltpu.CompilerParams(vmem_limit_bytes=(16 if streamed else 6) * MIB),
        cost_estimate=pl.CostEstimate(flops=1, bytes_accessed=1, transcendentals=0),
    )(*operands)


def packed_width(examples, columns):
    return -(-examples * columns // 128) * 128


def grams(stores, blocks, offsets, base=None):
    rows, parts = lax.axis_size("rows"), lax.axis_size("parts")
    shares = [side.shape[0] for side in blocks[0]]
    columns = blocks[0][0].shape[1] // len(offsets[0])
    count = len(stores)
    held = stores[0].shape[0] // rows
    examples = held // RANK
    width = packed_width(examples, columns)

    def kernel(*refs):
        store_refs, block_refs, out_ref = refs[:count], refs[count : count + 2 * len(blocks)], refs[-1]
        row, part = lax.axis_index("rows"), lax.axis_index("parts")
        if base is not None:
            base_ref = refs[-2]
            out_ref[...] = base_ref[...]

        def write():
            for at, block_offsets in enumerate(offsets):
                for j, store_ref in enumerate(store_refs):
                    sides = []
                    for side, begin in enumerate((0, shares[0])):
                        store = store_ref[:, begin : begin + shares[side]]
                        sides.append(
                            jnp.dot(store, block_refs[2 * at + side][...], preferred_element_type=jnp.float32)
                        )
                    owner_part = lax.rem(part + parts - j, parts)
                    for place, offset in enumerate(block_offsets):
                        shard = lax.rem(row + offset, rows) if base is None else jnp.where(row == 0, rows - 1, 0)
                        for owner in range(rows):
                            packed = []
                            for gram in sides:
                                pieces = [
                                    gram[
                                        owner * held + i * RANK : owner * held + (i + 1) * RANK,
                                        place * columns : (place + 1) * columns,
                                    ]
                                    for i in range(examples)
                                ]
                                fill = width - examples * columns
                                if fill:
                                    pieces.append(jnp.zeros((RANK, fill), jnp.float32))
                                packed.append(jnp.concatenate(pieces, axis=1))
                            out_ref[owner_part, lax.rem(row + rows - owner, rows), shard] = jnp.concatenate(packed, axis=0).astype(jnp.bfloat16)

        if base is None:
            write()
        else:
            pl.when(jnp.logical_or(row == 0, row == rows - 1))(write)

    operands = [*stores, *[side for block in blocks for side in block]]
    return pl.pallas_call(
        kernel,
        out_shape=jax.ShapeDtypeStruct((parts, rows, rows, 2 * RANK, width), jnp.bfloat16),
        compiler_params=pltpu.CompilerParams(vmem_limit_bytes=6 * MIB),
        cost_estimate=pl.CostEstimate(flops=1, bytes_accessed=1, transcendentals=0),
    )(*operands, *([] if base is None else [base]))


def along_four(query, bases, eigens, by_owner):
    row = lax.axis_index("rows")
    depth = bases[0].shape[1]
    eigens = [eigen.reshape(-1, 1) for eigen in eigens]
    after = lax.ppermute(query, "rows", [(1, 0), (2, 1), (3, 2)])
    before = lax.ppermute(query, "rows", [(0, 1), (1, 2), (2, 3)])
    sent = [lax.dynamic_index_in_dim(by_owner, (row + k) % 4, 0, False) for k in range(4)]
    query, sent = lax.optimization_barrier((query, sent))
    blocks = to_owners(sent)
    hidden = Side(bases[0], eigens[0], 0, keep=True)
    model = Side(bases[1], eigens[1], depth)
    *own, basis = rotate([query], [hidden, model])
    own, after, before = lax.optimization_barrier((own, after, before))
    after_two = lax.ppermute(after, "rows", [(1, 0), (2, 1)])
    before_two = lax.ppermute(before, "rows", [(1, 2), (2, 3)])
    hidden = hidden._replace(basis=basis, here=True)
    *near, basis = rotate([after, before], [hidden, model])
    near, blocks = lax.optimization_barrier((near, blocks))
    stores = to_parts(jnp.concatenate(blocks, axis=0))
    near, after_two, before_two = lax.optimization_barrier((near, after_two, before_two))
    two_hidden, two_model = (
        jnp.where(row < 2, after_two[:, side], before_two[:, side]) for side in (slice(0, depth), slice(depth, None))
    )
    ends = [(1, 0), (2, 3)]
    three_hidden = lax.ppermute(two_hidden, "rows", ends)
    hidden = hidden._replace(basis=basis)
    *far, basis = rotate([(after_two, before_two)], [hidden, model])
    far, three_hidden, two_model = lax.optimization_barrier((far, three_hidden, two_model))
    base = grams(stores, [own, near, far], [(0,), (1, 3), (2,)])
    three_model = lax.ppermute(two_model, "rows", ends)
    hidden = hidden._replace(basis=basis, keep=False)
    last_hidden, basis = rotate([three_hidden], [hidden, model._replace(begin=None, keep=True)])
    base, last_hidden, three_model = lax.optimization_barrier((base, last_hidden, three_model))
    last_model = rotate([three_model], [model._replace(basis=basis, begin=0, here=True)])
    return grams(stores, [[last_hidden, *last_model]], [(3,)], base)


def to_owners(sent):
    rows = lax.axis_size("rows")
    return sent[:1] + [
        lax.ppermute(sent[k], "rows", [(i, (i + k) % rows) for i in range(rows)]) for k in range(1, rows)
    ]


def to_parts(store):
    parts = lax.axis_size("parts")
    return [store] + [
        lax.ppermute(store, "parts", [(i, (i + j) % parts) for i in range(parts)]) for j in range(1, parts)
    ]


def per_device(
    query_hidden,
    query_model,
    train_hidden,
    train_model,
    hidden_basis,
    model_basis,
    hidden_eigen,
    model_eigen,
):
    rows = lax.axis_size("rows")
    parts = lax.axis_size("parts")
    layers = lax.axis_size("layer")
    part = lax.axis_index("parts")
    held = train_hidden.shape[1]
    examples = held // RANK
    columns = query_hidden.shape[1] // parts
    width = query_hidden.shape[1] * rows // RANK // layers
    bases = [hidden_basis[0], model_basis[0]]
    eigens = [hidden_eigen, model_eigen]
    share = bases[0].shape[0]
    depth = bases[0].shape[1]

    query = jnp.concatenate(
        [lax.dynamic_slice_in_dim(side[0], part * columns, columns, 0) for side in (query_hidden, query_model)],
        axis=1,
    )
    by_owner = jnp.concatenate(
        [side[0].reshape(held, rows, -1).transpose(1, 0, 2) for side in (train_hidden, train_model)], axis=2
    )
    if rows == 4:
        partial = along_four(query, bases, eigens, by_owner)
    else:
        received = lax.all_to_all(by_owner, "rows", 0, 0, tiled=True)
        stores = to_parts(received.reshape(rows * held, -1))
        every = lax.all_gather(query, "rows", axis=0, tiled=True)
        sides = []
        for basis, eigen, gathered, begin in zip(bases, eigens, (every[:, :depth], every[:, depth:]), (0, share)):
            rotated = jnp.einsum("eh,qh->eq", basis, gathered, preferred_element_type=jnp.float32)
            scaled = (rotated * (1.0 / (eigen[0] + damping))[:, None]).astype(jnp.bfloat16)
            sides.append(
                [
                    jnp.dot(one[:, begin : begin + basis.shape[0]], scaled, preferred_element_type=jnp.float32)
                    for one in stores
                ]
            )
        partial = jnp.array(sides).reshape(2, parts, rows, examples, RANK, layers, rows // layers * columns)
        partial = partial.transpose(1, 2, 5, 0, 4, 3, 6).reshape(parts, rows, layers, 2 * RANK, -1)
        fill = packed_width(examples, rows // layers * columns) - partial.shape[-1]
        partial = jnp.pad(partial.astype(jnp.bfloat16), [(0, 0)] * 4 + [(0, fill)])
        partial = jnp.stack([lax.dynamic_index_in_dim(partial, (part - j) % parts, 0, False) for j in range(parts)])

    received = lax.all_to_all(
        partial.reshape((parts * rows * layers,) + partial.shape[3:]), ("parts", "rows", "layer"), 0, 0, tiled=True
    )
    gram = received.astype(jnp.float32).reshape(parts, rows, layers, 2, RANK, -1).sum(axis=1)
    by_column = (gram[:, :, 0] * gram[:, :, 1]).sum(axis=(1, 2))[:, : examples * width * RANK // parts]
    by_column = by_column.reshape(parts, examples, rows // layers, columns).transpose(1, 2, 0, 3)
    return by_column.reshape(examples, width, RANK).sum(axis=2)


def solution(mesh):
    placed = (
        P("layer", "rows", None),
        P("layer", "rows", None),
        P("layer", ("parts", "rows"), None),
        P("layer", ("parts", "rows"), None),
        P("layer", "rows", None),
        P("layer", "rows", None),
        P("layer", "rows"),
        P("layer", "rows"),
    )
    return jax.shard_map(
        per_device,
        mesh=mesh,
        in_specs=placed,
        out_specs=P(("parts", "rows"), "layer"),
        check_vma=False,
    )
```

```python
import jax
import jax.numpy as jnp
from jax import lax
from jax.experimental import pallas as pl
from jax.experimental.pallas import tpu as pltpu
from jax.sharding import PartitionSpec as P

RANK = 8


damping = 0.1

MIB = 1024 * 1024
TILE = 256


def along(value, by):
    size = lax.axis_size("rows")
    return lax.ppermute(value, "rows", [(i, i + by) for i in range(size) if 0 <= i + by < size])


def rotate(bases, eigens, queries, begins):
    groups = [query if isinstance(query, tuple) else (query,) for query in queries]
    queries = [query for group in groups for query in group]
    columns = queries[0].shape[0]
    held = columns * len(groups)
    sides = len(bases)

    def kernel(*refs):
        basis_refs, eigen_refs = refs[:sides], refs[sides : 2 * sides]
        query_refs = list(refs[2 * sides : 2 * sides + len(queries)])
        out_refs, query = refs[2 * sides + len(queries) : -1], refs[-1]
        for place, group in enumerate(groups):
            block = query_refs.pop(0)[...]
            for _ in group[1:]:
                block = block + query_refs.pop(0)[...]
            query[place * columns : (place + 1) * columns, :] = block
        for basis_ref, eigen_ref, out_ref, begin in zip(basis_refs, eigen_refs, out_refs, begins):
            share, width = basis_ref.shape
            for tile in range(share // TILE):
                where = slice(tile * TILE, (tile + 1) * TILE)
                rotated = lax.dot_general(
                    basis_ref[where, :],
                    query[:, begin : begin + width],
                    (((1,), (1,)), ((), ())),
                    preferred_element_type=jnp.float32,
                )
                out_ref[where, :] = (rotated * (1.0 / (eigen_ref[where, :] + damping))).astype(jnp.bfloat16)

    return pl.pallas_call(
        kernel,
        out_shape=[jax.ShapeDtypeStruct((basis.shape[0], held), jnp.bfloat16) for basis in bases],
        scratch_shapes=[pltpu.VMEM((held, queries[0].shape[1]), jnp.bfloat16)],
        compiler_params=pltpu.CompilerParams(vmem_limit_bytes=8 * MIB),
        cost_estimate=pl.CostEstimate(flops=1, bytes_accessed=1, transcendentals=0),
    )(*[pltpu.with_memory_space_constraint(one, pltpu.VMEM) for one in (*bases, *eigens, *queries)])


def packed_width(examples, columns):
    return -(-examples * columns // 128) * 128


def grams(stores, blocks, offsets, base=None):
    rows, parts = lax.axis_size("rows"), lax.axis_size("parts")
    shares = [side.shape[0] for side in blocks[0]]
    columns = blocks[0][0].shape[1] // len(offsets[0])
    count = len(stores)
    held = stores[0].shape[0] // rows
    examples = held // RANK
    width = packed_width(examples, columns)

    def kernel(*refs):
        store_refs, block_refs, out_ref = refs[:count], refs[count : count + 2 * len(blocks)], refs[-1]
        row, part = lax.axis_index("rows"), lax.axis_index("parts")
        if base is not None:
            base_ref = refs[-2]
            out_ref[...] = base_ref[...]

        def write():
            for at, block_offsets in enumerate(offsets):
                for j, store_ref in enumerate(store_refs):
                    sides = []
                    for side, begin in enumerate((0, shares[0])):
                        store = store_ref[:, begin : begin + shares[side]]
                        sides.append(
                            jnp.dot(store, block_refs[2 * at + side][...], preferred_element_type=jnp.float32)
                        )
                    owner_part = lax.rem(part + parts - j, parts)
                    for place, offset in enumerate(block_offsets):
                        shard = lax.rem(row + offset, rows) if base is None else jnp.where(row == 0, rows - 1, 0)
                        for owner in range(rows):
                            packed = []
                            for gram in sides:
                                pieces = [
                                    gram[
                                        owner * held + i * RANK : owner * held + (i + 1) * RANK,
                                        place * columns : (place + 1) * columns,
                                    ]
                                    for i in range(examples)
                                ]
                                fill = width - examples * columns
                                if fill:
                                    pieces.append(jnp.zeros((RANK, fill), jnp.float32))
                                packed.append(jnp.concatenate(pieces, axis=1))
                            out_ref[owner_part, lax.rem(row + rows - owner, rows), shard] = jnp.concatenate(packed, axis=0).astype(jnp.bfloat16)

        if base is None:
            write()
        else:
            pl.when(jnp.logical_or(row == 0, row == rows - 1))(write)

    operands = [*stores, *[side for block in blocks for side in block]]
    return pl.pallas_call(
        kernel,
        out_shape=jax.ShapeDtypeStruct((parts, rows, rows, 2 * RANK, width), jnp.bfloat16),
        compiler_params=pltpu.CompilerParams(vmem_limit_bytes=6 * MIB),
        cost_estimate=pl.CostEstimate(flops=1, bytes_accessed=1, transcendentals=0),
    )(*operands, *([] if base is None else [base]))


def along_four(query, bases, eigens, by_owner):
    row = lax.axis_index("rows")
    depth = bases[0].shape[1]
    eigens = [eigen.reshape(-1, 1) for eigen in eigens]
    after = lax.ppermute(query, "rows", [(1, 0), (2, 1), (3, 2)])
    before = lax.ppermute(query, "rows", [(0, 1), (1, 2), (2, 3)])
    sent = [lax.dynamic_index_in_dim(by_owner, (row + k) % 4, 0, False) for k in range(4)]
    query, sent = lax.optimization_barrier((query, sent))
    blocks = to_owners(sent)
    query, after, before = lax.optimization_barrier((query, after, before))
    after_two = lax.ppermute(after, "rows", [(1, 0), (2, 1)])
    before_two = lax.ppermute(before, "rows", [(1, 2), (2, 3)])
    near = rotate(bases, eigens, [query, after, before], (0, depth))
    near, blocks = lax.optimization_barrier((near, blocks))
    stores = to_parts(jnp.concatenate(blocks, axis=0))
    near, after_two, before_two = lax.optimization_barrier((near, after_two, before_two))
    two_hidden, two_model = (
        jnp.where(row < 2, after_two[:, side], before_two[:, side]) for side in (slice(0, depth), slice(depth, None))
    )
    ends = [(1, 0), (2, 3)]
    three_hidden = lax.ppermute(two_hidden, "rows", ends)
    far = rotate(bases, eigens, [(after_two, before_two)], (0, depth))
    far, three_hidden, two_model = lax.optimization_barrier((far, three_hidden, two_model))
    base = grams(stores, [near, far], [(0, 1, 3), (2,)])
    three_model = lax.ppermute(two_model, "rows", ends)
    last_hidden = rotate(bases[:1], eigens[:1], [three_hidden], (0,))
    base, last_hidden, three_model = lax.optimization_barrier((base, last_hidden, three_model))
    last_model = rotate(bases[1:], eigens[1:], [three_model], (0,))
    return grams(stores, [last_hidden + last_model], [(3,)], base)


def to_owners(sent):
    rows = lax.axis_size("rows")
    return sent[:1] + [
        lax.ppermute(sent[k], "rows", [(i, (i + k) % rows) for i in range(rows)]) for k in range(1, rows)
    ]


def to_parts(store):
    parts = lax.axis_size("parts")
    return [store] + [
        lax.ppermute(store, "parts", [(i, (i + j) % parts) for i in range(parts)]) for j in range(1, parts)
    ]


def per_device(
    query_hidden,
    query_model,
    train_hidden,
    train_model,
    hidden_basis,
    model_basis,
    hidden_eigen,
    model_eigen,
):
    rows = lax.axis_size("rows")
    parts = lax.axis_size("parts")
    layers = lax.axis_size("layer")
    part = lax.axis_index("parts")
    held = train_hidden.shape[1]
    examples = held // RANK
    columns = query_hidden.shape[1] // parts
    width = query_hidden.shape[1] * rows // RANK // layers
    bases = [hidden_basis[0], model_basis[0]]
    eigens = [hidden_eigen, model_eigen]
    share = bases[0].shape[0]
    depth = bases[0].shape[1]

    query = jnp.concatenate(
        [lax.dynamic_slice_in_dim(side[0], part * columns, columns, 0) for side in (query_hidden, query_model)],
        axis=1,
    )
    by_owner = jnp.concatenate(
        [side[0].reshape(held, rows, -1).transpose(1, 0, 2) for side in (train_hidden, train_model)], axis=2
    )
    if rows == 4:
        partial = along_four(query, bases, eigens, by_owner)
    else:
        received = lax.all_to_all(by_owner, "rows", 0, 0, tiled=True)
        stores = to_parts(received.reshape(rows * held, -1))
        every = lax.all_gather(query, "rows", axis=0, tiled=True)
        sides = []
        for basis, eigen, gathered, begin in zip(bases, eigens, (every[:, :depth], every[:, depth:]), (0, share)):
            rotated = jnp.einsum("eh,qh->eq", basis, gathered, preferred_element_type=jnp.float32)
            scaled = (rotated * (1.0 / (eigen[0] + damping))[:, None]).astype(jnp.bfloat16)
            sides.append(
                [
                    jnp.dot(one[:, begin : begin + basis.shape[0]], scaled, preferred_element_type=jnp.float32)
                    for one in stores
                ]
            )
        partial = jnp.array(sides).reshape(2, parts, rows, examples, RANK, layers, rows // layers * columns)
        partial = partial.transpose(1, 2, 5, 0, 4, 3, 6).reshape(parts, rows, layers, 2 * RANK, -1)
        fill = packed_width(examples, rows // layers * columns) - partial.shape[-1]
        partial = jnp.pad(partial.astype(jnp.bfloat16), [(0, 0)] * 4 + [(0, fill)])
        partial = jnp.stack([lax.dynamic_index_in_dim(partial, (part - j) % parts, 0, False) for j in range(parts)])

    received = lax.all_to_all(
        partial.reshape((parts * rows * layers,) + partial.shape[3:]), ("parts", "rows", "layer"), 0, 0, tiled=True
    )
    gram = received.astype(jnp.float32).reshape(parts, rows, layers, 2, RANK, -1).sum(axis=1)
    by_column = (gram[:, :, 0] * gram[:, :, 1]).sum(axis=(1, 2))[:, : examples * width * RANK // parts]
    by_column = by_column.reshape(parts, examples, rows // layers, columns).transpose(1, 2, 0, 3)
    return by_column.reshape(examples, width, RANK).sum(axis=2)


def solution(mesh):
    placed = (
        P("layer", "rows", None),
        P("layer", "rows", None),
        P("layer", ("parts", "rows"), None),
        P("layer", ("parts", "rows"), None),
        P("layer", "rows", None),
        P("layer", "rows", None),
        P("layer", "rows"),
        P("layer", "rows"),
    )
    return jax.shard_map(
        per_device,
        mesh=mesh,
        in_specs=placed,
        out_specs=P(("parts", "rows"), "layer"),
        check_vma=False,
    )
```

```python
import jax
import jax.numpy as jnp
from jax import lax
from jax.experimental import pallas as pl
from jax.experimental.pallas import tpu as pltpu
from jax.sharding import PartitionSpec as P

RANK = 8


damping = 0.1

MIB = 1024 * 1024
TILE = 256


def along(value, by):
    size = lax.axis_size("rows")
    return lax.ppermute(value, "rows", [(i, i + by) for i in range(size) if 0 <= i + by < size])


def rotate(bases, eigens, queries, begins):
    groups = [query if isinstance(query, tuple) else (query,) for query in queries]
    queries = [query for group in groups for query in group]
    columns = queries[0].shape[0]
    held = columns * len(groups)
    sides = len(bases)

    def kernel(*refs):
        basis_refs, eigen_refs = refs[:sides], refs[sides : 2 * sides]
        query_refs = list(refs[2 * sides : 2 * sides + len(queries)])
        out_refs, query = refs[2 * sides + len(queries) : -1], refs[-1]
        for place, group in enumerate(groups):
            block = query_refs.pop(0)[...]
            for _ in group[1:]:
                block = block + query_refs.pop(0)[...]
            query[place * columns : (place + 1) * columns, :] = block
        for basis_ref, eigen_ref, out_ref, begin in zip(basis_refs, eigen_refs, out_refs, begins):
            share, width = basis_ref.shape
            for tile in range(share // TILE):
                where = slice(tile * TILE, (tile + 1) * TILE)
                rotated = lax.dot_general(
                    basis_ref[where, :],
                    query[:, begin : begin + width],
                    (((1,), (1,)), ((), ())),
                    preferred_element_type=jnp.float32,
                )
                out_ref[where, :] = (rotated * (1.0 / (eigen_ref[where, :] + damping))).astype(jnp.bfloat16)

    return pl.pallas_call(
        kernel,
        out_shape=[jax.ShapeDtypeStruct((basis.shape[0], held), jnp.bfloat16) for basis in bases],
        scratch_shapes=[pltpu.VMEM((held, queries[0].shape[1]), jnp.bfloat16)],
        compiler_params=pltpu.CompilerParams(vmem_limit_bytes=8 * MIB),
        cost_estimate=pl.CostEstimate(flops=1, bytes_accessed=1, transcendentals=0),
    )(*[pltpu.with_memory_space_constraint(one, pltpu.VMEM) for one in (*bases, *eigens, *queries)])


def packed_width(examples, columns):
    return -(-examples * columns // 128) * 128


def grams(stores, blocks, offsets, base=None):
    rows, parts = lax.axis_size("rows"), lax.axis_size("parts")
    shares = [side.shape[0] for side in blocks[0]]
    columns = blocks[0][0].shape[1] // len(offsets[0])
    count = len(stores)
    held = stores[0].shape[0] // rows
    examples = held // RANK
    width = packed_width(examples, columns)

    def kernel(*refs):
        store_refs, block_refs, out_ref = refs[:count], refs[count : count + 2 * len(blocks)], refs[-1]
        row, part = lax.axis_index("rows"), lax.axis_index("parts")
        if base is not None:
            base_ref = refs[-2]
            out_ref[...] = base_ref[...]

        def write():
            for at, block_offsets in enumerate(offsets):
                for j, store_ref in enumerate(store_refs):
                    sides = []
                    for side, begin in enumerate((0, shares[0])):
                        store = store_ref[:, begin : begin + shares[side]]
                        sides.append(
                            jnp.dot(store, block_refs[2 * at + side][...], preferred_element_type=jnp.float32)
                        )
                    owner_part = lax.rem(part + parts - j, parts)
                    for place, offset in enumerate(block_offsets):
                        shard = lax.rem(row + offset, rows) if base is None else jnp.where(row == 0, rows - 1, 0)
                        for owner in range(rows):
                            packed = []
                            for gram in sides:
                                pieces = [
                                    gram[
                                        owner * held + i * RANK : owner * held + (i + 1) * RANK,
                                        place * columns : (place + 1) * columns,
                                    ]
                                    for i in range(examples)
                                ]
                                fill = width - examples * columns
                                if fill:
                                    pieces.append(jnp.zeros((RANK, fill), jnp.float32))
                                packed.append(jnp.concatenate(pieces, axis=1))
                            out_ref[owner_part, owner, shard] = jnp.concatenate(packed, axis=0).astype(jnp.bfloat16)

        if base is None:
            write()
        else:
            pl.when(jnp.logical_or(row == 0, row == rows - 1))(write)

    operands = [*stores, *[side for block in blocks for side in block]]
    return pl.pallas_call(
        kernel,
        out_shape=jax.ShapeDtypeStruct((parts, rows, rows, 2 * RANK, width), jnp.bfloat16),
        compiler_params=pltpu.CompilerParams(vmem_limit_bytes=6 * MIB),
        cost_estimate=pl.CostEstimate(flops=1, bytes_accessed=1, transcendentals=0),
    )(*operands, *([] if base is None else [base]))


def along_four(queries, bases, eigens, by_owner):
    row = lax.axis_index("rows")
    eigens = [eigen.reshape(-1, 1) for eigen in eigens]
    one = [
        (
            query,
            lax.ppermute(query, "rows", [(1, 0), (2, 1), (3, 2)]),
            lax.ppermute(query, "rows", [(0, 1), (1, 2), (2, 3)]),
        )
        for query in queries
    ]
    store = lax.all_to_all(by_owner, "rows", 0, 0, tiled=True)
    one = [lax.optimization_barrier(side) for side in one]
    two = [
        (lax.ppermute(after, "rows", [(1, 0), (2, 1)]), lax.ppermute(before, "rows", [(1, 2), (2, 3)]))
        for _, after, before in one
    ]
    near = [rotate([basis], [eigen], side, (0,))[0] for basis, eigen, side in zip(bases, eigens, one)]
    near, two, store = lax.optimization_barrier((near, two, store))
    stores = to_parts(store.reshape(-1, store.shape[-1]))
    model = jnp.where(row < 2, *two[1])
    model, two[0] = lax.optimization_barrier((model, two[0]))
    hidden = jnp.where(row < 2, *two[0])
    three = [lax.ppermute(side, "rows", [(1, 0), (2, 3)]) for side in (hidden, model)]
    far = [rotate([basis], [eigen], [pair], (0,))[0] for basis, eigen, pair in zip(bases, eigens, two)]
    base = grams(stores, [near, far], [(0, 1, 3), (2,)])
    base, three = lax.optimization_barrier((base, three))
    last = [rotate([basis], [eigen], [side], (0,))[0] for basis, eigen, side in zip(bases, eigens, three)]
    return grams(stores, [last], [(3,)], base)


def to_parts(store):
    parts = lax.axis_size("parts")
    return [store] + [
        lax.ppermute(store, "parts", [(i, (i + j) % parts) for i in range(parts)]) for j in range(1, parts)
    ]


def per_device(
    query_hidden,
    query_model,
    train_hidden,
    train_model,
    hidden_basis,
    model_basis,
    hidden_eigen,
    model_eigen,
):
    rows = lax.axis_size("rows")
    parts = lax.axis_size("parts")
    layers = lax.axis_size("layer")
    part = lax.axis_index("parts")
    held = train_hidden.shape[1]
    examples = held // RANK
    columns = query_hidden.shape[1] // parts
    width = query_hidden.shape[1] * rows // RANK // layers
    bases = [hidden_basis[0], model_basis[0]]
    eigens = [hidden_eigen, model_eigen]
    share = bases[0].shape[0]
    depth = bases[0].shape[1]

    own = [lax.dynamic_slice_in_dim(side[0], part * columns, columns, 0) for side in (query_hidden, query_model)]
    by_owner = jnp.concatenate(
        [side[0].reshape(held, rows, -1).transpose(1, 0, 2) for side in (train_hidden, train_model)], axis=2
    )
    if rows == 4:
        partial = along_four(own, bases, eigens, by_owner)
    else:
        received = lax.all_to_all(by_owner, "rows", 0, 0, tiled=True)
        stores = to_parts(received.reshape(rows * held, -1))
        every = lax.all_gather(jnp.concatenate(own, axis=1), "rows", axis=0, tiled=True)
        sides = []
        for basis, eigen, gathered, begin in zip(bases, eigens, (every[:, :depth], every[:, depth:]), (0, share)):
            rotated = jnp.einsum("eh,qh->eq", basis, gathered, preferred_element_type=jnp.float32)
            scaled = (rotated * (1.0 / (eigen[0] + damping))[:, None]).astype(jnp.bfloat16)
            sides.append(
                [
                    jnp.dot(one[:, begin : begin + basis.shape[0]], scaled, preferred_element_type=jnp.float32)
                    for one in stores
                ]
            )
        partial = jnp.array(sides).reshape(2, parts, rows, examples, RANK, layers, rows // layers * columns)
        partial = partial.transpose(1, 2, 5, 0, 4, 3, 6).reshape(parts, rows, layers, 2 * RANK, -1)
        fill = packed_width(examples, rows // layers * columns) - partial.shape[-1]
        partial = jnp.pad(partial.astype(jnp.bfloat16), [(0, 0)] * 4 + [(0, fill)])
        partial = jnp.stack([lax.dynamic_index_in_dim(partial, (part - j) % parts, 0, False) for j in range(parts)])

    received = lax.all_to_all(
        partial.reshape((parts * rows * layers,) + partial.shape[3:]), ("parts", "rows", "layer"), 0, 0, tiled=True
    )
    gram = received.astype(jnp.float32).reshape(parts, rows, layers, 2, RANK, -1).sum(axis=1)
    by_column = (gram[:, :, 0] * gram[:, :, 1]).sum(axis=(1, 2))[:, : examples * width * RANK // parts]
    by_column = by_column.reshape(parts, examples, rows // layers, columns).transpose(1, 2, 0, 3)
    return by_column.reshape(examples, width, RANK).sum(axis=2)


def solution(mesh):
    placed = (
        P("layer", "rows", None),
        P("layer", "rows", None),
        P("layer", ("parts", "rows"), None),
        P("layer", ("parts", "rows"), None),
        P("layer", "rows", None),
        P("layer", "rows", None),
        P("layer", "rows"),
        P("layer", "rows"),
    )
    return jax.shard_map(
        per_device,
        mesh=mesh,
        in_specs=placed,
        out_specs=P(("parts", "rows"), "layer"),
        check_vma=False,
    )
```

```python
import jax
import jax.numpy as jnp
from jax import lax
from jax.experimental import pallas as pl
from jax.experimental.pallas import tpu as pltpu
from jax.sharding import PartitionSpec as P

RANK = 8


damping = 0.1

MIB = 1024 * 1024
TILE = 256


def along(value, by):
    size = lax.axis_size("rows")
    return lax.ppermute(value, "rows", [(i, i + by) for i in range(size) if 0 <= i + by < size])


def rotate(bases, eigens, queries, begins):
    groups = [query if isinstance(query, tuple) else (query,) for query in queries]
    queries = [query for group in groups for query in group]
    columns = queries[0].shape[0]
    held = columns * len(groups)
    sides = len(bases)

    def kernel(*refs):
        basis_refs, eigen_refs = refs[:sides], refs[sides : 2 * sides]
        query_refs = list(refs[2 * sides : 2 * sides + len(queries)])
        out_refs, query = refs[2 * sides + len(queries) : -1], refs[-1]
        for place, group in enumerate(groups):
            block = query_refs.pop(0)[...]
            for _ in group[1:]:
                block = block + query_refs.pop(0)[...]
            query[place * columns : (place + 1) * columns, :] = block
        for basis_ref, eigen_ref, out_ref, begin in zip(basis_refs, eigen_refs, out_refs, begins):
            share, width = basis_ref.shape
            for tile in range(share // TILE):
                where = slice(tile * TILE, (tile + 1) * TILE)
                rotated = lax.dot_general(
                    basis_ref[where, :],
                    query[:, begin : begin + width],
                    (((1,), (1,)), ((), ())),
                    preferred_element_type=jnp.float32,
                )
                out_ref[where, :] = (rotated * (1.0 / (eigen_ref[where, :] + damping))).astype(jnp.bfloat16)

    return pl.pallas_call(
        kernel,
        out_shape=[jax.ShapeDtypeStruct((basis.shape[0], held), jnp.bfloat16) for basis in bases],
        scratch_shapes=[pltpu.VMEM((held, queries[0].shape[1]), jnp.bfloat16)],
        compiler_params=pltpu.CompilerParams(vmem_limit_bytes=8 * MIB),
        cost_estimate=pl.CostEstimate(flops=1, bytes_accessed=1, transcendentals=0),
    )(*[pltpu.with_memory_space_constraint(one, pltpu.VMEM) for one in (*bases, *eigens, *queries)])


def packed_width(examples, columns):
    return -(-examples * columns // 128) * 128


def grams(stores, blocks, offsets, base=None):
    rows, parts = lax.axis_size("rows"), lax.axis_size("parts")
    shares = [side.shape[0] for side in blocks[0]]
    columns = blocks[0][0].shape[1] // len(offsets[0])
    count = len(stores)
    held = stores[0].shape[0] // rows
    examples = held // RANK
    width = packed_width(examples, columns)

    def kernel(*refs):
        store_refs, block_refs, out_ref = refs[:count], refs[count : count + 2 * len(blocks)], refs[-1]
        row, part = lax.axis_index("rows"), lax.axis_index("parts")
        if base is not None:
            base_ref = refs[-2]
            out_ref[...] = base_ref[...]

        def write():
            for at, block_offsets in enumerate(offsets):
                for j, store_ref in enumerate(store_refs):
                    sides = []
                    for side, begin in enumerate((0, shares[0])):
                        store = store_ref[:, begin : begin + shares[side]]
                        sides.append(
                            jnp.dot(store, block_refs[2 * at + side][...], preferred_element_type=jnp.float32)
                        )
                    owner_part = lax.rem(part + parts - j, parts)
                    for place, offset in enumerate(block_offsets):
                        shard = lax.rem(row + offset, rows) if base is None else jnp.where(row == 0, rows - 1, 0)
                        for owner in range(rows):
                            packed = []
                            for gram in sides:
                                pieces = [
                                    gram[
                                        owner * held + i * RANK : owner * held + (i + 1) * RANK,
                                        place * columns : (place + 1) * columns,
                                    ]
                                    for i in range(examples)
                                ]
                                fill = width - examples * columns
                                if fill:
                                    pieces.append(jnp.zeros((RANK, fill), jnp.float32))
                                packed.append(jnp.concatenate(pieces, axis=1))
                            out_ref[owner_part, owner, shard] = jnp.concatenate(packed, axis=0).astype(jnp.bfloat16)

        if base is None:
            write()
        else:
            pl.when(jnp.logical_or(row == 0, row == rows - 1))(write)

    operands = [*stores, *[side for block in blocks for side in block]]
    return pl.pallas_call(
        kernel,
        out_shape=jax.ShapeDtypeStruct((parts, rows, rows, 2 * RANK, width), jnp.bfloat16),
        compiler_params=pltpu.CompilerParams(vmem_limit_bytes=6 * MIB),
        cost_estimate=pl.CostEstimate(flops=1, bytes_accessed=1, transcendentals=0),
    )(*operands, *([] if base is None else [base]))


def along_four(query, bases, eigens, by_owner):
    row = lax.axis_index("rows")
    depth = bases[0].shape[1]
    eigens = [eigen.reshape(-1, 1) for eigen in eigens]
    after = lax.ppermute(query, "rows", [(1, 0), (2, 1), (3, 2)])
    before = lax.ppermute(query, "rows", [(0, 1), (1, 2), (2, 3)])
    by_owner, query, after, before = lax.optimization_barrier((by_owner, query, after, before))
    store = lax.all_to_all(by_owner, "rows", 0, 0, tiled=True)
    after_two = lax.ppermute(after, "rows", [(1, 0), (2, 1)])
    before_two = lax.ppermute(before, "rows", [(1, 2), (2, 3)])
    near = rotate(bases, eigens, [query, after, before], (0, depth))
    near, store = lax.optimization_barrier((near, store))
    stores = to_parts(store.reshape(-1, store.shape[-1]))
    near, after_two, before_two = lax.optimization_barrier((near, after_two, before_two))
    two_hidden, two_model = (
        jnp.where(row < 2, after_two[:, side], before_two[:, side]) for side in (slice(0, depth), slice(depth, None))
    )
    ends = [(1, 0), (2, 3)]
    three_hidden = lax.ppermute(two_hidden, "rows", ends)
    far = rotate(bases, eigens, [(after_two, before_two)], (0, depth))
    far, three_hidden, two_model = lax.optimization_barrier((far, three_hidden, two_model))
    base = grams(stores, [near, far], [(0, 1, 3), (2,)])
    three_model = lax.ppermute(two_model, "rows", ends)
    last_hidden = rotate(bases[:1], eigens[:1], [three_hidden], (0,))
    base, last_hidden, three_model = lax.optimization_barrier((base, last_hidden, three_model))
    last_model = rotate(bases[1:], eigens[1:], [three_model], (0,))
    return grams(stores, [last_hidden + last_model], [(3,)], base)


def to_parts(store):
    parts = lax.axis_size("parts")
    return [store] + [
        lax.ppermute(store, "parts", [(i, (i + j) % parts) for i in range(parts)]) for j in range(1, parts)
    ]


def per_device(
    query_hidden,
    query_model,
    train_hidden,
    train_model,
    hidden_basis,
    model_basis,
    hidden_eigen,
    model_eigen,
):
    rows = lax.axis_size("rows")
    parts = lax.axis_size("parts")
    layers = lax.axis_size("layer")
    part = lax.axis_index("parts")
    held = train_hidden.shape[1]
    examples = held // RANK
    columns = query_hidden.shape[1] // parts
    width = query_hidden.shape[1] * rows // RANK // layers
    bases = [hidden_basis[0], model_basis[0]]
    eigens = [hidden_eigen, model_eigen]
    share = bases[0].shape[0]
    depth = bases[0].shape[1]

    query = jnp.concatenate(
        [lax.dynamic_slice_in_dim(side[0], part * columns, columns, 0) for side in (query_hidden, query_model)],
        axis=1,
    )
    by_owner = jnp.concatenate(
        [side[0].reshape(held, rows, -1).transpose(1, 0, 2) for side in (train_hidden, train_model)], axis=2
    )
    if rows == 4:
        partial = along_four(query, bases, eigens, by_owner)
    else:
        received = lax.all_to_all(by_owner, "rows", 0, 0, tiled=True)
        stores = to_parts(received.reshape(rows * held, -1))
        every = lax.all_gather(query, "rows", axis=0, tiled=True)
        sides = []
        for basis, eigen, gathered, begin in zip(bases, eigens, (every[:, :depth], every[:, depth:]), (0, share)):
            rotated = jnp.einsum("eh,qh->eq", basis, gathered, preferred_element_type=jnp.float32)
            scaled = (rotated * (1.0 / (eigen[0] + damping))[:, None]).astype(jnp.bfloat16)
            sides.append(
                [
                    jnp.dot(one[:, begin : begin + basis.shape[0]], scaled, preferred_element_type=jnp.float32)
                    for one in stores
                ]
            )
        partial = jnp.array(sides).reshape(2, parts, rows, examples, RANK, layers, rows // layers * columns)
        partial = partial.transpose(1, 2, 5, 0, 4, 3, 6).reshape(parts, rows, layers, 2 * RANK, -1)
        fill = packed_width(examples, rows // layers * columns) - partial.shape[-1]
        partial = jnp.pad(partial.astype(jnp.bfloat16), [(0, 0)] * 4 + [(0, fill)])
        partial = jnp.stack([lax.dynamic_index_in_dim(partial, (part - j) % parts, 0, False) for j in range(parts)])

    received = lax.all_to_all(
        partial.reshape((parts * rows * layers,) + partial.shape[3:]), ("parts", "rows", "layer"), 0, 0, tiled=True
    )
    gram = received.astype(jnp.float32).reshape(parts, rows, layers, 2, RANK, -1).sum(axis=1)
    by_column = (gram[:, :, 0] * gram[:, :, 1]).sum(axis=(1, 2))[:, : examples * width * RANK // parts]
    by_column = by_column.reshape(parts, examples, rows // layers, columns).transpose(1, 2, 0, 3)
    return by_column.reshape(examples, width, RANK).sum(axis=2)


def solution(mesh):
    placed = (
        P("layer", "rows", None),
        P("layer", "rows", None),
        P("layer", ("parts", "rows"), None),
        P("layer", ("parts", "rows"), None),
        P("layer", "rows", None),
        P("layer", "rows", None),
        P("layer", "rows"),
        P("layer", "rows"),
    )
    return jax.shard_map(
        per_device,
        mesh=mesh,
        in_specs=placed,
        out_specs=P(("parts", "rows"), "layer"),
        check_vma=False,
    )
```

```python
import typing

import jax
import jax.numpy as jnp
from jax import lax
from jax.experimental import pallas as pl
from jax.experimental.pallas import tpu as pltpu
from jax.sharding import PartitionSpec as P

RANK = 8


damping = 0.1

MIB = 1024 * 1024
TILE = 256


def along(value, by):
    size = lax.axis_size("rows")
    return lax.ppermute(value, "rows", [(i, i + by) for i in range(size) if 0 <= i + by < size])


def rotate(bases, eigens, queries, begins):
    groups = [query if isinstance(query, tuple) else (query,) for query in queries]
    queries = [query for group in groups for query in group]
    columns = queries[0].shape[0]
    held = columns * len(groups)
    sides = len(bases)

    def kernel(*refs):
        basis_refs, eigen_refs = refs[:sides], refs[sides : 2 * sides]
        query_refs = list(refs[2 * sides : 2 * sides + len(queries)])
        out_refs, query = refs[2 * sides + len(queries) : -1], refs[-1]
        for place, group in enumerate(groups):
            block = query_refs.pop(0)[...]
            for _ in group[1:]:
                block = block + query_refs.pop(0)[...]
            query[place * columns : (place + 1) * columns, :] = block
        for basis_ref, eigen_ref, out_ref, begin in zip(basis_refs, eigen_refs, out_refs, begins):
            share, width = basis_ref.shape
            for tile in range(share // TILE):
                where = slice(tile * TILE, (tile + 1) * TILE)
                rotated = lax.dot_general(
                    basis_ref[where, :],
                    query[:, begin : begin + width],
                    (((1,), (1,)), ((), ())),
                    preferred_element_type=jnp.float32,
                )
                out_ref[where, :] = (rotated * (1.0 / (eigen_ref[where, :] + damping))).astype(jnp.bfloat16)

    return pl.pallas_call(
        kernel,
        out_shape=[jax.ShapeDtypeStruct((basis.shape[0], held), jnp.bfloat16) for basis in bases],
        scratch_shapes=[pltpu.VMEM((held, queries[0].shape[1]), jnp.bfloat16)],
        compiler_params=pltpu.CompilerParams(vmem_limit_bytes=8 * MIB),
        cost_estimate=pl.CostEstimate(flops=1, bytes_accessed=1, transcendentals=0),
    )(*[pltpu.with_memory_space_constraint(one, pltpu.VMEM) for one in (*bases, *eigens, *queries)])


def packed_width(examples, columns):
    return -(-examples * columns // 128) * 128


class Store(typing.NamedTuple):
    rows: jax.Array
    shift: int
    flips: tuple


def grams(stores, near, two, three):
    parts = lax.axis_size("parts")
    shares = [side.shape[0] for side in near]
    columns = two[0].shape[1]
    held = stores[0].rows.shape[0] // len(stores[0].flips)
    examples = held // RANK
    width = packed_width(examples, columns)
    fill = width - examples * columns

    def kernel(*refs):
        store_refs, block_refs, out_ref = refs[: len(stores)], refs[len(stores) : -1], refs[-1]
        row, part = lax.axis_index("rows"), lax.axis_index("parts")

        def packed(gram, block, place):
            pieces = [
                gram[
                    block * held + i * RANK : block * held + (i + 1) * RANK, place * columns : (place + 1) * columns
                ]
                for i in range(examples)
            ]
            if fill:
                pieces.append(jnp.zeros((RANK, fill), jnp.float32))
            return jnp.concatenate(pieces, axis=1)

        def write(sides, shards):
            for store, store_ref in zip(stores, store_refs):
                both = [
                    jnp.dot(store_ref[:, begin : begin + share], side[...], preferred_element_type=jnp.float32)
                    for side, begin, share in zip(sides, (0, shares[0]), shares)
                ]
                owner_part = lax.rem(part + parts - store.shift, parts)
                for block, flip in enumerate(store.flips):
                    for place, shard in enumerate(shards):
                        out_ref[owner_part, lax.bitwise_xor(row, flip), shard] = jnp.concatenate(
                            [packed(gram, block, place) for gram in both], axis=0
                        ).astype(jnp.bfloat16)

        write(block_refs[0:2], [row, lax.rem(row + 1, 4), lax.rem(row + 3, 4)])
        write(block_refs[2:4], [lax.rem(row + 2, 4)])

        @pl.when(jnp.logical_or(row == 0, row == 3))
        def _():
            write(block_refs[4:6], [jnp.where(row == 0, 3, 0)])

    return pl.pallas_call(
        kernel,
        out_shape=jax.ShapeDtypeStruct((parts, 4, 4, 2 * RANK, width), jnp.bfloat16),
        compiler_params=pltpu.CompilerParams(vmem_limit_bytes=6 * MIB),
        cost_estimate=pl.CostEstimate(flops=1, bytes_accessed=1, transcendentals=0),
    )(*[store.rows for store in stores], *near, *two, *three)


def along_four(query, bases, eigens, by_owner):
    row = lax.axis_index("rows")
    depth = bases[0].shape[1]
    eigens = [eigen.reshape(-1, 1) for eigen in eigens]
    after = lax.ppermute(query, "rows", [(1, 0), (2, 1), (3, 2)])
    before = lax.ppermute(query, "rows", [(0, 1), (1, 2), (2, 3)])
    sent = [lax.dynamic_index_in_dim(by_owner, lax.bitwise_xor(row, flip), 0, False) for flip in range(4)]
    query, sent = lax.optimization_barrier((query, sent))
    early = [sent[0], flipped(sent[1], 1)]
    query, after, before = lax.optimization_barrier((query, after, before))
    after_two = lax.ppermute(after, "rows", [(1, 0), (2, 1)])
    before_two = lax.ppermute(before, "rows", [(1, 2), (2, 3)])
    near = rotate(bases, eigens, [query, after, before], (0, depth))
    near, early = lax.optimization_barrier((near, early))
    stores = to_parts(jnp.concatenate(early, axis=0), (0, 1))
    near, after_two, before_two, sent = lax.optimization_barrier((near, after_two, before_two, sent))
    two_hidden, two_model = (
        jnp.where(row < 2, after_two[:, side], before_two[:, side]) for side in (slice(0, depth), slice(depth, None))
    )
    ends = [(1, 0), (2, 3)]
    three_hidden = lax.ppermute(two_hidden, "rows", ends)
    late = [flipped(sent[flip], flip) for flip in (2, 3)]
    far = rotate(bases, eigens, [(after_two, before_two)], (0, depth))
    far, three_hidden, two_model, late = lax.optimization_barrier((far, three_hidden, two_model, late))
    three_model = lax.ppermute(two_model, "rows", ends)
    last_hidden = rotate(bases[:1], eigens[:1], [three_hidden], (0,))
    stores += to_parts(jnp.concatenate(late, axis=0), (2, 3))
    last_hidden, three_model = lax.optimization_barrier((last_hidden, three_model))
    last_model = rotate(bases[1:], eigens[1:], [three_model], (0,))
    return grams(stores, near, far, last_hidden + last_model)


def flipped(block, flip):
    return lax.ppermute(block, "rows", [(i, i ^ flip) for i in range(4)])


def to_parts(rows, flips):
    parts = lax.axis_size("parts")
    return [Store(rows, 0, flips)] + [
        Store(lax.ppermute(rows, "parts", [(i, (i + j) % parts) for i in range(parts)]), j, flips)
        for j in range(1, parts)
    ]


def per_device(
    query_hidden,
    query_model,
    train_hidden,
    train_model,
    hidden_basis,
    model_basis,
    hidden_eigen,
    model_eigen,
):
    rows = lax.axis_size("rows")
    parts = lax.axis_size("parts")
    layers = lax.axis_size("layer")
    part = lax.axis_index("parts")
    held = train_hidden.shape[1]
    examples = held // RANK
    columns = query_hidden.shape[1] // parts
    width = query_hidden.shape[1] * rows // RANK // layers
    bases = [hidden_basis[0], model_basis[0]]
    eigens = [hidden_eigen, model_eigen]
    share = bases[0].shape[0]
    depth = bases[0].shape[1]

    query = jnp.concatenate(
        [lax.dynamic_slice_in_dim(side[0], part * columns, columns, 0) for side in (query_hidden, query_model)],
        axis=1,
    )
    by_owner = jnp.concatenate(
        [side[0].reshape(held, rows, -1).transpose(1, 0, 2) for side in (train_hidden, train_model)], axis=2
    )
    if rows == 4:
        partial = along_four(query, bases, eigens, by_owner)
    else:
        received = lax.all_to_all(by_owner, "rows", 0, 0, tiled=True)
        stores = [store.rows for store in to_parts(received.reshape(rows * held, -1), ())]
        every = lax.all_gather(query, "rows", axis=0, tiled=True)
        sides = []
        for basis, eigen, gathered, begin in zip(bases, eigens, (every[:, :depth], every[:, depth:]), (0, share)):
            rotated = jnp.einsum("eh,qh->eq", basis, gathered, preferred_element_type=jnp.float32)
            scaled = (rotated * (1.0 / (eigen[0] + damping))[:, None]).astype(jnp.bfloat16)
            sides.append(
                [
                    jnp.dot(one[:, begin : begin + basis.shape[0]], scaled, preferred_element_type=jnp.float32)
                    for one in stores
                ]
            )
        partial = jnp.array(sides).reshape(2, parts, rows, examples, RANK, layers, rows // layers * columns)
        partial = partial.transpose(1, 2, 5, 0, 4, 3, 6).reshape(parts, rows, layers, 2 * RANK, -1)
        fill = packed_width(examples, rows // layers * columns) - partial.shape[-1]
        partial = jnp.pad(partial.astype(jnp.bfloat16), [(0, 0)] * 4 + [(0, fill)])
        partial = jnp.stack([lax.dynamic_index_in_dim(partial, (part - j) % parts, 0, False) for j in range(parts)])

    received = lax.all_to_all(
        partial.reshape((parts * rows * layers,) + partial.shape[3:]), ("parts", "rows", "layer"), 0, 0, tiled=True
    )
    gram = received.astype(jnp.float32).reshape(parts, rows, layers, 2, RANK, -1).sum(axis=1)
    by_column = (gram[:, :, 0] * gram[:, :, 1]).sum(axis=(1, 2))[:, : examples * width * RANK // parts]
    by_column = by_column.reshape(parts, examples, rows // layers, columns).transpose(1, 2, 0, 3)
    return by_column.reshape(examples, width, RANK).sum(axis=2)


def solution(mesh):
    placed = (
        P("layer", "rows", None),
        P("layer", "rows", None),
        P("layer", ("parts", "rows"), None),
        P("layer", ("parts", "rows"), None),
        P("layer", "rows", None),
        P("layer", "rows", None),
        P("layer", "rows"),
        P("layer", "rows"),
    )
    return jax.shard_map(
        per_device,
        mesh=mesh,
        in_specs=placed,
        out_specs=P(("parts", "rows"), "layer"),
        check_vma=False,
    )
```

```python
import jax
import jax.numpy as jnp
from jax import lax
from jax.experimental import pallas as pl
from jax.experimental.pallas import tpu as pltpu
from jax.sharding import PartitionSpec as P

RANK = 8


damping = 0.1

MIB = 1024 * 1024
TILE = 256


def along(value, by):
    size = lax.axis_size("rows")
    return lax.ppermute(value, "rows", [(i, i + by) for i in range(size) if 0 <= i + by < size])


def rotate(bases, eigens, queries, begins):
    groups = [query if isinstance(query, tuple) else (query,) for query in queries]
    queries = [query for group in groups for query in group]
    columns = queries[0].shape[0]
    held = columns * len(groups)
    sides = len(bases)

    def kernel(*refs):
        basis_refs, eigen_refs = refs[:sides], refs[sides : 2 * sides]
        query_refs = list(refs[2 * sides : 2 * sides + len(queries)])
        out_refs, query = refs[2 * sides + len(queries) : -1], refs[-1]
        for place, group in enumerate(groups):
            block = query_refs.pop(0)[...]
            for _ in group[1:]:
                block = block + query_refs.pop(0)[...]
            query[place * columns : (place + 1) * columns, :] = block
        for basis_ref, eigen_ref, out_ref, begin in zip(basis_refs, eigen_refs, out_refs, begins):
            share, width = basis_ref.shape
            for tile in range(share // TILE):
                where = slice(tile * TILE, (tile + 1) * TILE)
                rotated = lax.dot_general(
                    basis_ref[where, :],
                    query[:, begin : begin + width],
                    (((1,), (1,)), ((), ())),
                    preferred_element_type=jnp.float32,
                )
                out_ref[where, :] = (rotated * (1.0 / (eigen_ref[where, :] + damping))).astype(jnp.bfloat16)

    return pl.pallas_call(
        kernel,
        out_shape=[jax.ShapeDtypeStruct((basis.shape[0], held), jnp.bfloat16) for basis in bases],
        scratch_shapes=[pltpu.VMEM((held, queries[0].shape[1]), jnp.bfloat16)],
        compiler_params=pltpu.CompilerParams(vmem_limit_bytes=8 * MIB),
        cost_estimate=pl.CostEstimate(flops=1, bytes_accessed=1, transcendentals=0),
    )(*[pltpu.with_memory_space_constraint(one, pltpu.VMEM) for one in (*bases, *eigens, *queries)])


def packed_width(examples, columns):
    return -(-examples * columns // 128) * 128


def grams(stores, blocks, offsets, base=None):
    rows, parts = lax.axis_size("rows"), lax.axis_size("parts")
    shares = [side.shape[0] for side in blocks[0]]
    columns = blocks[0][0].shape[1] // len(offsets[0])
    count = len(stores)
    held = stores[0].shape[0] // rows
    examples = held // RANK
    width = packed_width(examples, columns)

    def kernel(*refs):
        store_refs, block_refs, out_ref = refs[:count], refs[count : count + 2 * len(blocks)], refs[-1]
        row, part = lax.axis_index("rows"), lax.axis_index("parts")
        if base is not None:
            base_ref = refs[-2]
            out_ref[...] = base_ref[...]

        def write():
            for at, block_offsets in enumerate(offsets):
                for j, store_ref in enumerate(store_refs):
                    sides = []
                    for side, begin in enumerate((0, shares[0])):
                        store = store_ref[:, begin : begin + shares[side]]
                        sides.append(
                            jnp.dot(store, block_refs[2 * at + side][...], preferred_element_type=jnp.float32)
                        )
                    owner_part = lax.rem(part + parts - j, parts)
                    for place, offset in enumerate(block_offsets):
                        shard = lax.rem(row + offset, rows) if base is None else jnp.where(row == 0, rows - 1, 0)
                        for owner in range(rows):
                            packed = []
                            for gram in sides:
                                pieces = [
                                    gram[
                                        owner * held + i * RANK : owner * held + (i + 1) * RANK,
                                        place * columns : (place + 1) * columns,
                                    ]
                                    for i in range(examples)
                                ]
                                fill = width - examples * columns
                                if fill:
                                    pieces.append(jnp.zeros((RANK, fill), jnp.float32))
                                packed.append(jnp.concatenate(pieces, axis=1))
                            out_ref[owner_part, lax.rem(row + rows - owner, rows), shard] = jnp.concatenate(packed, axis=0).astype(jnp.bfloat16)

        if base is None:
            write()
        else:
            pl.when(jnp.logical_or(row == 0, row == rows - 1))(write)

    operands = [*stores, *[side for block in blocks for side in block]]
    return pl.pallas_call(
        kernel,
        out_shape=jax.ShapeDtypeStruct((parts, rows, rows, 2 * RANK, width), jnp.bfloat16),
        compiler_params=pltpu.CompilerParams(vmem_limit_bytes=6 * MIB),
        cost_estimate=pl.CostEstimate(flops=1, bytes_accessed=1, transcendentals=0),
    )(*operands, *([] if base is None else [base]))


def along_four(query, bases, eigens, train):
    row = lax.axis_index("rows")
    depth = bases[0].shape[1]
    eigens = [eigen.reshape(-1, 1) for eigen in eigens]
    after = lax.ppermute(query, "rows", [(1, 0), (2, 1), (3, 2)])
    before = lax.ppermute(query, "rows", [(0, 1), (1, 2), (2, 3)])
    train, after, before = lax.optimization_barrier((train, after, before))
    after_two = lax.ppermute(after, "rows", [(1, 0), (2, 1)])
    before_two = lax.ppermute(before, "rows", [(1, 2), (2, 3)])
    by_owner = cut_by_owner(*train)
    blocks = to_owners([lax.dynamic_index_in_dim(by_owner, (row + k) % 4, 0, False) for k in range(4)])
    two_hidden, two_model = (
        jnp.where(row < 2, after_two[:, side], before_two[:, side]) for side in (slice(0, depth), slice(depth, None))
    )
    ends = [(1, 0), (2, 3)]
    three_hidden = lax.ppermute(two_hidden, "rows", ends)
    _, blocks = lax.optimization_barrier((two_hidden, blocks))
    stores = to_parts(jnp.concatenate(blocks, axis=0))
    far = rotate(bases, eigens, [query, after, before, (after_two, before_two)], (0, depth))
    far, three_hidden, two_model = lax.optimization_barrier((far, three_hidden, two_model))
    base = grams(stores, [far], [(0, 1, 3, 2)])
    three_model = lax.ppermute(two_model, "rows", ends)
    last_hidden = rotate(bases[:1], eigens[:1], [three_hidden], (0,))
    base, last_hidden, three_model = lax.optimization_barrier((base, last_hidden, three_model))
    last_model = rotate(bases[1:], eigens[1:], [three_model], (0,))
    return grams(stores, [last_hidden + last_model], [(3,)], base)


def cut_by_owner(train_hidden, train_model):
    rows = lax.axis_size("rows")
    held = train_hidden.shape[0]
    return jnp.concatenate(
        [side.reshape(held, rows, -1).transpose(1, 0, 2) for side in (train_hidden, train_model)], axis=2
    )


def to_owners(sent):
    rows = lax.axis_size("rows")
    return sent[:1] + [
        lax.ppermute(sent[k], "rows", [(i, (i + k) % rows) for i in range(rows)]) for k in range(1, rows)
    ]


def to_parts(store):
    parts = lax.axis_size("parts")
    return [store] + [
        lax.ppermute(store, "parts", [(i, (i + j) % parts) for i in range(parts)]) for j in range(1, parts)
    ]


def per_device(
    query_hidden,
    query_model,
    train_hidden,
    train_model,
    hidden_basis,
    model_basis,
    hidden_eigen,
    model_eigen,
):
    rows = lax.axis_size("rows")
    parts = lax.axis_size("parts")
    layers = lax.axis_size("layer")
    part = lax.axis_index("parts")
    held = train_hidden.shape[1]
    examples = held // RANK
    columns = query_hidden.shape[1] // parts
    width = query_hidden.shape[1] * rows // RANK // layers
    bases = [hidden_basis[0], model_basis[0]]
    eigens = [hidden_eigen, model_eigen]
    share = bases[0].shape[0]
    depth = bases[0].shape[1]

    query = jnp.concatenate(
        [lax.dynamic_slice_in_dim(side[0], part * columns, columns, 0) for side in (query_hidden, query_model)],
        axis=1,
    )
    if rows == 4:
        partial = along_four(query, bases, eigens, (train_hidden[0], train_model[0]))
    else:
        by_owner = cut_by_owner(train_hidden[0], train_model[0])
        received = lax.all_to_all(by_owner, "rows", 0, 0, tiled=True)
        stores = to_parts(received.reshape(rows * held, -1))
        every = lax.all_gather(query, "rows", axis=0, tiled=True)
        sides = []
        for basis, eigen, gathered, begin in zip(bases, eigens, (every[:, :depth], every[:, depth:]), (0, share)):
            rotated = jnp.einsum("eh,qh->eq", basis, gathered, preferred_element_type=jnp.float32)
            scaled = (rotated * (1.0 / (eigen[0] + damping))[:, None]).astype(jnp.bfloat16)
            sides.append(
                [
                    jnp.dot(one[:, begin : begin + basis.shape[0]], scaled, preferred_element_type=jnp.float32)
                    for one in stores
                ]
            )
        partial = jnp.array(sides).reshape(2, parts, rows, examples, RANK, layers, rows // layers * columns)
        partial = partial.transpose(1, 2, 5, 0, 4, 3, 6).reshape(parts, rows, layers, 2 * RANK, -1)
        fill = packed_width(examples, rows // layers * columns) - partial.shape[-1]
        partial = jnp.pad(partial.astype(jnp.bfloat16), [(0, 0)] * 4 + [(0, fill)])
        partial = jnp.stack([lax.dynamic_index_in_dim(partial, (part - j) % parts, 0, False) for j in range(parts)])

    received = lax.all_to_all(
        partial.reshape((parts * rows * layers,) + partial.shape[3:]), ("parts", "rows", "layer"), 0, 0, tiled=True
    )
    gram = received.astype(jnp.float32).reshape(parts, rows, layers, 2, RANK, -1).sum(axis=1)
    by_column = (gram[:, :, 0] * gram[:, :, 1]).sum(axis=(1, 2))[:, : examples * width * RANK // parts]
    by_column = by_column.reshape(parts, examples, rows // layers, columns).transpose(1, 2, 0, 3)
    return by_column.reshape(examples, width, RANK).sum(axis=2)


def solution(mesh):
    placed = (
        P("layer", "rows", None),
        P("layer", "rows", None),
        P("layer", ("parts", "rows"), None),
        P("layer", ("parts", "rows"), None),
        P("layer", "rows", None),
        P("layer", "rows", None),
        P("layer", "rows"),
        P("layer", "rows"),
    )
    return jax.shard_map(
        per_device,
        mesh=mesh,
        in_specs=placed,
        out_specs=P(("parts", "rows"), "layer"),
        check_vma=False,
    )
```

```python
import jax
import jax.numpy as jnp
from jax import lax
from jax.experimental import pallas as pl
from jax.experimental.pallas import tpu as pltpu
from jax.sharding import PartitionSpec as P

RANK = 8


damping = 0.1

MIB = 1024 * 1024
TILE = 256
AHEAD = 3


def along(value, by):
    size = lax.axis_size("rows")
    return lax.ppermute(value, "rows", [(i, i + by) for i in range(size) if 0 <= i + by < size])


def rotate(bases, eigens, queries, begins, load=False):
    groups = [query if isinstance(query, tuple) else (query,) for query in queries]
    queries = [query for group in groups for query in group]
    columns = queries[0].shape[0]
    held = columns * len(groups)
    sides = len(bases)

    def kernel(*refs):
        basis_refs, eigen_refs = refs[:sides], refs[sides : 2 * sides]
        query_refs = list(refs[2 * sides : 2 * sides + len(queries)])
        out_refs, rest = refs[2 * sides + len(queries) :][:sides], refs[3 * sides + len(queries) :]
        copies = []
        if load:
            loaded, query, semaphores = rest
            for tile in range(loaded.shape[0] // TILE):
                where = slice(tile * TILE, (tile + 1) * TILE)
                copies.append(pltpu.make_async_copy(basis_refs[0].at[where], loaded.at[where], semaphores.at[tile]))
            for copy in copies[:AHEAD]:
                copy.start()
            basis_refs = [loaded, *basis_refs[1:]]
        else:
            (query,) = rest
        for place, group in enumerate(groups):
            block = query_refs.pop(0)[...]
            for _ in group[1:]:
                block = block + query_refs.pop(0)[...]
            query[place * columns : (place + 1) * columns, :] = block
        for side in reversed(range(sides)):
            basis_ref, eigen_ref, out_ref, begin = basis_refs[side], eigen_refs[side], out_refs[side], begins[side]
            share, width = basis_ref.shape
            for tile in range(share // TILE):
                where = slice(tile * TILE, (tile + 1) * TILE)
                if load and side == 0:
                    copies[tile].wait()
                    if tile + AHEAD < len(copies):
                        copies[tile + AHEAD].start()
                rotated = lax.dot_general(
                    basis_ref[where, :],
                    query[:, begin : begin + width],
                    (((1,), (1,)), ((), ())),
                    preferred_element_type=jnp.float32,
                )
                out_ref[where, :] = (rotated * (1.0 / (eigen_ref[where, :] + damping))).astype(jnp.bfloat16)

    spaces = [pltpu.HBM if load and side == 0 else pltpu.VMEM for side in range(sides)]
    spaces += [pltpu.VMEM] * (sides + len(queries))
    constrained = [
        pltpu.with_memory_space_constraint(one, space) for one, space in zip((*bases, *eigens, *queries), spaces)
    ]
    return pl.pallas_call(
        kernel,
        in_specs=[pl.BlockSpec(memory_space=space) for space in spaces],
        out_specs=[pl.BlockSpec(memory_space=pltpu.VMEM)] * (sides + load),
        out_shape=[jax.ShapeDtypeStruct((basis.shape[0], held), jnp.bfloat16) for basis in bases]
        + ([pltpu.VMEM(bases[0].shape, bases[0].dtype)] if load else []),
        scratch_shapes=[pltpu.VMEM((held, queries[0].shape[1]), jnp.bfloat16)]
        + ([pltpu.SemaphoreType.DMA((bases[0].shape[0] // TILE,))] if load else []),
        compiler_params=pltpu.CompilerParams(vmem_limit_bytes=8 * MIB),
        cost_estimate=pl.CostEstimate(flops=1, bytes_accessed=1, transcendentals=0),
    )(*constrained)


def own_rows(query_hidden, query_model, columns):
    if columns % 16:
        start = lax.axis_index("parts") * columns
        return jnp.concatenate(
            [lax.dynamic_slice_in_dim(side, start, columns, 0) for side in (query_hidden, query_model)], axis=1
        )
    depth = query_hidden.shape[1]

    def kernel(hidden_ref, model_ref, out_ref, semaphores):
        rows = pl.ds(pl.multiple_of(lax.axis_index("parts") * columns, columns), columns)
        copies = [
            pltpu.make_async_copy(hidden_ref.at[rows], out_ref.at[:, :depth], semaphores.at[0]),
            pltpu.make_async_copy(model_ref.at[rows], out_ref.at[:, depth:], semaphores.at[1]),
        ]
        for copy in copies:
            copy.start()
        for copy in copies:
            copy.wait()

    return pl.pallas_call(
        kernel,
        in_specs=[pl.BlockSpec(memory_space=pltpu.HBM)] * 2,
        out_specs=pl.BlockSpec(memory_space=pltpu.VMEM),
        out_shape=pltpu.VMEM((columns, depth + query_model.shape[1]), query_hidden.dtype),
        scratch_shapes=[pltpu.SemaphoreType.DMA((2,))],
        compiler_params=pltpu.CompilerParams(vmem_limit_bytes=2 * MIB),
        cost_estimate=pl.CostEstimate(flops=1, bytes_accessed=1, transcendentals=0),
    )(*[pltpu.with_memory_space_constraint(side, pltpu.HBM) for side in (query_hidden, query_model)])


def packed_width(examples, columns):
    return -(-examples * columns // 128) * 128


def grams(stores, blocks, offsets, base=None):
    rows, parts = lax.axis_size("rows"), lax.axis_size("parts")
    shares = [side.shape[0] for side in blocks[0]]
    columns = blocks[0][0].shape[1] // len(offsets[0])
    count = len(stores)
    held = stores[0].shape[0] // rows
    examples = held // RANK
    width = packed_width(examples, columns)

    def kernel(*refs):
        store_refs, block_refs, out_ref = refs[:count], refs[count : count + 2 * len(blocks)], refs[-1]
        row, part = lax.axis_index("rows"), lax.axis_index("parts")
        if base is not None:
            base_ref = refs[-2]
            out_ref[...] = base_ref[...]

        def write():
            for at, block_offsets in enumerate(offsets):
                for j, store_ref in enumerate(store_refs):
                    sides = []
                    for side, begin in enumerate((0, shares[0])):
                        store = store_ref[:, begin : begin + shares[side]]
                        sides.append(
                            jnp.dot(store, block_refs[2 * at + side][...], preferred_element_type=jnp.float32)
                        )
                    owner_part = lax.rem(part + parts - j, parts)
                    for place, offset in enumerate(block_offsets):
                        shard = lax.rem(row + offset, rows) if base is None else jnp.where(row == 0, rows - 1, 0)
                        for owner in range(rows):
                            packed = []
                            for gram in sides:
                                pieces = [
                                    gram[
                                        owner * held + i * RANK : owner * held + (i + 1) * RANK,
                                        place * columns : (place + 1) * columns,
                                    ]
                                    for i in range(examples)
                                ]
                                fill = width - examples * columns
                                if fill:
                                    pieces.append(jnp.zeros((RANK, fill), jnp.float32))
                                packed.append(jnp.concatenate(pieces, axis=1))
                            out_ref[owner_part, lax.rem(row + rows - owner, rows), shard] = jnp.concatenate(packed, axis=0).astype(jnp.bfloat16)

        if base is None:
            write()
        else:
            pl.when(jnp.logical_or(row == 0, row == rows - 1))(write)

    operands = [*stores, *[side for block in blocks for side in block]]
    return pl.pallas_call(
        kernel,
        out_shape=jax.ShapeDtypeStruct((parts, rows, rows, 2 * RANK, width), jnp.bfloat16),
        compiler_params=pltpu.CompilerParams(vmem_limit_bytes=6 * MIB),
        cost_estimate=pl.CostEstimate(flops=1, bytes_accessed=1, transcendentals=0),
    )(*operands, *([] if base is None else [base]))


def along_four(query, bases, eigens, by_owner):
    row = lax.axis_index("rows")
    depth = bases[0].shape[1]
    eigens = [eigen.reshape(-1, 1) for eigen in eigens]
    after = lax.ppermute(query, "rows", [(1, 0), (2, 1), (3, 2)])
    before = lax.ppermute(query, "rows", [(0, 1), (1, 2), (2, 3)])
    sent = [lax.dynamic_index_in_dim(by_owner, (row + k) % 4, 0, False) for k in range(4)]
    query, sent = lax.optimization_barrier((query, sent))
    blocks = to_owners(sent)
    query, after, before = lax.optimization_barrier((query, after, before))
    after_two = lax.ppermute(after, "rows", [(1, 0), (2, 1)])
    before_two = lax.ppermute(before, "rows", [(1, 2), (2, 3)])
    *near, hidden_here = rotate(bases, eigens, [query, after, before], (0, depth), load=True)
    bases = [hidden_here, bases[1]]
    near, blocks = lax.optimization_barrier((near, blocks))
    stores = to_parts(jnp.concatenate(blocks, axis=0))
    near, after_two, before_two = lax.optimization_barrier((near, after_two, before_two))
    two_hidden, two_model = (
        jnp.where(row < 2, after_two[:, side], before_two[:, side]) for side in (slice(0, depth), slice(depth, None))
    )
    ends = [(1, 0), (2, 3)]
    three_hidden = lax.ppermute(two_hidden, "rows", ends)
    far = rotate(bases, eigens, [(after_two, before_two)], (0, depth))
    far, three_hidden, two_model = lax.optimization_barrier((far, three_hidden, two_model))
    base = grams(stores, [near, far], [(0, 1, 3), (2,)])
    three_model = lax.ppermute(two_model, "rows", ends)
    last_hidden = rotate(bases[:1], eigens[:1], [three_hidden], (0,))
    base, last_hidden, three_model = lax.optimization_barrier((base, last_hidden, three_model))
    last_model = rotate(bases[1:], eigens[1:], [three_model], (0,))
    return grams(stores, [last_hidden + last_model], [(3,)], base)


def to_owners(sent):
    rows = lax.axis_size("rows")
    return sent[:1] + [
        lax.ppermute(sent[k], "rows", [(i, (i + k) % rows) for i in range(rows)]) for k in range(1, rows)
    ]


def to_parts(store):
    parts = lax.axis_size("parts")
    return [store] + [
        lax.ppermute(store, "parts", [(i, (i + j) % parts) for i in range(parts)]) for j in range(1, parts)
    ]


def per_device(
    query_hidden,
    query_model,
    train_hidden,
    train_model,
    hidden_basis,
    model_basis,
    hidden_eigen,
    model_eigen,
):
    rows = lax.axis_size("rows")
    parts = lax.axis_size("parts")
    layers = lax.axis_size("layer")
    part = lax.axis_index("parts")
    held = train_hidden.shape[1]
    examples = held // RANK
    columns = query_hidden.shape[1] // parts
    width = query_hidden.shape[1] * rows // RANK // layers
    bases = [hidden_basis[0], model_basis[0]]
    eigens = [hidden_eigen, model_eigen]
    share = bases[0].shape[0]
    depth = bases[0].shape[1]

    query = own_rows(query_hidden[0], query_model[0], columns)
    by_owner = jnp.concatenate(
        [side[0].reshape(held, rows, -1).transpose(1, 0, 2) for side in (train_hidden, train_model)], axis=2
    )
    if rows == 4:
        partial = along_four(query, bases, eigens, by_owner)
    else:
        received = lax.all_to_all(by_owner, "rows", 0, 0, tiled=True)
        stores = to_parts(received.reshape(rows * held, -1))
        every = lax.all_gather(query, "rows", axis=0, tiled=True)
        sides = []
        for basis, eigen, gathered, begin in zip(bases, eigens, (every[:, :depth], every[:, depth:]), (0, share)):
            rotated = jnp.einsum("eh,qh->eq", basis, gathered, preferred_element_type=jnp.float32)
            scaled = (rotated * (1.0 / (eigen[0] + damping))[:, None]).astype(jnp.bfloat16)
            sides.append(
                [
                    jnp.dot(one[:, begin : begin + basis.shape[0]], scaled, preferred_element_type=jnp.float32)
                    for one in stores
                ]
            )
        partial = jnp.array(sides).reshape(2, parts, rows, examples, RANK, layers, rows // layers * columns)
        partial = partial.transpose(1, 2, 5, 0, 4, 3, 6).reshape(parts, rows, layers, 2 * RANK, -1)
        fill = packed_width(examples, rows // layers * columns) - partial.shape[-1]
        partial = jnp.pad(partial.astype(jnp.bfloat16), [(0, 0)] * 4 + [(0, fill)])
        partial = jnp.stack([lax.dynamic_index_in_dim(partial, (part - j) % parts, 0, False) for j in range(parts)])

    received = lax.all_to_all(
        partial.reshape((parts * rows * layers,) + partial.shape[3:]), ("parts", "rows", "layer"), 0, 0, tiled=True
    )
    gram = received.astype(jnp.float32).reshape(parts, rows, layers, 2, RANK, -1).sum(axis=1)
    by_column = (gram[:, :, 0] * gram[:, :, 1]).sum(axis=(1, 2))[:, : examples * width * RANK // parts]
    by_column = by_column.reshape(parts, examples, rows // layers, columns).transpose(1, 2, 0, 3)
    return by_column.reshape(examples, width, RANK).sum(axis=2)


def solution(mesh):
    placed = (
        P("layer", "rows", None),
        P("layer", "rows", None),
        P("layer", ("parts", "rows"), None),
        P("layer", ("parts", "rows"), None),
        P("layer", "rows", None),
        P("layer", "rows", None),
        P("layer", "rows"),
        P("layer", "rows"),
    )
    return jax.shard_map(
        per_device,
        mesh=mesh,
        in_specs=placed,
        out_specs=P(("parts", "rows"), "layer"),
        check_vma=False,
    )
```

```python
import jax
import jax.numpy as jnp
from jax import lax
from jax.experimental import pallas as pl
from jax.experimental.pallas import tpu as pltpu
from jax.sharding import PartitionSpec as P

RANK = 8


damping = 0.1

MIB = 1024 * 1024
TILE = 256
AHEAD = 3


def rotate(bases, eigens, queries, begins, load=False):
    groups = [query if isinstance(query, tuple) else (query,) for query in queries]
    queries = [query for group in groups for query in group]
    columns = queries[0].shape[0]
    held = columns * len(groups)
    sides = len(bases)

    def kernel(*refs):
        basis_refs, eigen_refs = refs[:sides], refs[sides : 2 * sides]
        query_refs = list(refs[2 * sides : 2 * sides + len(queries)])
        out_refs, rest = refs[2 * sides + len(queries) :][:sides], refs[3 * sides + len(queries) :]
        copies = []
        if load:
            loaded, query, semaphores = rest
            for tile in range(loaded.shape[0] // TILE):
                where = slice(tile * TILE, (tile + 1) * TILE)
                copies.append(pltpu.make_async_copy(basis_refs[0].at[where], loaded.at[where], semaphores.at[tile]))
            for copy in copies[:AHEAD]:
                copy.start()
            basis_refs = [loaded, *basis_refs[1:]]
        else:
            (query,) = rest
        for place, group in enumerate(groups):
            block = query_refs.pop(0)[...]
            for _ in group[1:]:
                block = block + query_refs.pop(0)[...]
            query[place * columns : (place + 1) * columns, :] = block
        for side in reversed(range(sides)):
            basis_ref, eigen_ref, out_ref, begin = basis_refs[side], eigen_refs[side], out_refs[side], begins[side]
            share, width = basis_ref.shape
            for tile in range(share // TILE):
                where = slice(tile * TILE, (tile + 1) * TILE)
                if load and side == 0:
                    copies[tile].wait()
                    if tile + AHEAD < len(copies):
                        copies[tile + AHEAD].start()
                rotated = lax.dot_general(
                    basis_ref[where, :],
                    query[:, begin : begin + width],
                    (((1,), (1,)), ((), ())),
                    preferred_element_type=jnp.float32,
                )
                out_ref[where, :] = (rotated * (1.0 / (eigen_ref[where, :] + damping))).astype(jnp.bfloat16)

    spaces = [pltpu.HBM if load and side == 0 else pltpu.VMEM for side in range(sides)]
    spaces += [pltpu.VMEM] * (sides + len(queries))
    constrained = [
        pltpu.with_memory_space_constraint(one, space) for one, space in zip((*bases, *eigens, *queries), spaces)
    ]
    return pl.pallas_call(
        kernel,
        in_specs=[pl.BlockSpec(memory_space=space) for space in spaces],
        out_specs=[pl.BlockSpec(memory_space=pltpu.VMEM)] * (sides + load),
        out_shape=[jax.ShapeDtypeStruct((basis.shape[0], held), jnp.bfloat16) for basis in bases]
        + ([pltpu.VMEM(bases[0].shape, bases[0].dtype)] if load else []),
        scratch_shapes=[pltpu.VMEM((held, queries[0].shape[1]), jnp.bfloat16)]
        + ([pltpu.SemaphoreType.DMA((bases[0].shape[0] // TILE,))] if load else []),
        compiler_params=pltpu.CompilerParams(vmem_limit_bytes=8 * MIB),
        cost_estimate=pl.CostEstimate(flops=1, bytes_accessed=1, transcendentals=0),
    )(*constrained)


def own_rows(query_hidden, query_model, columns):
    if columns % 16:
        start = lax.axis_index("parts") * columns
        return jnp.concatenate(
            [lax.dynamic_slice_in_dim(side, start, columns, 0) for side in (query_hidden, query_model)], axis=1
        )
    depth = query_hidden.shape[1]

    def kernel(hidden_ref, model_ref, out_ref, semaphores):
        rows = pl.ds(pl.multiple_of(lax.axis_index("parts") * columns, columns), columns)
        copies = [
            pltpu.make_async_copy(hidden_ref.at[rows], out_ref.at[:, :depth], semaphores.at[0]),
            pltpu.make_async_copy(model_ref.at[rows], out_ref.at[:, depth:], semaphores.at[1]),
        ]
        for copy in copies:
            copy.start()
        for copy in copies:
            copy.wait()

    return pl.pallas_call(
        kernel,
        in_specs=[pl.BlockSpec(memory_space=pltpu.HBM)] * 2,
        out_specs=pl.BlockSpec(memory_space=pltpu.VMEM),
        out_shape=pltpu.VMEM((columns, depth + query_model.shape[1]), query_hidden.dtype),
        scratch_shapes=[pltpu.SemaphoreType.DMA((2,))],
        compiler_params=pltpu.CompilerParams(vmem_limit_bytes=2 * MIB),
        cost_estimate=pl.CostEstimate(flops=1, bytes_accessed=1, transcendentals=0),
    )(*[pltpu.with_memory_space_constraint(side, pltpu.HBM) for side in (query_hidden, query_model)])


def packed_width(examples, columns):
    return -(-examples * columns // 128) * 128


def grams(stores, blocks, offsets, base=None):
    rows, parts = lax.axis_size("rows"), lax.axis_size("parts")
    shares = [side.shape[0] for side in blocks[0]]
    columns = blocks[0][0].shape[1] // len(offsets[0])
    count = len(stores)
    held = stores[0].shape[0] // rows
    examples = held // RANK
    width = packed_width(examples, columns)

    def kernel(*refs):
        store_refs, block_refs, out_ref = refs[:count], refs[count : count + 2 * len(blocks)], refs[-1]
        row, part = lax.axis_index("rows"), lax.axis_index("parts")
        if base is not None:
            base_ref = refs[-2]
            out_ref[...] = base_ref[...]

        def write():
            for at, block_offsets in enumerate(offsets):
                for j, store_ref in enumerate(store_refs):
                    sides = []
                    for side, begin in enumerate((0, shares[0])):
                        store = store_ref[:, begin : begin + shares[side]]
                        sides.append(
                            jnp.dot(store, block_refs[2 * at + side][...], preferred_element_type=jnp.float32)
                        )
                    owner_part = lax.rem(part + parts - j, parts)
                    for place, offset in enumerate(block_offsets):
                        shard = lax.bitwise_xor(row, offset)
                        for owner in range(rows):
                            packed = []
                            for gram in sides:
                                pieces = [
                                    gram[
                                        owner * held + i * RANK : owner * held + (i + 1) * RANK,
                                        place * columns : (place + 1) * columns,
                                    ]
                                    for i in range(examples)
                                ]
                                fill = width - examples * columns
                                if fill:
                                    pieces.append(jnp.zeros((RANK, fill), jnp.float32))
                                packed.append(jnp.concatenate(pieces, axis=1))
                            out_ref[owner_part, lax.rem(row + rows - owner, rows), shard] = jnp.concatenate(packed, axis=0).astype(jnp.bfloat16)

        if base is None:
            write()
        else:
            pl.when(jnp.logical_or(row == 0, row == rows - 1))(write)

    operands = [*stores, *[side for block in blocks for side in block]]
    return pl.pallas_call(
        kernel,
        out_shape=jax.ShapeDtypeStruct((parts, rows, rows, 2 * RANK, width), jnp.bfloat16),
        compiler_params=pltpu.CompilerParams(vmem_limit_bytes=6 * MIB),
        cost_estimate=pl.CostEstimate(flops=1, bytes_accessed=1, transcendentals=0),
    )(*operands, *([] if base is None else [base]))


def along_four(query, bases, eigens, by_owner):
    row = lax.axis_index("rows")
    depth = bases[0].shape[1]
    eigens = [eigen.reshape(-1, 1) for eigen in eigens]
    across, outwards = [(1, 2), (2, 1)], [(1, 0), (2, 3)]
    beside = lax.ppermute(query, "rows", [(0, 1), (1, 0), (2, 3), (3, 2)])
    opposite = lax.ppermute(query, "rows", across)
    sent = [lax.dynamic_index_in_dim(by_owner, (row + k) % 4, 0, False) for k in range(4)]
    query, sent = lax.optimization_barrier((query, sent))
    blocks = to_owners(sent)
    query, beside = lax.optimization_barrier((query, beside))
    two_across = lax.ppermute(beside, "rows", across)
    query, beside, opposite = lax.optimization_barrier((query, beside, opposite))
    two_outwards = lax.ppermute(opposite, "rows", outwards)
    *near, hidden_here = rotate(bases, eigens, [query, beside, opposite], (0, depth), load=True)
    bases = [hidden_here, bases[1]]
    near, blocks = lax.optimization_barrier((near, blocks))
    stores = to_parts(jnp.concatenate(blocks, axis=0))
    near, two_across = lax.optimization_barrier((near, two_across))
    two_model = two_across[:, depth:]
    three_hidden = lax.ppermute(two_across[:, :depth], "rows", outwards)
    far = rotate(bases, eigens, [(two_across, two_outwards)], (0, depth))
    far, three_hidden, two_model = lax.optimization_barrier((far, three_hidden, two_model))
    base = grams(stores, [near, far], [(0, 1, 3), (2,)])
    three_model = lax.ppermute(two_model, "rows", outwards)
    last_hidden = rotate(bases[:1], eigens[:1], [three_hidden], (0,))
    base, last_hidden, three_model = lax.optimization_barrier((base, last_hidden, three_model))
    last_model = rotate(bases[1:], eigens[1:], [three_model], (0,))
    return grams(stores, [last_hidden + last_model], [(3,)], base)


def to_owners(sent):
    rows = lax.axis_size("rows")
    return sent[:1] + [
        lax.ppermute(sent[k], "rows", [(i, (i + k) % rows) for i in range(rows)]) for k in range(1, rows)
    ]


def to_parts(store):
    parts = lax.axis_size("parts")
    return [store] + [
        lax.ppermute(store, "parts", [(i, (i + j) % parts) for i in range(parts)]) for j in range(1, parts)
    ]


def per_device(
    query_hidden,
    query_model,
    train_hidden,
    train_model,
    hidden_basis,
    model_basis,
    hidden_eigen,
    model_eigen,
):
    rows = lax.axis_size("rows")
    parts = lax.axis_size("parts")
    layers = lax.axis_size("layer")
    part = lax.axis_index("parts")
    held = train_hidden.shape[1]
    examples = held // RANK
    columns = query_hidden.shape[1] // parts
    width = query_hidden.shape[1] * rows // RANK // layers
    bases = [hidden_basis[0], model_basis[0]]
    eigens = [hidden_eigen, model_eigen]
    share = bases[0].shape[0]
    depth = bases[0].shape[1]

    query = own_rows(query_hidden[0], query_model[0], columns)
    by_owner = jnp.concatenate(
        [side[0].reshape(held, rows, -1).transpose(1, 0, 2) for side in (train_hidden, train_model)], axis=2
    )
    if rows == 4:
        partial = along_four(query, bases, eigens, by_owner)
    else:
        received = lax.all_to_all(by_owner, "rows", 0, 0, tiled=True)
        stores = to_parts(received.reshape(rows * held, -1))
        every = lax.all_gather(query, "rows", axis=0, tiled=True)
        sides = []
        for basis, eigen, gathered, begin in zip(bases, eigens, (every[:, :depth], every[:, depth:]), (0, share)):
            rotated = jnp.einsum("eh,qh->eq", basis, gathered, preferred_element_type=jnp.float32)
            scaled = (rotated * (1.0 / (eigen[0] + damping))[:, None]).astype(jnp.bfloat16)
            sides.append(
                [
                    jnp.dot(one[:, begin : begin + basis.shape[0]], scaled, preferred_element_type=jnp.float32)
                    for one in stores
                ]
            )
        partial = jnp.array(sides).reshape(2, parts, rows, examples, RANK, layers, rows // layers * columns)
        partial = partial.transpose(1, 2, 5, 0, 4, 3, 6).reshape(parts, rows, layers, 2 * RANK, -1)
        fill = packed_width(examples, rows // layers * columns) - partial.shape[-1]
        partial = jnp.pad(partial.astype(jnp.bfloat16), [(0, 0)] * 4 + [(0, fill)])
        partial = jnp.stack([lax.dynamic_index_in_dim(partial, (part - j) % parts, 0, False) for j in range(parts)])

    received = lax.all_to_all(
        partial.reshape((parts * rows * layers,) + partial.shape[3:]), ("parts", "rows", "layer"), 0, 0, tiled=True
    )
    gram = received.astype(jnp.float32).reshape(parts, rows, layers, 2, RANK, -1).sum(axis=1)
    by_column = (gram[:, :, 0] * gram[:, :, 1]).sum(axis=(1, 2))[:, : examples * width * RANK // parts]
    by_column = by_column.reshape(parts, examples, rows // layers, columns).transpose(1, 2, 0, 3)
    return by_column.reshape(examples, width, RANK).sum(axis=2)


def solution(mesh):
    placed = (
        P("layer", "rows", None),
        P("layer", "rows", None),
        P("layer", ("parts", "rows"), None),
        P("layer", ("parts", "rows"), None),
        P("layer", "rows", None),
        P("layer", "rows", None),
        P("layer", "rows"),
        P("layer", "rows"),
    )
    return jax.shard_map(
        per_device,
        mesh=mesh,
        in_specs=placed,
        out_specs=P(("parts", "rows"), "layer"),
        check_vma=False,
    )
```

```python
import jax
import jax.numpy as jnp
from jax import lax
from jax.experimental import pallas as pl
from jax.experimental.pallas import tpu as pltpu
from jax.sharding import PartitionSpec as P

RANK = 8


damping = 0.1

MIB = 1024 * 1024
TILE = 256
AHEAD = 3


def rotate(bases, eigens, queries, begins, load=False):
    groups = [query if isinstance(query, tuple) else (query,) for query in queries]
    queries = [query for group in groups for query in group]
    columns = queries[0].shape[0]
    held = columns * len(groups)
    sides = len(bases)

    def kernel(*refs):
        basis_refs, eigen_refs = refs[:sides], refs[sides : 2 * sides]
        query_refs = list(refs[2 * sides : 2 * sides + len(queries)])
        out_refs, rest = refs[2 * sides + len(queries) :][:sides], refs[3 * sides + len(queries) :]
        copies = []
        if load:
            loaded, query, semaphores = rest
            for tile in range(loaded.shape[0] // TILE):
                where = slice(tile * TILE, (tile + 1) * TILE)
                copies.append(pltpu.make_async_copy(basis_refs[0].at[where], loaded.at[where], semaphores.at[tile]))
            for copy in copies[:AHEAD]:
                copy.start()
            basis_refs = [loaded, *basis_refs[1:]]
        else:
            (query,) = rest
        for place, group in enumerate(groups):
            block = query_refs.pop(0)[...]
            for _ in group[1:]:
                block = block + query_refs.pop(0)[...]
            query[place * columns : (place + 1) * columns, :] = block
        for side in reversed(range(sides)):
            basis_ref, eigen_ref, out_ref, begin = basis_refs[side], eigen_refs[side], out_refs[side], begins[side]
            share, width = basis_ref.shape
            for tile in range(share // TILE):
                where = slice(tile * TILE, (tile + 1) * TILE)
                if load and side == 0:
                    copies[tile].wait()
                    if tile + AHEAD < len(copies):
                        copies[tile + AHEAD].start()
                rotated = lax.dot_general(
                    basis_ref[where, :],
                    query[:, begin : begin + width],
                    (((1,), (1,)), ((), ())),
                    preferred_element_type=jnp.float32,
                )
                out_ref[where, :] = (rotated * (1.0 / (eigen_ref[where, :] + damping))).astype(jnp.bfloat16)

    spaces = [pltpu.HBM if load and side == 0 else pltpu.VMEM for side in range(sides)]
    spaces += [pltpu.VMEM] * (sides + len(queries))
    constrained = [
        pltpu.with_memory_space_constraint(one, space) for one, space in zip((*bases, *eigens, *queries), spaces)
    ]
    return pl.pallas_call(
        kernel,
        in_specs=[pl.BlockSpec(memory_space=space) for space in spaces],
        out_specs=[pl.BlockSpec(memory_space=pltpu.VMEM)] * (sides + load),
        out_shape=[jax.ShapeDtypeStruct((basis.shape[0], held), jnp.bfloat16) for basis in bases]
        + ([pltpu.VMEM(bases[0].shape, bases[0].dtype)] if load else []),
        scratch_shapes=[pltpu.VMEM((held, queries[0].shape[1]), jnp.bfloat16)]
        + ([pltpu.SemaphoreType.DMA((bases[0].shape[0] // TILE,))] if load else []),
        compiler_params=pltpu.CompilerParams(vmem_limit_bytes=8 * MIB),
        cost_estimate=pl.CostEstimate(flops=1, bytes_accessed=1, transcendentals=0),
    )(*constrained)


def own_rows(query_hidden, query_model, columns):
    if columns % 16:
        start = lax.axis_index("parts") * columns
        return jnp.concatenate(
            [lax.dynamic_slice_in_dim(side, start, columns, 0) for side in (query_hidden, query_model)], axis=1
        )
    depth = query_hidden.shape[1]

    def kernel(hidden_ref, model_ref, out_ref, semaphores):
        rows = pl.ds(pl.multiple_of(lax.axis_index("parts") * columns, columns), columns)
        copies = [
            pltpu.make_async_copy(hidden_ref.at[rows], out_ref.at[:, :depth], semaphores.at[0]),
            pltpu.make_async_copy(model_ref.at[rows], out_ref.at[:, depth:], semaphores.at[1]),
        ]
        for copy in copies:
            copy.start()
        for copy in copies:
            copy.wait()

    return pl.pallas_call(
        kernel,
        in_specs=[pl.BlockSpec(memory_space=pltpu.HBM)] * 2,
        out_specs=pl.BlockSpec(memory_space=pltpu.VMEM),
        out_shape=pltpu.VMEM((columns, depth + query_model.shape[1]), query_hidden.dtype),
        scratch_shapes=[pltpu.SemaphoreType.DMA((2,))],
        compiler_params=pltpu.CompilerParams(vmem_limit_bytes=2 * MIB),
        cost_estimate=pl.CostEstimate(flops=1, bytes_accessed=1, transcendentals=0),
    )(*[pltpu.with_memory_space_constraint(side, pltpu.HBM) for side in (query_hidden, query_model)])


def packed_width(examples, columns):
    return -(-examples * columns // 128) * 128


def grams(stores, blocks, offsets, base=None):
    rows, parts = lax.axis_size("rows"), lax.axis_size("parts")
    shares = [side.shape[0] for side in blocks[0]]
    columns = blocks[0][0].shape[1] // len(offsets[0])
    count = len(stores)
    held = stores[0][0].shape[0] // len(stores[0][2])
    examples = held // RANK
    width = packed_width(examples, columns)

    def kernel(*refs):
        store_refs, block_refs, out_ref = refs[:count], refs[count : count + 2 * len(blocks)], refs[-1]
        row, part = lax.axis_index("rows"), lax.axis_index("parts")
        if base is not None:
            base_ref = refs[-2]
            out_ref[...] = base_ref[...]

        def write():
            for at, block_offsets in enumerate(offsets):
                for (_, j, ks), store_ref in zip(stores, store_refs):
                    sides = []
                    for side, begin in enumerate((0, shares[0])):
                        store = store_ref[:, begin : begin + shares[side]]
                        sides.append(
                            jnp.dot(store, block_refs[2 * at + side][...], preferred_element_type=jnp.float32)
                        )
                    owner_part = lax.rem(part + parts - j, parts)
                    for place, offset in enumerate(block_offsets):
                        shard = lax.bitwise_xor(row, offset)
                        for place_of, k in enumerate(ks):
                            packed = []
                            for gram in sides:
                                pieces = [
                                    gram[
                                        place_of * held + i * RANK : place_of * held + (i + 1) * RANK,
                                        place * columns : (place + 1) * columns,
                                    ]
                                    for i in range(examples)
                                ]
                                fill = width - examples * columns
                                if fill:
                                    pieces.append(jnp.zeros((RANK, fill), jnp.float32))
                                packed.append(jnp.concatenate(pieces, axis=1))
                            out_ref[owner_part, lax.rem(row + rows - k, rows), shard] = jnp.concatenate(packed, axis=0).astype(jnp.bfloat16)

        if base is None:
            write()
        else:
            pl.when(jnp.logical_or(row == 0, row == rows - 1))(write)

    operands = [*[store for store, _, _ in stores], *[side for block in blocks for side in block]]
    return pl.pallas_call(
        kernel,
        out_shape=jax.ShapeDtypeStruct((parts, rows, rows, 2 * RANK, width), jnp.bfloat16),
        compiler_params=pltpu.CompilerParams(vmem_limit_bytes=6 * MIB),
        cost_estimate=pl.CostEstimate(flops=1, bytes_accessed=1, transcendentals=0),
    )(*operands, *([] if base is None else [base]))


def along_four(query, bases, eigens, by_owner):
    row = lax.axis_index("rows")
    depth = bases[0].shape[1]
    eigens = [eigen.reshape(-1, 1) for eigen in eigens]
    across, outwards = [(1, 2), (2, 1)], [(1, 0), (2, 3)]
    beside = lax.ppermute(query, "rows", [(0, 1), (1, 0), (2, 3), (3, 2)])
    opposite = lax.ppermute(query, "rows", across)
    sent = [lax.dynamic_index_in_dim(by_owner, (row + k) % 4, 0, False) for k in range(4)]
    query, sent = lax.optimization_barrier((query, sent))
    blocks = [sent[0], further(sent[1], 1), further(sent[3], 3)]
    query, beside = lax.optimization_barrier((query, beside))
    two_across = lax.ppermute(beside, "rows", across)
    query, beside, opposite = lax.optimization_barrier((query, beside, opposite))
    two_outwards = lax.ppermute(opposite, "rows", outwards)
    *near, hidden_here = rotate(bases, eigens, [query, beside, opposite], (0, depth), load=True)
    bases = [hidden_here, bases[1]]
    near, blocks = lax.optimization_barrier((near, blocks))
    stores = [(store, j, (0, 1, 3)) for j, store in enumerate(to_parts(jnp.concatenate(blocks, axis=0)))]
    near, two_across, late = lax.optimization_barrier((near, two_across, sent[2]))
    two_model = two_across[:, depth:]
    three_hidden = lax.ppermute(two_across[:, :depth], "rows", outwards)
    late = further(late, 2)
    far = rotate(bases, eigens, [(two_across, two_outwards)], (0, depth))
    far, late = lax.optimization_barrier((far, late))
    stores += [(store, j, (2,)) for j, store in enumerate(to_parts(late))]
    far, three_hidden, two_model = lax.optimization_barrier((far, three_hidden, two_model))
    base = grams(stores, [near, far], [(0, 1, 3), (2,)])
    three_model = lax.ppermute(two_model, "rows", outwards)
    last_hidden = rotate(bases[:1], eigens[:1], [three_hidden], (0,))
    base, last_hidden, three_model = lax.optimization_barrier((base, last_hidden, three_model))
    last_model = rotate(bases[1:], eigens[1:], [three_model], (0,))
    return grams(stores, [last_hidden + last_model], [(3,)], base)


def further(block, k):
    rows = lax.axis_size("rows")
    return lax.ppermute(block, "rows", [(i, (i + k) % rows) for i in range(rows)])


def to_parts(store):
    parts = lax.axis_size("parts")
    return [store] + [
        lax.ppermute(store, "parts", [(i, (i + j) % parts) for i in range(parts)]) for j in range(1, parts)
    ]


def per_device(
    query_hidden,
    query_model,
    train_hidden,
    train_model,
    hidden_basis,
    model_basis,
    hidden_eigen,
    model_eigen,
):
    rows = lax.axis_size("rows")
    parts = lax.axis_size("parts")
    layers = lax.axis_size("layer")
    part = lax.axis_index("parts")
    held = train_hidden.shape[1]
    examples = held // RANK
    columns = query_hidden.shape[1] // parts
    width = query_hidden.shape[1] * rows // RANK // layers
    bases = [hidden_basis[0], model_basis[0]]
    eigens = [hidden_eigen, model_eigen]
    share = bases[0].shape[0]
    depth = bases[0].shape[1]

    query = own_rows(query_hidden[0], query_model[0], columns)
    by_owner = jnp.concatenate(
        [side[0].reshape(held, rows, -1).transpose(1, 0, 2) for side in (train_hidden, train_model)], axis=2
    )
    if rows == 4:
        partial = along_four(query, bases, eigens, by_owner)
    else:
        received = lax.all_to_all(by_owner, "rows", 0, 0, tiled=True)
        stores = to_parts(received.reshape(rows * held, -1))
        every = lax.all_gather(query, "rows", axis=0, tiled=True)
        sides = []
        for basis, eigen, gathered, begin in zip(bases, eigens, (every[:, :depth], every[:, depth:]), (0, share)):
            rotated = jnp.einsum("eh,qh->eq", basis, gathered, preferred_element_type=jnp.float32)
            scaled = (rotated * (1.0 / (eigen[0] + damping))[:, None]).astype(jnp.bfloat16)
            sides.append(
                [
                    jnp.dot(one[:, begin : begin + basis.shape[0]], scaled, preferred_element_type=jnp.float32)
                    for one in stores
                ]
            )
        partial = jnp.array(sides).reshape(2, parts, rows, examples, RANK, layers, rows // layers * columns)
        partial = partial.transpose(1, 2, 5, 0, 4, 3, 6).reshape(parts, rows, layers, 2 * RANK, -1)
        fill = packed_width(examples, rows // layers * columns) - partial.shape[-1]
        partial = jnp.pad(partial.astype(jnp.bfloat16), [(0, 0)] * 4 + [(0, fill)])
        partial = jnp.stack([lax.dynamic_index_in_dim(partial, (part - j) % parts, 0, False) for j in range(parts)])

    received = lax.all_to_all(
        partial.reshape((parts * rows * layers,) + partial.shape[3:]), ("parts", "rows", "layer"), 0, 0, tiled=True
    )
    gram = received.astype(jnp.float32).reshape(parts, rows, layers, 2, RANK, -1).sum(axis=1)
    by_column = (gram[:, :, 0] * gram[:, :, 1]).sum(axis=(1, 2))[:, : examples * width * RANK // parts]
    by_column = by_column.reshape(parts, examples, rows // layers, columns).transpose(1, 2, 0, 3)
    return by_column.reshape(examples, width, RANK).sum(axis=2)


def solution(mesh):
    placed = (
        P("layer", "rows", None),
        P("layer", "rows", None),
        P("layer", ("parts", "rows"), None),
        P("layer", ("parts", "rows"), None),
        P("layer", "rows", None),
        P("layer", "rows", None),
        P("layer", "rows"),
        P("layer", "rows"),
    )
    return jax.shard_map(
        per_device,
        mesh=mesh,
        in_specs=placed,
        out_specs=P(("parts", "rows"), "layer"),
        check_vma=False,
    )
```

```python
import jax
import jax.numpy as jnp
from jax import lax
from jax.experimental import pallas as pl
from jax.experimental.pallas import tpu as pltpu
from jax.sharding import PartitionSpec as P

RANK = 8


damping = 0.1

MIB = 1024 * 1024
TILE = 256
AHEAD = 3


def inverses(eigens):
    def kernel(*refs):
        for eigen_ref, out_ref in zip(refs[: len(eigens)], refs[len(eigens) :]):
            out_ref[...] = 1.0 / (eigen_ref[...] + damping)

    return pl.pallas_call(
        kernel,
        out_shape=[jax.ShapeDtypeStruct(eigen.shape, eigen.dtype) for eigen in eigens],
        compiler_params=pltpu.CompilerParams(vmem_limit_bytes=2 * MIB),
        cost_estimate=pl.CostEstimate(flops=1, bytes_accessed=1, transcendentals=0),
    )(*eigens)


def rotate(bases, inverses, queries, begins, load=False):
    groups = [query if isinstance(query, tuple) else (query,) for query in queries]
    queries = [query for group in groups for query in group]
    columns = queries[0].shape[0]
    held = columns * len(groups)
    sides = len(bases)

    def kernel(*refs):
        basis_refs, inverse_refs = refs[:sides], refs[sides : 2 * sides]
        query_refs = list(refs[2 * sides : 2 * sides + len(queries)])
        out_refs, rest = refs[2 * sides + len(queries) :][:sides], refs[3 * sides + len(queries) :]
        copies = []
        if load:
            loaded, query, semaphores = rest
            for tile in range(loaded.shape[0] // TILE):
                where = slice(tile * TILE, (tile + 1) * TILE)
                copies.append(pltpu.make_async_copy(basis_refs[0].at[where], loaded.at[where], semaphores.at[tile]))
            for copy in copies[:AHEAD]:
                copy.start()
            basis_refs = [loaded, *basis_refs[1:]]
        else:
            (query,) = rest
        for place, group in enumerate(groups):
            block = query_refs.pop(0)[...]
            for _ in group[1:]:
                block = block + query_refs.pop(0)[...]
            query[place * columns : (place + 1) * columns, :] = block
        for side in reversed(range(sides)):
            basis_ref, inverse_ref, out_ref, begin = basis_refs[side], inverse_refs[side], out_refs[side], begins[side]
            share, width = basis_ref.shape
            for tile in range(share // TILE):
                where = slice(tile * TILE, (tile + 1) * TILE)
                if load and side == 0:
                    copies[tile].wait()
                    if tile + AHEAD < len(copies):
                        copies[tile + AHEAD].start()
                rotated = lax.dot_general(
                    basis_ref[where, :],
                    query[:, begin : begin + width],
                    (((1,), (1,)), ((), ())),
                    preferred_element_type=jnp.float32,
                )
                out_ref[where, :] = (rotated * inverse_ref[where, :]).astype(jnp.bfloat16)

    spaces = [pltpu.HBM if load and side == 0 else pltpu.VMEM for side in range(sides)]
    spaces += [pltpu.VMEM] * (sides + len(queries))
    constrained = [
        pltpu.with_memory_space_constraint(one, space) for one, space in zip((*bases, *inverses, *queries), spaces)
    ]
    return pl.pallas_call(
        kernel,
        in_specs=[pl.BlockSpec(memory_space=space) for space in spaces],
        out_specs=[pl.BlockSpec(memory_space=pltpu.VMEM)] * (sides + load),
        out_shape=[jax.ShapeDtypeStruct((basis.shape[0], held), jnp.bfloat16) for basis in bases]
        + ([pltpu.VMEM(bases[0].shape, bases[0].dtype)] if load else []),
        scratch_shapes=[pltpu.VMEM((held, queries[0].shape[1]), jnp.bfloat16)]
        + ([pltpu.SemaphoreType.DMA((bases[0].shape[0] // TILE,))] if load else []),
        compiler_params=pltpu.CompilerParams(vmem_limit_bytes=8 * MIB),
        cost_estimate=pl.CostEstimate(flops=1, bytes_accessed=1, transcendentals=0),
    )(*constrained)


def own_rows(query_hidden, query_model, columns):
    if columns % 16:
        start = lax.axis_index("parts") * columns
        return jnp.concatenate(
            [lax.dynamic_slice_in_dim(side, start, columns, 0) for side in (query_hidden, query_model)], axis=1
        )
    depth = query_hidden.shape[1]

    def kernel(hidden_ref, model_ref, out_ref, semaphores):
        rows = pl.ds(pl.multiple_of(lax.axis_index("parts") * columns, columns), columns)
        copies = [
            pltpu.make_async_copy(hidden_ref.at[rows], out_ref.at[:, :depth], semaphores.at[0]),
            pltpu.make_async_copy(model_ref.at[rows], out_ref.at[:, depth:], semaphores.at[1]),
        ]
        for copy in copies:
            copy.start()
        for copy in copies:
            copy.wait()

    return pl.pallas_call(
        kernel,
        in_specs=[pl.BlockSpec(memory_space=pltpu.HBM)] * 2,
        out_specs=pl.BlockSpec(memory_space=pltpu.VMEM),
        out_shape=pltpu.VMEM((columns, depth + query_model.shape[1]), query_hidden.dtype),
        scratch_shapes=[pltpu.SemaphoreType.DMA((2,))],
        compiler_params=pltpu.CompilerParams(vmem_limit_bytes=2 * MIB),
        cost_estimate=pl.CostEstimate(flops=1, bytes_accessed=1, transcendentals=0),
    )(*[pltpu.with_memory_space_constraint(side, pltpu.HBM) for side in (query_hidden, query_model)])


def packed_width(examples, columns):
    return -(-examples * columns // 128) * 128


def grams(stores, blocks, offsets, base=None):
    rows, parts = lax.axis_size("rows"), lax.axis_size("parts")
    shares = [side.shape[0] for side in blocks[0]]
    columns = blocks[0][0].shape[1] // len(offsets[0])
    count = len(stores)
    held = stores[0][0].shape[0] // len(stores[0][2])
    examples = held // RANK
    width = packed_width(examples, columns)

    def kernel(*refs):
        store_refs, block_refs, out_ref = refs[:count], refs[count : count + 2 * len(blocks)], refs[-1]
        row, part = lax.axis_index("rows"), lax.axis_index("parts")
        if base is not None:
            base_ref = refs[-2]
            out_ref[...] = base_ref[...]

        def write():
            for at, block_offsets in enumerate(offsets):
                for (_, j, ks), store_ref in zip(stores, store_refs):
                    sides = []
                    for side, begin in enumerate((0, shares[0])):
                        store = store_ref[:, begin : begin + shares[side]]
                        sides.append(
                            jnp.dot(store, block_refs[2 * at + side][...], preferred_element_type=jnp.float32)
                        )
                    owner_part = lax.rem(part + parts - j, parts)
                    for place, offset in enumerate(block_offsets):
                        shard = lax.bitwise_xor(row, offset)
                        for place_of, k in enumerate(ks):
                            packed = []
                            for gram in sides:
                                pieces = [
                                    gram[
                                        place_of * held + i * RANK : place_of * held + (i + 1) * RANK,
                                        place * columns : (place + 1) * columns,
                                    ]
                                    for i in range(examples)
                                ]
                                fill = width - examples * columns
                                if fill:
                                    pieces.append(jnp.zeros((RANK, fill), jnp.float32))
                                packed.append(jnp.concatenate(pieces, axis=1))
                            out_ref[owner_part, lax.rem(row + rows - k, rows), shard] = jnp.concatenate(packed, axis=0).astype(jnp.bfloat16)

        if base is None:
            write()
        else:
            pl.when(jnp.logical_or(row == 0, row == rows - 1))(write)

    operands = [*[store for store, _, _ in stores], *[side for block in blocks for side in block]]
    return pl.pallas_call(
        kernel,
        out_shape=jax.ShapeDtypeStruct((parts, rows, rows, 2 * RANK, width), jnp.bfloat16),
        compiler_params=pltpu.CompilerParams(vmem_limit_bytes=6 * MIB),
        cost_estimate=pl.CostEstimate(flops=1, bytes_accessed=1, transcendentals=0),
    )(*operands, *([] if base is None else [base]))


def along_four(query, bases, eigens, by_owner):
    row = lax.axis_index("rows")
    depth = bases[0].shape[1]
    across, outwards = [(1, 2), (2, 1)], [(1, 0), (2, 3)]
    beside = lax.ppermute(query, "rows", [(0, 1), (1, 0), (2, 3), (3, 2)])
    opposite = lax.ppermute(query, "rows", across)
    sent = [lax.dynamic_index_in_dim(by_owner, (row + k) % 4, 0, False) for k in range(4)]
    query, sent, eigens = lax.optimization_barrier((query, sent, eigens))
    eigens = inverses([eigen.reshape(-1, 1) for eigen in eigens])
    blocks = [sent[0], further(sent[1], 1), further(sent[3], 3)]
    query, beside, eigens = lax.optimization_barrier((query, beside, eigens))
    two_across = lax.ppermute(beside, "rows", across)
    query, beside, opposite = lax.optimization_barrier((query, beside, opposite))
    two_outwards = lax.ppermute(opposite, "rows", outwards)
    *near, hidden_here = rotate(bases, eigens, [query, beside, opposite], (0, depth), load=True)
    bases = [hidden_here, bases[1]]
    near, blocks = lax.optimization_barrier((near, blocks))
    stores = [(store, j, (0, 1, 3)) for j, store in enumerate(to_parts(jnp.concatenate(blocks, axis=0)))]
    near, two_across, late = lax.optimization_barrier((near, two_across, sent[2]))
    two_model = two_across[:, depth:]
    three_hidden = lax.ppermute(two_across[:, :depth], "rows", outwards)
    late = further(late, 2)
    far = rotate(bases, eigens, [(two_across, two_outwards)], (0, depth))
    far, late = lax.optimization_barrier((far, late))
    stores += [(store, j, (2,)) for j, store in enumerate(to_parts(late))]
    far, three_hidden, two_model = lax.optimization_barrier((far, three_hidden, two_model))
    base = grams(stores, [near, far], [(0, 1, 3), (2,)])
    three_model = lax.ppermute(two_model, "rows", outwards)
    last_hidden = rotate(bases[:1], eigens[:1], [three_hidden], (0,))
    base, last_hidden, three_model = lax.optimization_barrier((base, last_hidden, three_model))
    last_model = rotate(bases[1:], eigens[1:], [three_model], (0,))
    return grams(stores, [last_hidden + last_model], [(3,)], base)


def further(block, k):
    rows = lax.axis_size("rows")
    return lax.ppermute(block, "rows", [(i, (i + k) % rows) for i in range(rows)])


def to_parts(store):
    parts = lax.axis_size("parts")
    return [store] + [
        lax.ppermute(store, "parts", [(i, (i + j) % parts) for i in range(parts)]) for j in range(1, parts)
    ]


def per_device(
    query_hidden,
    query_model,
    train_hidden,
    train_model,
    hidden_basis,
    model_basis,
    hidden_eigen,
    model_eigen,
):
    rows = lax.axis_size("rows")
    parts = lax.axis_size("parts")
    layers = lax.axis_size("layer")
    part = lax.axis_index("parts")
    held = train_hidden.shape[1]
    examples = held // RANK
    columns = query_hidden.shape[1] // parts
    width = query_hidden.shape[1] * rows // RANK // layers
    bases = [hidden_basis[0], model_basis[0]]
    eigens = [hidden_eigen, model_eigen]
    share = bases[0].shape[0]
    depth = bases[0].shape[1]

    query = own_rows(query_hidden[0], query_model[0], columns)
    by_owner = jnp.concatenate(
        [side[0].reshape(held, rows, -1).transpose(1, 0, 2) for side in (train_hidden, train_model)], axis=2
    )
    if rows == 4:
        partial = along_four(query, bases, eigens, by_owner)
    else:
        received = lax.all_to_all(by_owner, "rows", 0, 0, tiled=True)
        stores = to_parts(received.reshape(rows * held, -1))
        every = lax.all_gather(query, "rows", axis=0, tiled=True)
        sides = []
        for basis, eigen, gathered, begin in zip(bases, eigens, (every[:, :depth], every[:, depth:]), (0, share)):
            rotated = jnp.einsum("eh,qh->eq", basis, gathered, preferred_element_type=jnp.float32)
            scaled = (rotated * (1.0 / (eigen[0] + damping))[:, None]).astype(jnp.bfloat16)
            sides.append(
                [
                    jnp.dot(one[:, begin : begin + basis.shape[0]], scaled, preferred_element_type=jnp.float32)
                    for one in stores
                ]
            )
        partial = jnp.array(sides).reshape(2, parts, rows, examples, RANK, layers, rows // layers * columns)
        partial = partial.transpose(1, 2, 5, 0, 4, 3, 6).reshape(parts, rows, layers, 2 * RANK, -1)
        fill = packed_width(examples, rows // layers * columns) - partial.shape[-1]
        partial = jnp.pad(partial.astype(jnp.bfloat16), [(0, 0)] * 4 + [(0, fill)])
        partial = jnp.stack([lax.dynamic_index_in_dim(partial, (part - j) % parts, 0, False) for j in range(parts)])

    received = lax.all_to_all(
        partial.reshape((parts * rows * layers,) + partial.shape[3:]), ("parts", "rows", "layer"), 0, 0, tiled=True
    )
    gram = received.astype(jnp.float32).reshape(parts, rows, layers, 2, RANK, -1).sum(axis=1)
    by_column = (gram[:, :, 0] * gram[:, :, 1]).sum(axis=(1, 2))[:, : examples * width * RANK // parts]
    by_column = by_column.reshape(parts, examples, rows // layers, columns).transpose(1, 2, 0, 3)
    return by_column.reshape(examples, width, RANK).sum(axis=2)


def solution(mesh):
    placed = (
        P("layer", "rows", None),
        P("layer", "rows", None),
        P("layer", ("parts", "rows"), None),
        P("layer", ("parts", "rows"), None),
        P("layer", "rows", None),
        P("layer", "rows", None),
        P("layer", "rows"),
        P("layer", "rows"),
    )
    return jax.shard_map(
        per_device,
        mesh=mesh,
        in_specs=placed,
        out_specs=P(("parts", "rows"), "layer"),
        check_vma=False,
    )
```

```python
import jax
import jax.numpy as jnp
from jax import lax
from jax.experimental import pallas as pl
from jax.experimental.pallas import tpu as pltpu
from jax.sharding import PartitionSpec as P

RANK = 8


damping = 0.1

MIB = 1024 * 1024
TILE = 256
AHEAD = 3


def inverses(eigens):
    def kernel(*refs):
        for eigen_ref, out_ref in zip(refs[: len(eigens)], refs[len(eigens) :]):
            out_ref[...] = 1.0 / (eigen_ref[...] + damping)

    return pl.pallas_call(
        kernel,
        out_shape=[jax.ShapeDtypeStruct(eigen.shape, eigen.dtype) for eigen in eigens],
        compiler_params=pltpu.CompilerParams(vmem_limit_bytes=2 * MIB),
        cost_estimate=pl.CostEstimate(flops=1, bytes_accessed=1, transcendentals=0),
    )(*eigens)


def rotate(bases, inverses, queries, begins, load=False):
    groups = [query if isinstance(query, tuple) else (query,) for query in queries]
    queries = [query for group in groups for query in group]
    columns = queries[0].shape[0]
    held = columns * len(groups)
    sides = len(bases)

    def kernel(*refs):
        basis_refs, inverse_refs = refs[:sides], refs[sides : 2 * sides]
        query_refs = list(refs[2 * sides : 2 * sides + len(queries)])
        out_refs, rest = refs[2 * sides + len(queries) :][:sides], refs[3 * sides + len(queries) :]
        copies = []
        if load:
            loaded, query, semaphores = rest
            for tile in range(loaded.shape[0] // TILE):
                where = slice(tile * TILE, (tile + 1) * TILE)
                copies.append(pltpu.make_async_copy(basis_refs[0].at[where], loaded.at[where], semaphores.at[tile]))
            for copy in copies[:AHEAD]:
                copy.start()
            basis_refs = [loaded, *basis_refs[1:]]
        else:
            (query,) = rest
        for place, group in enumerate(groups):
            block = query_refs.pop(0)[...]
            for _ in group[1:]:
                block = block + query_refs.pop(0)[...]
            query[place * columns : (place + 1) * columns, :] = block
        for side in reversed(range(sides)):
            basis_ref, inverse_ref, out_ref, begin = basis_refs[side], inverse_refs[side], out_refs[side], begins[side]
            share, width = basis_ref.shape
            for tile in range(share // TILE):
                where = slice(tile * TILE, (tile + 1) * TILE)
                if load and side == 0:
                    copies[tile].wait()
                    if tile + AHEAD < len(copies):
                        copies[tile + AHEAD].start()
                rotated = lax.dot_general(
                    basis_ref[where, :],
                    query[:, begin : begin + width],
                    (((1,), (1,)), ((), ())),
                    preferred_element_type=jnp.float32,
                )
                out_ref[where, :] = (rotated * inverse_ref[where, :]).astype(jnp.bfloat16)

    spaces = [pltpu.HBM if load and side == 0 else pltpu.VMEM for side in range(sides)]
    spaces += [pltpu.VMEM] * (sides + len(queries))
    constrained = [
        pltpu.with_memory_space_constraint(one, space) for one, space in zip((*bases, *inverses, *queries), spaces)
    ]
    return pl.pallas_call(
        kernel,
        in_specs=[pl.BlockSpec(memory_space=space) for space in spaces],
        out_specs=[pl.BlockSpec(memory_space=pltpu.VMEM)] * (sides + load),
        out_shape=[jax.ShapeDtypeStruct((basis.shape[0], held), jnp.bfloat16) for basis in bases]
        + ([pltpu.VMEM(bases[0].shape, bases[0].dtype)] if load else []),
        scratch_shapes=[pltpu.VMEM((held, queries[0].shape[1]), jnp.bfloat16)]
        + ([pltpu.SemaphoreType.DMA((bases[0].shape[0] // TILE,))] if load else []),
        compiler_params=pltpu.CompilerParams(vmem_limit_bytes=8 * MIB),
        cost_estimate=pl.CostEstimate(flops=1, bytes_accessed=1, transcendentals=0),
    )(*constrained)


def own_rows(query_hidden, query_model, columns):
    if columns % 16:
        start = lax.axis_index("parts") * columns
        return jnp.concatenate(
            [lax.dynamic_slice_in_dim(side, start, columns, 0) for side in (query_hidden, query_model)], axis=1
        )
    depth = query_hidden.shape[1]

    def kernel(hidden_ref, model_ref, out_ref, semaphores):
        rows = pl.ds(pl.multiple_of(lax.axis_index("parts") * columns, columns), columns)
        copies = [
            pltpu.make_async_copy(hidden_ref.at[rows], out_ref.at[:, :depth], semaphores.at[0]),
            pltpu.make_async_copy(model_ref.at[rows], out_ref.at[:, depth:], semaphores.at[1]),
        ]
        for copy in copies:
            copy.start()
        for copy in copies:
            copy.wait()

    return pl.pallas_call(
        kernel,
        in_specs=[pl.BlockSpec(memory_space=pltpu.HBM)] * 2,
        out_specs=pl.BlockSpec(memory_space=pltpu.VMEM),
        out_shape=pltpu.VMEM((columns, depth + query_model.shape[1]), query_hidden.dtype),
        scratch_shapes=[pltpu.SemaphoreType.DMA((2,))],
        compiler_params=pltpu.CompilerParams(vmem_limit_bytes=2 * MIB),
        cost_estimate=pl.CostEstimate(flops=1, bytes_accessed=1, transcendentals=0),
    )(*[pltpu.with_memory_space_constraint(side, pltpu.HBM) for side in (query_hidden, query_model)])


def packed_width(examples, columns):
    return -(-examples * columns // 128) * 128


def grams(stores, blocks, offsets, base=None):
    rows, parts = lax.axis_size("rows"), lax.axis_size("parts")
    shares = [side.shape[0] for side in blocks[0]]
    columns = blocks[0][0].shape[1] // len(offsets[0])
    count = len(stores)
    held = stores[0][0].shape[0] // len(stores[0][2])
    examples = held // RANK
    width = packed_width(examples, columns)

    def kernel(*refs):
        store_refs, block_refs, out_ref = refs[:count], refs[count : count + 2 * len(blocks)], refs[-1]
        row, part = lax.axis_index("rows"), lax.axis_index("parts")
        if base is not None:
            base_ref = refs[-2]
            out_ref[...] = base_ref[...]

        def write():
            for at, block_offsets in enumerate(offsets):
                for (_, j, ks), store_ref in zip(stores, store_refs):
                    sides = []
                    for side, begin in enumerate((0, shares[0])):
                        store = store_ref[:, begin : begin + shares[side]]
                        sides.append(
                            jnp.dot(store, block_refs[2 * at + side][...], preferred_element_type=jnp.float32)
                        )
                    owner_part = lax.rem(part + parts - j, parts)
                    for place, offset in enumerate(block_offsets):
                        shard = lax.bitwise_xor(row, offset)
                        for place_of, k in enumerate(ks):
                            packed = []
                            for gram in sides:
                                pieces = [
                                    gram[
                                        place_of * held + i * RANK : place_of * held + (i + 1) * RANK,
                                        place * columns : (place + 1) * columns,
                                    ]
                                    for i in range(examples)
                                ]
                                fill = width - examples * columns
                                if fill:
                                    pieces.append(jnp.zeros((RANK, fill), jnp.float32))
                                packed.append(jnp.concatenate(pieces, axis=1))
                            out_ref[owner_part, lax.rem(row + rows - k, rows), shard] = jnp.concatenate(packed, axis=0).astype(jnp.bfloat16)

        if base is None:
            write()
        else:
            pl.when(jnp.logical_or(row == 0, row == rows - 1))(write)

    operands = [*[store for store, _, _ in stores], *[side for block in blocks for side in block]]
    return pl.pallas_call(
        kernel,
        out_shape=jax.ShapeDtypeStruct((parts, rows, rows, 2 * RANK, width), jnp.bfloat16),
        compiler_params=pltpu.CompilerParams(vmem_limit_bytes=6 * MIB),
        cost_estimate=pl.CostEstimate(flops=1, bytes_accessed=1, transcendentals=0),
    )(*operands, *([] if base is None else [base]))


def along_four(query, bases, eigens, by_owner):
    row = lax.axis_index("rows")
    depth = bases[0].shape[1]
    across, outwards = [(1, 2), (2, 1)], [(1, 0), (2, 3)]
    beside = lax.ppermute(query, "rows", [(0, 1), (1, 0), (2, 3), (3, 2)])
    opposite = lax.ppermute(query, "rows", across)
    sent = [lax.dynamic_index_in_dim(by_owner, (row + k) % 4, 0, False) for k in range(4)]
    query, sent, eigens = lax.optimization_barrier((query, sent, eigens))
    eigens = inverses([eigen.reshape(-1, 1) for eigen in eigens])
    blocks = [sent[0], further(sent[1], 1), further(sent[3], 3)]
    query, beside, eigens = lax.optimization_barrier((query, beside, eigens))
    two_across = lax.ppermute(beside, "rows", across)
    query, beside, opposite = lax.optimization_barrier((query, beside, opposite))
    two_outwards = lax.ppermute(opposite, "rows", outwards)
    *near, hidden_here = rotate(bases, eigens, [query, beside, opposite], (0, depth), load=True)
    bases = [hidden_here, bases[1]]
    near, two_across, late = lax.optimization_barrier((near, two_across, sent[2]))
    two_model = two_across[:, depth:]
    two_hidden = two_across[:, :depth]
    three_hidden = lax.ppermute(two_hidden, "rows", outwards)
    _, blocks = lax.optimization_barrier((two_hidden, blocks))
    stores = [(store, j, (0, 1, 3)) for j, store in enumerate(to_parts(jnp.concatenate(blocks, axis=0)))]
    late = further(late, 2)
    far = rotate(bases, eigens, [(two_across, two_outwards)], (0, depth))
    far, late = lax.optimization_barrier((far, late))
    stores += [(store, j, (2,)) for j, store in enumerate(to_parts(late))]
    far, three_hidden, two_model = lax.optimization_barrier((far, three_hidden, two_model))
    base = grams(stores, [near, far], [(0, 1, 3), (2,)])
    three_model = lax.ppermute(two_model, "rows", outwards)
    last_hidden = rotate(bases[:1], eigens[:1], [three_hidden], (0,))
    base, last_hidden, three_model = lax.optimization_barrier((base, last_hidden, three_model))
    last_model = rotate(bases[1:], eigens[1:], [three_model], (0,))
    return grams(stores, [last_hidden + last_model], [(3,)], base)


def further(block, k):
    rows = lax.axis_size("rows")
    return lax.ppermute(block, "rows", [(i, (i + k) % rows) for i in range(rows)])


def to_parts(store):
    parts = lax.axis_size("parts")
    return [store] + [
        lax.ppermute(store, "parts", [(i, (i + j) % parts) for i in range(parts)]) for j in range(1, parts)
    ]


def per_device(
    query_hidden,
    query_model,
    train_hidden,
    train_model,
    hidden_basis,
    model_basis,
    hidden_eigen,
    model_eigen,
):
    rows = lax.axis_size("rows")
    parts = lax.axis_size("parts")
    layers = lax.axis_size("layer")
    part = lax.axis_index("parts")
    held = train_hidden.shape[1]
    examples = held // RANK
    columns = query_hidden.shape[1] // parts
    width = query_hidden.shape[1] * rows // RANK // layers
    bases = [hidden_basis[0], model_basis[0]]
    eigens = [hidden_eigen, model_eigen]
    share = bases[0].shape[0]
    depth = bases[0].shape[1]

    query = own_rows(query_hidden[0], query_model[0], columns)
    by_owner = jnp.concatenate(
        [side[0].reshape(held, rows, -1).transpose(1, 0, 2) for side in (train_hidden, train_model)], axis=2
    )
    if rows == 4:
        partial = along_four(query, bases, eigens, by_owner)
    else:
        received = lax.all_to_all(by_owner, "rows", 0, 0, tiled=True)
        stores = to_parts(received.reshape(rows * held, -1))
        every = lax.all_gather(query, "rows", axis=0, tiled=True)
        sides = []
        for basis, eigen, gathered, begin in zip(bases, eigens, (every[:, :depth], every[:, depth:]), (0, share)):
            rotated = jnp.einsum("eh,qh->eq", basis, gathered, preferred_element_type=jnp.float32)
            scaled = (rotated * (1.0 / (eigen[0] + damping))[:, None]).astype(jnp.bfloat16)
            sides.append(
                [
                    jnp.dot(one[:, begin : begin + basis.shape[0]], scaled, preferred_element_type=jnp.float32)
                    for one in stores
                ]
            )
        partial = jnp.array(sides).reshape(2, parts, rows, examples, RANK, layers, rows // layers * columns)
        partial = partial.transpose(1, 2, 5, 0, 4, 3, 6).reshape(parts, rows, layers, 2 * RANK, -1)
        fill = packed_width(examples, rows // layers * columns) - partial.shape[-1]
        partial = jnp.pad(partial.astype(jnp.bfloat16), [(0, 0)] * 4 + [(0, fill)])
        partial = jnp.stack([lax.dynamic_index_in_dim(partial, (part - j) % parts, 0, False) for j in range(parts)])

    received = lax.all_to_all(
        partial.reshape((parts * rows * layers,) + partial.shape[3:]), ("parts", "rows", "layer"), 0, 0, tiled=True
    )
    gram = received.astype(jnp.float32).reshape(parts, rows, layers, 2, RANK, -1).sum(axis=1)
    by_column = (gram[:, :, 0] * gram[:, :, 1]).sum(axis=(1, 2))[:, : examples * width * RANK // parts]
    by_column = by_column.reshape(parts, examples, rows // layers, columns).transpose(1, 2, 0, 3)
    return by_column.reshape(examples, width, RANK).sum(axis=2)


def solution(mesh):
    placed = (
        P("layer", "rows", None),
        P("layer", "rows", None),
        P("layer", ("parts", "rows"), None),
        P("layer", ("parts", "rows"), None),
        P("layer", "rows", None),
        P("layer", "rows", None),
        P("layer", "rows"),
        P("layer", "rows"),
    )
    return jax.shard_map(
        per_device,
        mesh=mesh,
        in_specs=placed,
        out_specs=P(("parts", "rows"), "layer"),
        check_vma=False,
    )
```
